32 devices in a mesh: dp: 8 (over y, x, core), mem: 4 (over z).
Axes of the slice: x: 2, y: 2, z: 4, core: 2. Of those that a mesh axis runs over, the one named last changes fastest.
Arguments:
- decoder_input: bfloat16 [32, 1024, 512], P(('dp', 'mem')), may hold values from -6 to 6
- timesteps: int32 [32], P(('dp', 'mem')), may hold values from 0 to 49
- memory: bfloat16 [32, 1024, 512], P('dp', 'mem'), may hold values from -6 to 6
- cotangent: bfloat16 [32, 1024, 512], P(('dp', 'mem')), may hold values from -6 to 6
- time_weight: bfloat16 [512, 512], P('dp'), may hold values from -0.25 to 0.25
- attn_query: bfloat16 [512, 512], P('dp'), may hold values from -0.375 to 0.375
- attn_key: bfloat16 [512, 512], P('dp'), may hold values from -0.25 to 0.25
- attn_value: bfloat16 [512, 512], P('dp'), may hold values from -0.25 to 0.25
- attn_out: bfloat16 [512, 512], P('dp'), may hold values from -4 to 4
- cross_query: bfloat16 [512, 512], P('dp'), may hold values from -0.375 to 0.375
- cross_key: bfloat16 [512, 512], P('dp'), may hold values from -0.25 to 0.25
- cross_value: bfloat16 [512, 512], P('dp'), may hold values from -0.25 to 0.25
- cross_out: bfloat16 [512, 512], P('dp'), may hold values from -4 to 4
- ffn_in: bfloat16 [512, 2048], P('dp'), may hold values from -0.25 to 0.25
- ffn_out: bfloat16 [2048, 512], P('dp'), may hold values from -0.125 to 0.125
- norm_gains: float32 [512, 3], replicated, may hold values from 0.25 to 1.75
Outputs:
- layer_output: bfloat16 [32, 1024, 512], P(('dp', 'mem'))
- input_grad: bfloat16 [32, 1024, 512], P(('dp', 'mem'))
- memory_grad: bfloat16 [32, 1024, 512], P('dp', 'mem')
- grad_time: float32 [512, 512], P('dp', 'mem')
- grad_attn_query: float32 [512, 512], P('dp', 'mem')
- grad_attn_key: float32 [512, 512], P('dp', 'mem')
- grad_attn_value: float32 [512, 512], P('dp', 'mem')
- grad_attn_out: float32 [512, 512], P('dp', 'mem')
- grad_cross_query: float32 [512, 512], P('dp', 'mem')
- grad_cross_key: float32 [512, 512], P('dp', 'mem')
- grad_cross_value: float32 [512, 512], P('dp', 'mem')
- grad_cross_out: float32 [512, 512], P('dp', 'mem')
- grad_ffn_in: float32 [512, 2048], P('dp', 'mem')
- grad_ffn_out: float32 [2048, 512], P('dp', 'mem')
- grad_gains: float32 [512, 3], P('dp')
The draws below stay inside these ranges and needn't reach their ends.
All inputs are finite; a program needn't handle non-finite values.
Results may differ from the reference program's by a relative error of at most 0.022.
Values may be sent and summed in bfloat16 or wider, within the bound.
No kernel may reach another device: no remote copies, remote signals or barrier semaphores. Data moves between devices by JAX's collectives and lax.ppermute only.
A program may use at most 320 MiB of HBM per device.

```python
import math
import jax
import jax.numpy as jnp
from jax import lax

D = 512
HEADS = 8
HEAD = 64
FF = 2048
STEPS = 50
LEN = 1024
SRC = 1024
SEGMENTS = 32


def set_ends(values, key, least, top_value):
    place = [jax.random.randint(jax.random.fold_in(key, axis), (), 0, length) for axis, length in enumerate(values.shape)]
    widest = values.shape.index(max(values.shape))
    next_to = place[:widest] + [(place[widest] + 1) % values.shape[widest]] + place[widest + 1:]
    return values.at[tuple(place)].set(least).at[tuple(next_to)].set(top_value)


def level_of(rng, extent, shards, least, largest):
    level, own = 1.0, jax.random.fold_in(rng, 6)
    for axis_at, shards_of in shards:
        draws = jnp.exp(jax.random.uniform(jax.random.fold_in(own, axis_at), (shards_of,), jnp.float32, least / len(shards), largest / len(shards)))
        level = level * jnp.repeat(draws, extent[axis_at] // shards_of).reshape([-1 if axis == axis_at else 1 for axis in range(len(extent))])
    return level


def bell_draw(stream_key, extent, deviation, bound, split=(), held_as=jnp.bfloat16):
    values = jax.random.normal(stream_key, extent, jnp.float32) * deviation
    if len(split) > 0:
        values = level_of(stream_key, extent, split, -0.22, 0.18) * values
    return jnp.clip(values, min=-bound, max=bound).astype(held_as)


def setup_inputs(seed: int = 0) -> dict:
    splits = jax.random.split(jax.random.key(seed), 17)
    return {
        "decoder_input": bell_draw(splits[0], (SEGMENTS, LEN, D), 1.0, 6.0, ((0, 32),)),
        "timesteps": set_ends(jax.random.randint(splits[1], (SEGMENTS,), 0, STEPS), jax.random.fold_in(splits[1], 1), 0, STEPS - 1).astype(jnp.int32),
        "memory": bell_draw(splits[2], (SEGMENTS, SRC, D), 1.0, 6.0, ((0, 8), (1, 4))),
        "cotangent": bell_draw(splits[3], (SEGMENTS, LEN, D), 1.0, 6.0, ((0, 32),)),
        "time_weight": bell_draw(splits[4], (D, D), D ** -0.5, 0.25, ((0, 8),)),
        "attn_query": bell_draw(splits[5], (D, D), (D // 2) ** -0.5, 0.375, ((0, 8),)),
        "attn_key": bell_draw(splits[6], (D, D), D ** -0.5, 0.25, ((0, 8),)),
        "attn_value": bell_draw(splits[7], (D, D), D ** -0.5, 0.25, ((0, 8),)),
        "attn_out": bell_draw(splits[8], (D, D), (max(1, D // 256)) ** -0.5, 4.0, ((0, 8),)),
        "cross_query": bell_draw(splits[9], (D, D), (D // 2) ** -0.5, 0.375, ((0, 8),)),
        "cross_key": bell_draw(splits[10], (D, D), D ** -0.5, 0.25, ((0, 8),)),
        "cross_value": bell_draw(splits[11], (D, D), D ** -0.5, 0.25, ((0, 8),)),
        "cross_out": bell_draw(splits[12], (D, D), (max(1, D // 256)) ** -0.5, 4.0, ((0, 8),)),
        "ffn_in": bell_draw(splits[13], (D, FF), D ** -0.5, 0.25, ((0, 8),)),
        "ffn_out": bell_draw(splits[14], (FF, D), FF ** -0.5, 0.125, ((0, 8),)),
        "norm_gains": jnp.clip(1.0 + 0.15 * jax.random.normal(splits[15], (D, 3), jnp.float32), 0.25, 1.75),
    }


@jax.custom_vjp
def low(v):
    return lax.optimization_barrier(v.astype(jnp.bfloat16)).astype(jnp.float32)

@jax.custom_vjp
def low_back(v):
    return v

def low_keep(v):
    return (low(v), None)

def low_pass(kept, grad):
    return (grad,)

def back_keep(v):
    return (v, None)

def back_low(kept, grad):
    return (low(grad),)
low.defvjp(low_keep, low_pass)
low_back.defvjp(back_keep, back_low)

def highest(first_op, second_op):
    return jnp.dot(first_op, second_op, precision=lax.Precision.HIGHEST)

def layer_norm(values, gain_vec):
    row_mean = lax.optimization_barrier(jnp.mean(values, axis=-1, keepdims=True))
    centred = values - row_mean
    variance = lax.optimization_barrier(jnp.mean(centred * centred, axis=-1, keepdims=True))
    return centred * lax.rsqrt(variance + 1e-05) * gain_vec

def step_signal(step_ids):
    half_width = D // 2
    frequency = jnp.exp(-math.log(10000.0) * jnp.arange(half_width, dtype=jnp.float32) / half_width)
    angles = step_ids.astype(jnp.float32)[:, None] * frequency[None, :]
    return jnp.concatenate([jnp.sin(angles), jnp.cos(angles)], axis=1)

def attend_block(query_block, keys, values):
    score_scale = 1.0 / math.sqrt(HEAD)
    query_heads = query_block.reshape(query_block.shape[0], HEADS, HEAD)
    key_heads = keys.reshape(keys.shape[0], HEADS, HEAD)
    value_heads = values.reshape(values.shape[0], HEADS, HEAD)
    scores = low_back(jnp.einsum('qhd,khd->hqk', query_heads, key_heads, precision=lax.Precision.HIGHEST) * score_scale)
    probs_full = jax.nn.softmax(scores, axis=-1)
    mixed_heads = jnp.einsum('hqk,khd->qhd', low(probs_full), value_heads, precision=lax.Precision.HIGHEST)
    return mixed_heads.reshape(query_block.shape[0], D)

def attend(queries, keys, values):
    length_here = queries.shape[0]
    block_rows = math.gcd(length_here, 512)
    blocked = queries.reshape(length_here // block_rows, block_rows, D)
    mapped = lax.map(jax.checkpoint(lambda query_block: attend_block(query_block, keys, values)), blocked)
    return mapped.reshape(length_here, D)

def segment_forward(inputs, signal, source_rows, weights, gains):
    time_weight, attn_query, attn_key, attn_value, attn_out, cross_query, cross_key, cross_value, cross_out, ffn_in, ffn_out = weights
    resid = inputs + highest(low(signal)[None, :], time_weight)
    normed_one = low(layer_norm(resid, gains[:, 0]))
    queries = low(low_back(highest(normed_one, attn_query)))
    keys = low(low_back(highest(normed_one, attn_key)))
    values = low(low_back(highest(normed_one, attn_value)))
    attended = low(low_back(attend(queries, keys, values)))
    mid = resid + low_back(highest(attended, attn_out))
    normed_two = low(layer_norm(mid, gains[:, 1]))
    cross_q = low(low_back(highest(normed_two, cross_query)))
    cross_keys = low(low_back(highest(source_rows, cross_key)))
    cross_values = low(low_back(highest(source_rows, cross_value)))
    crossed = low(low_back(attend(cross_q, cross_keys, cross_values)))
    late = mid + low_back(highest(crossed, cross_out))
    normed_three = low(layer_norm(late, gains[:, 2]))
    inner = low_back(highest(normed_three, ffn_in))
    active = low(jax.nn.gelu(inner, approximate=False))
    return late + low_back(highest(active, ffn_out))

def reference(decoder_input, timesteps, memory, cotangent, time_weight, attn_query, attn_key, attn_value, attn_out, cross_query, cross_key, cross_value, cross_out, ffn_in, ffn_out, norm_gains):
    weights = tuple((matrix.astype(jnp.float32) for matrix in (time_weight, attn_query, attn_key, attn_value, attn_out, cross_query, cross_key, cross_value, cross_out, ffn_in, ffn_out)))
    inputs = decoder_input.astype(jnp.float32)
    sources = memory.astype(jnp.float32)
    signals = step_signal(timesteps)
    group_size = math.gcd(SEGMENTS, max(1, 4096 // LEN))
    group_count = SEGMENTS // group_size

    def forward(inputs, sources, weights, gains):

        def one_segment(seg_input, seg_signal, seg_source):
            return segment_forward(seg_input, seg_signal, seg_source, weights, gains)
        run_group = jax.checkpoint(jax.vmap(one_segment))

        def one_group(carried, group_item):
            return (carried, run_group(group_item[0], group_item[1], group_item[2]))
        packed = (inputs.reshape(group_count, group_size, LEN, D), signals.reshape(group_count, group_size, D), sources.reshape(group_count, group_size, SRC, D))
        _, outputs = lax.scan(one_group, jnp.zeros((), jnp.float32), packed)
        return outputs.reshape(SEGMENTS, LEN, D)
    result, pullback = jax.vjp(forward, inputs, sources, weights, norm_gains)
    grad_inputs, grad_sources, grad_weights, grad_norms = pullback(cotangent.astype(jnp.float32))
    squares = jnp.sum(grad_norms * grad_norms)
    for grad_item in grad_weights:
        squares = squares + jnp.sum(grad_item * grad_item)
    limit = math.sqrt(9 * D * D + 2 * D * FF + 3 * D)
    factor = jnp.minimum(1.0, limit * lax.rsqrt(squares))
    clipped = tuple((grad_item * factor for grad_item in grad_weights))
    return (result.astype(jnp.bfloat16), grad_inputs.astype(jnp.bfloat16), grad_sources.astype(jnp.bfloat16), clipped[0], clipped[1], clipped[2], clipped[3], clipped[4], clipped[5], clipped[6], clipped[7], clipped[8], clipped[9], clipped[10], grad_norms * factor)
```

```python
import functools
import math

import jax
import jax.numpy as jnp
from jax import lax
from jax.experimental import pallas as pl
from jax.experimental.pallas import tpu as pltpu
from jax.sharding import PartitionSpec as P

D = 512
HEADS = 8
HEAD = 64
FF = 2048
PAIRS = HEADS // 2
PAIR = 2 * HEAD
CHUNKS = FF // D
BF = jnp.bfloat16
F32 = jnp.float32
SCALE = 1.0 / math.sqrt(HEAD)
ROOT_HALF = math.sqrt(0.5)
BELL = 1.0 / math.sqrt(2.0 * math.pi)


def dot(a, b, ca=1, cb=0):
    return lax.dot_general(a, b, (((ca,), (cb,)), ((), ())), preferred_element_type=F32)


def row_mean(v):
    return jnp.sum(v, axis=-1, keepdims=True) * (1.0 / v.shape[-1])


def norm_parts(v):
    centred = v - row_mean(v)
    scale = lax.rsqrt(row_mean(centred * centred) + 1e-05)
    return centred * scale, scale


def norm_back(v, gain, grad):
    normed, scale = norm_parts(v)
    c = grad * gain
    gain_part = jnp.sum(grad * normed, axis=0, keepdims=True)
    return scale * (c - row_mean(c) - normed * row_mean(c * normed)), gain_part


def build(dst, src, which, me):
    blocks, _, rows, _ = src.shape
    for b in range(blocks):
        dst[rows * b : rows * (b + 1), :] = src[b ^ me, which]


def put(ref, at, mat):
    mat = mat.astype(ref.dtype)
    if len(ref.shape) == 3:
        ref[at] = mat
        return
    rb, cb, _, cols = ref.shape
    rows = D // rb
    for a in range(rb):
        for j in range(cb):
            ref[a, j, rows * at : rows * (at + 1), :] = mat[
                rows * a : rows * (a + 1), cols * j : cols * (j + 1)
            ]


def attend(i, qT, k, vT, oT, lse):
    n = qT.shape[2]
    row = lax.broadcasted_iota(jnp.int32, (PAIR, n), 0)
    zero = jnp.zeros((), BF)
    scores = []
    for h in range(2):
        mine = jnp.where((row // HEAD) == h, qT[i], zero)
        scores.append(dot(k[i], mine))
    for h in range(2):
        top = jnp.max(scores[h], axis=0, keepdims=True)
        e = jnp.exp(scores[h] - top)
        total = jnp.sum(e, axis=0, keepdims=True)
        out = dot(vT[i, HEAD * h : HEAD * (h + 1), :], e.astype(BF))
        oT[i, HEAD * h : HEAD * (h + 1), :] = (out * (1.0 / total)).astype(BF)
        lse[0, h : h + 1, :] = top + jnp.log(total)


def attend_back(i, q, qT, k, kT, v, g, gT, lse, delta, dqT, dk, dv):
    n = qT.shape[2]
    block = min(n, 512)
    row = lax.broadcasted_iota(jnp.int32, (PAIR, block), 0)
    lane = lax.broadcasted_iota(jnp.int32, (block, PAIR), 1)
    zero = jnp.zeros((), BF)
    acc_k = acc_v = None
    for j in range(n // block):
        at = slice(j * block, (j + 1) * block)
        for h in range(2):
            mine = jnp.where((row // HEAD) == h, qT[i, :, at], zero)
            s = dot(k[i], mine)
            dp = dot(v[i], jnp.where((row // HEAD) == h, gT[i, :, at], zero))
            p = jnp.exp(s - lse[0, h : h + 1, at])
            ds = (p * (dp - delta[i, h : h + 1, at])).astype(BF)
            one_v = dot(p.astype(BF), jnp.where((lane // HEAD) == h, g[i, at, :], zero))
            one_k = dot(ds, jnp.where((lane // HEAD) == h, q[i, at, :], zero))
            own = slice(HEAD * h, HEAD * (h + 1))
            dqT[i, own, at] = (dot(kT[i, own, :], ds) * SCALE).astype(BF)
            acc_v = one_v if acc_v is None else acc_v + one_v
            acc_k = one_k if acc_k is None else acc_k + one_k
    dk[i] = (acc_k * SCALE).astype(BF)
    dv[i] = acc_v.astype(BF)


def pairs_in(dst, src):
    for p in range(PAIRS):
        dst[p] = src[:, PAIR * p : PAIR * (p + 1)]


def pairs_in_T(dst, src, scale=None):
    for p in range(PAIRS):
        t = src[:, PAIR * p : PAIR * (p + 1)].T
        dst[p] = t if scale is None else t * jnp.asarray(scale, BF)


def from_pairs(src):
    return jnp.concatenate([src[p] for p in range(PAIRS)], axis=1)


def from_pairs_T(src):
    return jnp.concatenate([src[p].T for p in range(PAIRS)], axis=1)


def self_forward(me, x, emb, gains, g1, g2, n1, q, k, v, lse, att, mid, n2, cq, w, qs, ks, vs, qT, vT, oT):
    i = pl.program_id(0)

    @pl.when(i == 0)
    def _():
        resid = x[...].astype(F32) + emb[...]
        normed = (norm_parts(resid)[0] * gains[0:1, :]).astype(BF)
        n1[...] = normed
        for t, dst in ((1, qs), (2, ks), (3, vs)):
            build(w, g1, t, me[0])
            pairs_in(dst, dot(normed, w[...]).astype(BF))
        for p in range(PAIRS):
            qT[p] = qs[p].T * jnp.asarray(SCALE, BF)
            vT[p] = vs[p].T

    attend(i, qT, ks, vT, oT, lse)
    q[...] = qs[i]
    k[...] = ks[i]
    v[...] = vs[i]

    @pl.when(i == PAIRS - 1)
    def _():
        joined = from_pairs_T(oT)
        att[...] = joined
        build(w, g2, 0, me[0])
        new = x[...].astype(F32) + emb[...] + dot(joined, w[...])
        mid[...] = new
        normed = (norm_parts(new)[0] * gains[1:2, :]).astype(BF)
        n2[...] = normed
        build(w, g2, 1, me[0])
        cq[...] = dot(normed, w[...]).astype(BF)


def cross_forward(me, mem, cq, mid, gains, g2, k, v, lse, crossed, late, n3, w, ks, vs, qT, vT, oT):
    i = pl.program_id(0)

    @pl.when(i == 0)
    def _():
        for t, dst in ((2, ks), (3, vs)):
            build(w, g2, t, me[0])
            pairs_in(dst, dot(mem[...], w[...]).astype(BF))
        pairs_in_T(qT, cq, SCALE)
        for p in range(PAIRS):
            vT[p] = vs[p].T

    attend(i, qT, ks, vT, oT, lse)
    k[...] = ks[i]
    v[...] = vs[i]

    @pl.when(i == PAIRS - 1)
    def _():
        joined = from_pairs_T(oT)
        crossed[...] = joined
        build(w, g2, 4, me[0])
        new = mid[...] + dot(joined, w[...])
        late[...] = new
        n3[...] = (norm_parts(new)[0] * gains[2:3, :]).astype(BF)


def feed_forward(me, n3, late, cot, gains, g3, out, gl, bt, gain3, raw, win, wout, n3T, acc, gacc):
    i = pl.program_id(0)
    blocks, _, rows, _ = g3.shape

    @pl.when(i == 0)
    def _():
        n3T[...] = n3[...].T
        acc[...] = late[...]
        gacc[...] = jnp.zeros_like(gacc)

    build(win, g3, i, me[0])
    if blocks == 1:
        wout[...] = g3[0, CHUNKS + i]
    else:
        each = blocks // CHUNKS
        for u in range(each):
            for t in range(CHUNKS):
                lo = rows * (CHUNKS * u + t)
                wout[lo : lo + rows, :] = g3[(each * i + u) ^ me[0], CHUNKS + t]
    inner = dot(n3[...], win[...])
    share = 0.5 * (1.0 + lax.erf(inner * ROOT_HALF))
    active = (inner * share).astype(BF)
    acc[...] += dot(active, wout[...])
    grad_active = dot(cot[...], wout[...], 1, 1)
    slope = share + inner * (jnp.exp(-0.5 * inner * inner) * BELL)
    grad_inner = (slope * grad_active).astype(BF)
    raw_out = dot(active, cot[...], 0, 0).astype(BF)
    raw_in = dot(n3T[...], grad_inner).astype(BF)
    gacc[...] += dot(grad_inner, win[...], 1, 1)
    if blocks == 1:
        raw[i] = raw_in
        raw[CHUNKS + i] = raw_out
    else:
        cols = D // CHUNKS
        for a in range(blocks):
            for t in range(CHUNKS):
                raw[a, i, rows * t : rows * (t + 1), :] = raw_in[
                    rows * a : rows * (a + 1), cols * t : cols * (t + 1)
                ]
        tall = D // each
        for u in range(each):
            for j in range(CHUNKS):
                raw[each * i + u, j, tall : 2 * tall, :] = raw_out[
                    tall * u : tall * (u + 1), cols * j : cols * (j + 1)
                ]

    @pl.when(i == CHUNKS - 1)
    def _():
        out[...] = acc[...].astype(BF)
        part, gain_part = norm_back(late[...], gains[2:3, :], gacc[...])
        gain3[...] = gain_part
        total = cot[...].astype(F32) + part
        gl[...] = total
        bt[...] = total.astype(BF)


def start_back(branch, weight, joined, g, gT, delta):
    grad = dot(branch, weight, 1, 1).astype(BF)
    pairs_in(g, grad)
    for p in range(PAIRS):
        gT[p] = g[p].T
        other = joined[:, PAIR * p : PAIR * (p + 1)].T
        both = gT[p].astype(F32) * other.astype(F32)
        for h in range(2):
            delta[p, h : h + 1, :] = jnp.sum(both[HEAD * h : HEAD * (h + 1), :], axis=0, keepdims=True)


def cross_back(
    me, bt, gl, crossed, cq, k, v, lse, mem, n2, mid, gains, g2, att,
    raw, mem_grad, gm, b1, gain2,
    w, q, qT, ks, kT, vs, g, gT, delta, dqT, dk, dv,
):
    i = pl.program_id(0)

    @pl.when(i == 0)
    def _():
        build(w, g2, 4, me[0])
        start_back(bt[...], w[...], crossed, g, gT, delta)
        put(raw, 0, dot(crossed[...].T, bt[...]))
        pairs_in(q, cq)
        pairs_in_T(qT, cq, SCALE)
        pairs_in(ks, k)
        pairs_in_T(kT, k)
        pairs_in(vs, v)

    attend_back(i, q, qT, ks, kT, vs, g, gT, lse, delta, dqT, dk, dv)

    @pl.when(i == PAIRS - 1)
    def _():
        grad_q = from_pairs_T(dqT)
        grad_k = from_pairs(dk)
        grad_v = from_pairs(dv)
        put(raw, 1, dot(n2[...].T, grad_q))
        mT = mem[...].T
        put(raw, 2, dot(mT, grad_k))
        put(raw, 3, dot(mT, grad_v))
        build(w, g2, 1, me[0])
        part, gain_part = norm_back(mid[...], gains[1:2, :], dot(grad_q, w[...], 1, 1))
        gain2[...] = gain_part
        total = gl[...] + part
        gm[...] = total
        low = total.astype(BF)
        b1[...] = low
        put(raw, 4, dot(att[...].T, low))
        build(w, g2, 2, me[0])
        back = dot(grad_k, w[...], 1, 1)
        build(w, g2, 3, me[0])
        mem_grad[...] = (back + dot(grad_v, w[...], 1, 1)).astype(BF)


def self_back(
    me, b1, att, qn, k, v, lse, n1, g1, g2,
    raw, gn,
    w, q, qT, ks, kT, vs, g, gT, delta, dqT, dk, dv,
):
    i = pl.program_id(0)

    @pl.when(i == 0)
    def _():
        build(w, g2, 0, me[0])
        start_back(b1[...], w[...], att, g, gT, delta)
        pairs_in(q, qn)
        pairs_in_T(qT, qn, SCALE)
        pairs_in(ks, k)
        pairs_in_T(kT, k)
        pairs_in(vs, v)

    attend_back(i, q, qT, ks, kT, vs, g, gT, lse, delta, dqT, dk, dv)

    @pl.when(i == PAIRS - 1)
    def _():
        nT = n1[...].T
        grads = (from_pairs_T(dqT), from_pairs(dk), from_pairs(dv))
        for t in range(3):
            put(raw, t, dot(nT, grads[t]))
        total = None
        for t in range(3):
            build(w, g1, t + 1, me[0])
            one = dot(grads[t], w[...], 1, 1)
            total = one if total is None else total + one
        gn[...] = total


def finish_back(x, emb, gm, gn, gains, grad, sums):
    part, gain_part = norm_back(x[...].astype(F32) + emb[...], gains[0:1, :], gn[...])
    total = gm[...] + part
    grad[...] = total.astype(BF)
    sums[0:1, :] = jnp.sum(total, axis=0, keepdims=True)
    sums[1:2, :] = gain_part


def full(shape):
    return pl.BlockSpec(shape, lambda i: (0,) * len(shape))


def call(body, name, args, outs, scratch, steps, flops, limit=48):
    in_specs = [pl.BlockSpec(memory_space=pltpu.SMEM)]
    arrays = [args[0]]
    for a in args[1:]:
        if isinstance(a, tuple):
            arrays.append(a[0])
            in_specs.append(a[1])
        else:
            arrays.append(a)
            in_specs.append(full(a.shape))
    size = sum(math.prod(a.shape) * a.dtype.itemsize for a in arrays)
    size += sum(math.prod(s) * jnp.dtype(t).itemsize for s, t, _ in outs)
    return pl.pallas_call(
        body,
        grid=(steps,),
        in_specs=in_specs,
        out_specs=tuple(full(s) if b is None else b for s, _, b in outs),
        out_shape=tuple(jax.ShapeDtypeStruct(s, t) for s, t, _ in outs),
        scratch_shapes=scratch,
        compiler_params=pltpu.CompilerParams(vmem_limit_bytes=limit * 2**20),
        cost_estimate=pl.CostEstimate(flops=int(flops), bytes_accessed=size, transcendentals=0),
        name=name,
    )(*arrays)


def step_signal(step_ids, feat_width):
    half_width = feat_width // 2
    frequency = jnp.exp(-math.log(10000.0) * jnp.arange(half_width, dtype=F32) / half_width)
    angles = step_ids.astype(F32)[:, None] * frequency[None, :]
    return jnp.concatenate([jnp.sin(angles), jnp.cos(angles)], axis=1)


def segment_layer(me, x, emb, mem, cot, gains, g1, g2, g3, blocked):
    n = x.shape[0]
    r = mem.shape[0]
    nat = pl.BlockSpec((n, PAIR), lambda i: (0, i))
    nat_r = pl.BlockSpec((r, PAIR), lambda i: (0, i))
    rows2 = pl.BlockSpec((1, 2, n), lambda i: (i, 0, 0))
    wide = lambda m: pltpu.VMEM((PAIRS, m, PAIR), BF)
    tall = lambda m: pltpu.VMEM((PAIRS, PAIR, m), BF)
    weight = pltpu.VMEM((D, D), BF)
    proj = 2 * n * D * D * 1.5
    att = 2 * n * r * D * 5
    lse_out = ((PAIRS, 2, n), F32, rows2)
    n1, q, k, v, lse1, attended, mid, n2, cq = call(
        self_forward, "self_forward", (me, x, emb, gains, g1, g2),
        [((n, D), BF, None)] + [((n, D), BF, nat)] * 3
        + [lse_out, ((n, D), BF, None), ((n, D), F32, None), ((n, D), BF, None), ((n, D), BF, None)],
        [weight, wide(n), wide(n), wide(n), tall(n), tall(n), tall(n)],
        PAIRS, 5 * proj + 2 * att,
    )
    ck, cv, lse2, crossed, late, n3 = call(
        cross_forward, "cross_forward", (me, mem, cq, mid, gains, g2),
        [((r, D), BF, nat_r)] * 2 + [lse_out, ((n, D), BF, None), ((n, D), F32, None), ((n, D), BF, None)],
        [weight, wide(r), wide(r), tall(n), tall(r), tall(n)],
        PAIRS, 3 * proj + 2 * att,
    )

    def raw_shape(count):
        if blocked is None:
            return ((count, D, D), BF, None)
        dp, cols = blocked
        return ((dp, cols, count * D // dp, D // cols), BF, None)

    out, gl, bt, gain3, raw3 = call(
        feed_forward, "feed_forward", (me, n3, late, cot, gains, g3),
        [((n, D), BF, None), ((n, D), F32, None), ((n, D), BF, None), ((1, D), F32, None), raw_shape(2 * CHUNKS)],
        [weight, weight, pltpu.VMEM((D, n), BF), pltpu.VMEM((n, D), F32), pltpu.VMEM((n, D), F32)],
        CHUNKS, 24 * proj,
    )
    back_scratch = lambda m: [
        weight, wide(n), tall(n), wide(m), tall(m), wide(m), wide(n), tall(n),
        pltpu.VMEM((PAIRS, 2, n), F32), tall(n), wide(m), wide(m),
    ]
    raw2, mem_grad, gm, b1, gain2 = call(
        cross_back, "cross_back",
        (me, bt, gl, crossed, cq, ck, cv, (lse2, rows2), mem, n2, mid, gains, g2, attended),
        [raw_shape(5), ((r, D), BF, None), ((n, D), F32, None), ((n, D), BF, None), ((1, D), F32, None)],
        back_scratch(r), PAIRS, 9 * proj + 5 * att,
    )
    raw1, gn = call(
        self_back, "self_back",
        (me, b1, attended, q, k, v, (lse1, rows2), n1, g1, g2),
        [raw_shape(3), ((n, D), F32, None)],
        back_scratch(n), PAIRS, 7 * proj + 5 * att,
    )

    def last(me_ref, *refs):
        finish_back(*refs)

    input_grad, sums = call(
        last, "finish_back", (me, x, emb, gm, gn, gains),
        [((n, D), BF, None), ((2, D), F32, None)], [], 1, 100 * n * D,
    )
    return out, input_grad, mem_grad, (raw1, raw2, raw3), sums, gain2, gain3


def per_device(
    decoder_input, timesteps, memory, cotangent, time_weight, attn_query, attn_key, attn_value, attn_out,
    cross_query, cross_key, cross_value, cross_out, ffn_in, ffn_out, norm_gains,
):
    dp = lax.axis_size("dp")
    mem_count = lax.axis_size("mem")
    rows = D // dp
    blocked = (dp, mem_count) if rows % 16 == 0 and mem_count == CHUNKS and dp % CHUNKS == 0 else None

    def gather(parts):
        got = lax.all_gather(jnp.stack(parts, 0), "dp", axis=0, tiled=False)
        if blocked is None:
            got = got.transpose(1, 0, 2, 3).reshape(1, len(parts), D, D)
        return got

    g1 = gather((time_weight, attn_query, attn_key, attn_value))
    g2 = gather((attn_out, cross_query, cross_key, cross_value, cross_out))
    in_parts = [ffn_in[:, D * c : D * (c + 1)] for c in range(CHUNKS)]
    if blocked is None:
        whole_out = lax.all_gather(ffn_out, "dp", axis=0, tiled=True).reshape(1, CHUNKS, D, D)
        g3 = jnp.concatenate([gather(in_parts), whole_out], axis=1)
    else:
        g3 = gather(in_parts + [ffn_out[rows * c : rows * (c + 1)] for c in range(CHUNKS)])
    me = jnp.zeros((1,), jnp.int32)
    mem_rows = lax.all_to_all(memory, "mem", split_axis=0, concat_axis=1, tiled=True)[0]
    signal = step_signal(timesteps, D).astype(BF)
    w_time = g1[:, 0].reshape(D, D)
    emb = jnp.dot(signal, w_time, preferred_element_type=F32)
    out, input_grad, mem_grad, raws, sums, gain2, gain3 = segment_layer(
        me, decoder_input[0], emb, mem_rows, cotangent[0], norm_gains.T, g1, g2, g3, blocked
    )
    memory_grad = lax.all_to_all(mem_grad[None], "mem", split_axis=1, concat_axis=0, tiled=True)

    def scatter(raw):
        if blocked is None:
            count = raw.shape[0]
            part = lax.psum_scatter(raw, "dp", scatter_dimension=1, tiled=True)
            part = lax.psum_scatter(part, "mem", scatter_dimension=2, tiled=True)
            return [part[t].astype(F32) for t in range(count)]
        part = lax.psum_scatter(raw, "dp", scatter_dimension=0, tiled=False)
        part = lax.psum_scatter(part, "mem", scatter_dimension=0, tiled=False).astype(F32)
        return [part[rows * t : rows * (t + 1)] for t in range(part.shape[0] // rows)]

    if blocked is None:
        raw3 = raws[2]
        part = scatter(raw3[:CHUNKS].transpose(1, 0, 2).reshape(1, D, FF))
        ffn_in_grad = part[0]
        ffn_out_grad = scatter(raw3[CHUNKS:].reshape(1, FF, D))[0]
    else:
        part = scatter(raws[2])
        ffn_in_grad = jnp.concatenate(part[:CHUNKS], axis=1)
        ffn_out_grad = jnp.concatenate(part[CHUNKS:], axis=0)
    d_query, d_key, d_value = scatter(raws[0])
    d_cout, d_cquery, d_ckey, d_cvalue, d_out = scatter(raws[1])
    packed = jnp.concatenate([sums, gain2, gain3, signal.astype(F32)], axis=0)
    everyone = lax.all_gather(packed, ("dp", "mem"), axis=0, tiled=False)
    row0 = lax.axis_index("dp") * rows
    cols = D // mem_count
    col0 = lax.axis_index("mem") * cols
    my_signal = lax.dynamic_slice_in_dim(everyone[:, 4], row0, rows, axis=1)
    my_sums = lax.dynamic_slice_in_dim(everyone[:, 0], col0, cols, axis=1)
    d_time = jnp.dot(my_signal.T, my_sums, precision=lax.Precision.HIGHEST)
    all_gains = jnp.sum(everyone[:, 1:4], axis=0)
    d_gains = lax.dynamic_slice_in_dim(all_gains, row0, rows, axis=1).T
    weights = [
        d_time, d_query, d_key, d_value, d_out, d_cquery, d_ckey, d_cvalue, d_cout, ffn_in_grad, ffn_out_grad,
    ]
    local = sum(jnp.sum(w * w) for w in weights)
    squares = lax.psum(local, ("dp", "mem")) + jnp.sum(all_gains * all_gains)
    limit = math.sqrt(9 * D * D + 2 * D * FF + 3 * D)
    factor = jnp.minimum(1.0, limit * lax.rsqrt(squares))
    return (out[None], input_grad[None], memory_grad) + tuple(w * factor for w in weights) + (d_gains * factor,)


def solution(mesh):
    tokens = P(("dp", "mem"), None, None)
    weight = P("dp", None)
    in_specs = (tokens, P(("dp", "mem")), P("dp", "mem", None), tokens) + (weight,) * 11 + (P(),)
    out_specs = (tokens, tokens, P("dp", "mem", None)) + (P("dp", "mem"),) * 11 + (P("dp", None),)
    return jax.shard_map(per_device, mesh=mesh, in_specs=in_specs, out_specs=out_specs, check_vma=False)
```

```python
import functools
import math

import jax
import jax.numpy as jnp
from jax import lax
from jax.experimental import pallas as pl
from jax.experimental.pallas import tpu as pltpu
from jax.sharding import PartitionSpec as P

D = 512
HEADS = 8
HEAD = 64
FF = 2048
PAIRS = HEADS // 2
PAIR = 2 * HEAD
CHUNKS = FF // D
BF = jnp.bfloat16
F32 = jnp.float32
SCALE = 1.0 / math.sqrt(HEAD)
ROOT_HALF = math.sqrt(0.5)
BELL = 1.0 / math.sqrt(2.0 * math.pi)


def dot(a, b, ca=1, cb=0):
    return lax.dot_general(a, b, (((ca,), (cb,)), ((), ())), preferred_element_type=F32)


def row_mean(v):
    return jnp.sum(v, axis=-1, keepdims=True) * (1.0 / v.shape[-1])


def norm_parts(v):
    centred = v - row_mean(v)
    scale = lax.rsqrt(row_mean(centred * centred) + 1e-05)
    return centred * scale, scale


def norm_back(v, gain, grad):
    normed, scale = norm_parts(v)
    c = grad * gain
    gain_part = jnp.sum(grad * normed, axis=0, keepdims=True)
    return scale * (c - row_mean(c) - normed * row_mean(c * normed)), gain_part


def build(w, slot, parts, which, me):
    dst = w.at[slot]
    if len(parts) == 1:
        blocks, _, rows, _ = parts[0].shape
        for b in range(blocks):
            dst[rows * b : rows * (b + 1), :] = parts[0][b, which]
        return
    rows = parts[0].shape[1]
    for r, part in enumerate(parts):
        lo = pl.multiple_of((r ^ me) * rows, rows)
        dst[pl.ds(lo, rows), :] = part[which]


def put(refs, at, mat, core):
    mat = mat.astype(refs[0].dtype)
    if len(refs) == 1:
        refs[0][at] = mat
        return
    half, cb, _, cols = refs[0].shape
    rows = D // (2 * half)

    def cut(own, other):
        for a in range(2 * half):
            ref = own if a % 2 == 0 else other
            for j in range(cb):
                ref[a // 2, j, rows * at : rows * (at + 1), :] = mat[
                    rows * a : rows * (a + 1), cols * j : cols * (j + 1)
                ]

    @pl.when(core == 0)
    def _():
        cut(refs[0], refs[1])

    @pl.when(core == 1)
    def _():
        cut(refs[1], refs[0])


def attend(i, qT, k, vT, oT, lse):
    n = qT.shape[2]
    row = lax.broadcasted_iota(jnp.int32, (PAIR, n), 0)
    zero = jnp.zeros((), BF)
    scores = []
    for h in range(2):
        mine = jnp.where((row // HEAD) == h, qT[i], zero)
        scores.append(dot(k[i], mine))
    for h in range(2):
        top = jnp.max(scores[h], axis=0, keepdims=True)
        e = jnp.exp(scores[h] - top)
        total = jnp.sum(e, axis=0, keepdims=True)
        out = dot(vT[i, HEAD * h : HEAD * (h + 1), :], e.astype(BF))
        oT[i, HEAD * h : HEAD * (h + 1), :] = (out * (1.0 / total)).astype(BF)
        lse[0, h : h + 1, :] = top + jnp.log(total)


def attend_back(i, q, qT, k, kT, v, g, gT, lse, delta, dqT, dk, dv):
    n = qT.shape[2]
    block = min(n, 512)
    row = lax.broadcasted_iota(jnp.int32, (PAIR, block), 0)
    lane = lax.broadcasted_iota(jnp.int32, (block, PAIR), 1)
    zero = jnp.zeros((), BF)
    acc_k = acc_v = None
    for j in range(n // block):
        at = slice(j * block, (j + 1) * block)
        for h in range(2):
            mine = jnp.where((row // HEAD) == h, qT[i, :, at], zero)
            s = dot(k[i], mine)
            dp = dot(v[i], jnp.where((row // HEAD) == h, gT[i, :, at], zero))
            p = jnp.exp(s - lse[0, h : h + 1, at])
            ds = (p * (dp - delta[i, h : h + 1, at])).astype(BF)
            one_v = dot(p.astype(BF), jnp.where((lane // HEAD) == h, g[i, at, :], zero))
            one_k = dot(ds, jnp.where((lane // HEAD) == h, q[i, at, :], zero))
            own = slice(HEAD * h, HEAD * (h + 1))
            dqT[i, own, at] = (dot(kT[i, own, :], ds) * SCALE).astype(BF)
            acc_v = one_v if acc_v is None else acc_v + one_v
            acc_k = one_k if acc_k is None else acc_k + one_k
    dk[i] = (acc_k * SCALE).astype(BF)
    dv[i] = acc_v.astype(BF)


def pairs_in(dst, src):
    for p in range(PAIRS):
        dst[p] = src[:, PAIR * p : PAIR * (p + 1)]


def pairs_in_T(dst, src, scale=None):
    for p in range(PAIRS):
        t = src[:, PAIR * p : PAIR * (p + 1)].T
        dst[p] = t if scale is None else t * jnp.asarray(scale, BF)


def from_pairs(src):
    return jnp.concatenate([src[p] for p in range(PAIRS)], axis=1)


def from_pairs_T(src):
    return jnp.concatenate([src[p].T for p in range(PAIRS)], axis=1)


def rows_of(mem):
    return jnp.concatenate([m[...] for m in mem], axis=0) if len(mem) > 1 else mem[0][...]


def self_forward(me, x, sig, gains, g1, emb, n1, q, k, v, lse, att, w, n1s, qs, ks, vs, qT, vT, oT):
    i = pl.program_id(0)

    @pl.when(i == 0)
    def _():
        build(w, 0, g1, 0, me[0])
        embedded = dot(sig[...], w[0])[0:1, :]
        emb[...] = embedded
        resid = x[...].astype(F32) + embedded
        normed = (norm_parts(resid)[0] * gains[0:1, :]).astype(BF)
        pairs_in(n1s, normed)
        for t, dst in ((1, qs), (2, ks), (3, vs)):
            build(w, t, g1, t, me[0])
            pairs_in(dst, dot(normed, w[t]).astype(BF))
        for p in range(PAIRS):
            qT[p] = qs[p].T * jnp.asarray(SCALE, BF)
            vT[p] = vs[p].T

    attend(i, qT, ks, vT, oT, lse)
    n1[...] = n1s[i]
    q[...] = qs[i]
    k[...] = ks[i]
    v[...] = vs[i]
    att[...] = oT[i].T


def cross_forward(
    me, x, emb, att, mem, gains, g2, mid, n2, cq, k, v, lse, crossed, w, mids, n2s, qs, ks, vs, qT, vT, oT
):
    i = pl.program_id(0)

    @pl.when(i == 0)
    def _():
        build(w, 0, g2, 0, me[0])
        new = x[...].astype(F32) + emb[...] + dot(att[...], w[0])
        pairs_in(mids, new)
        normed = (norm_parts(new)[0] * gains[1:2, :]).astype(BF)
        pairs_in(n2s, normed)
        build(w, 1, g2, 1, me[0])
        pairs_in(qs, dot(normed, w[1]).astype(BF))
        rows = rows_of(mem)
        for t, dst in ((2, ks), (3, vs)):
            build(w, t, g2, t, me[0])
            pairs_in(dst, dot(rows, w[t]).astype(BF))
        for p in range(PAIRS):
            qT[p] = qs[p].T * jnp.asarray(SCALE, BF)
            vT[p] = vs[p].T

    attend(i, qT, ks, vT, oT, lse)
    mid[...] = mids[i]
    n2[...] = n2s[i]
    cq[...] = qs[i]
    k[...] = ks[i]
    v[...] = vs[i]
    crossed[...] = oT[i].T


def feed_forward(
    me, mid, crossed, cot, gains, g2, fin, fout, out, gl, bt, gain3, raw, wlate, win, wout, n3, n3T, late, acc, gacc
):
    i = pl.program_id(0)
    blocks, _, rows, _ = fin.shape

    @pl.when(i == 0)
    def _():
        build(wlate, 0, g2, 0, me[0])
        new = mid[...] + dot(crossed[...], wlate[0])
        late[...] = new
        normed = (norm_parts(new)[0] * gains[2:3, :]).astype(BF)
        n3[...] = normed
        n3T[...] = normed.T

    for b in range(blocks):
        win[rows * b : rows * (b + 1), :] = fin[b, 0]
    each, per, tall, _ = fout.shape
    for u in range(each):
        for t in range(per):
            lo = tall * (per * u + t)
            wout[lo : lo + tall, :] = fout[u, t]
    inner = dot(n3[...], win[...])
    share = 0.5 * (1.0 + lax.erf(inner * ROOT_HALF))
    active = (inner * share).astype(BF)
    one = dot(active, wout[...])
    grad_active = dot(cot[...], wout[...], 1, 1)
    slope = share + inner * (jnp.exp(-0.5 * inner * inner) * BELL)
    grad_inner = (slope * grad_active).astype(BF)
    raw_out = dot(active, cot[...], 0, 0).astype(BF)
    raw_in = dot(n3T[...], grad_inner).astype(BF)
    back = dot(grad_inner, win[...], 1, 1)

    @pl.when(i == 0)
    def _():
        acc[...] = late[...] + one
        gacc[...] = back

    @pl.when(i > 0)
    def _():
        acc[...] += one
        gacc[...] += back

    if blocks == 1:
        raw[i] = raw_in
        raw[CHUNKS + i] = raw_out
    else:
        cols = D // CHUNKS
        for a in range(blocks):
            for t in range(CHUNKS):
                raw[a, i, rows * t : rows * (t + 1), :] = raw_in[
                    rows * a : rows * (a + 1), cols * t : cols * (t + 1)
                ]
        tall = D // each
        for u in range(each):
            for j in range(CHUNKS):
                raw[each * i + u, j, tall : 2 * tall, :] = raw_out[
                    tall * u : tall * (u + 1), cols * j : cols * (j + 1)
                ]

    @pl.when(i == CHUNKS - 1)
    def _():
        out[...] = acc[...].astype(BF)
        part, gain_part = norm_back(late[...], gains[2:3, :], gacc[...])
        gain3[...] = gain_part
        total = cot[...].astype(F32) + part
        gl[...] = total
        bt[...] = total.astype(BF)


def start_back(branch, weight, joined, g, gT, delta):
    grad = dot(branch, weight, 1, 1).astype(BF)
    pairs_in(g, grad)
    for p in range(PAIRS):
        gT[p] = g[p].T
        other = joined[:, PAIR * p : PAIR * (p + 1)].T
        both = gT[p].astype(F32) * other.astype(F32)
        for h in range(2):
            delta[p, h : h + 1, :] = jnp.sum(both[HEAD * h : HEAD * (h + 1), :], axis=0, keepdims=True)


def cross_back(
    me, bt, gl, crossed, cq, k, v, lse, mem, n2, mid, gains, g2, att,
    raw, mem_grad, gm, b1, gain2,
    w, q, qT, ks, kT, vs, g, gT, delta, dqT, dk, dv,
):
    i = pl.program_id(0)
    core = me[0] % 2

    @pl.when(i == 0)
    def _():
        build(w, 4, g2, 4, me[0])
        start_back(bt[...], w[4], crossed, g, gT, delta)
        put(raw, 0, dot(crossed[...].T, bt[...]), core)
        pairs_in(q, cq)
        pairs_in_T(qT, cq, SCALE)
        pairs_in(ks, k)
        pairs_in_T(kT, k)
        pairs_in(vs, v)

    attend_back(i, q, qT, ks, kT, vs, g, gT, lse, delta, dqT, dk, dv)

    @pl.when(i == PAIRS - 1)
    def _():
        grad_q = from_pairs_T(dqT)
        grad_k = from_pairs(dk)
        grad_v = from_pairs(dv)
        put(raw, 1, dot(n2[...].T, grad_q), core)
        mT = rows_of(mem).T
        put(raw, 2, dot(mT, grad_k), core)
        put(raw, 3, dot(mT, grad_v), core)
        build(w, 1, g2, 1, me[0])
        part, gain_part = norm_back(mid[...], gains[1:2, :], dot(grad_q, w[1], 1, 1))
        gain2[...] = gain_part
        total = gl[...] + part
        gm[...] = total
        low = total.astype(BF)
        b1[...] = low
        put(raw, 4, dot(att[...].T, low), core)
        build(w, 2, g2, 2, me[0])
        back = dot(grad_k, w[2], 1, 1)
        build(w, 3, g2, 3, me[0])
        back = (back + dot(grad_v, w[3], 1, 1)).astype(BF)
        size = back.shape[0] // len(mem_grad)
        for t, ref in enumerate(mem_grad):
            ref[...] = back[size * t : size * (t + 1)]


def self_back(
    me, b1, att, qn, k, v, lse, n1, g1, g2,
    raw, gn,
    w, q, qT, ks, kT, vs, g, gT, delta, dqT, dk, dv,
):
    i = pl.program_id(0)
    core = me[0] % 2

    @pl.when(i == 0)
    def _():
        build(w, 0, g2, 0, me[0])
        start_back(b1[...], w[0], att, g, gT, delta)
        pairs_in(q, qn)
        pairs_in_T(qT, qn, SCALE)
        pairs_in(ks, k)
        pairs_in_T(kT, k)
        pairs_in(vs, v)

    attend_back(i, q, qT, ks, kT, vs, g, gT, lse, delta, dqT, dk, dv)

    @pl.when(i == PAIRS - 1)
    def _():
        nT = n1[...].T
        grads = (from_pairs_T(dqT), from_pairs(dk), from_pairs(dv))
        for t in range(3):
            put(raw, t, dot(nT, grads[t]), core)
        total = None
        for t in range(3):
            build(w, t + 1, g1, t + 1, me[0])
            one = dot(grads[t], w[t + 1], 1, 1)
            total = one if total is None else total + one
        gn[...] = total


def finish_back(me, x, emb, gm, gn, gains, sig, gain2, gain3, grad, sums):
    part, gain_part = norm_back(x[...].astype(F32) + emb[...], gains[0:1, :], gn[...])
    total = gm[...] + part
    grad[...] = total.astype(BF)
    sums[0:1, :] = jnp.sum(total, axis=0, keepdims=True)
    sums[1:2, :] = gain_part
    sums[2:3, :] = gain2[...]
    sums[3:4, :] = gain3[...]
    sums[4:8, :] = sig[0:4, :].astype(F32)


def pack(me, *refs):
    out = refs[-1]
    rows = out.shape[1]
    at = 0
    for ref in refs[:-1]:
        for c in range(ref.shape[1] // D):
            for r in range(ref.shape[0] // rows):
                out[at] = ref[rows * r : rows * (r + 1), D * c : D * (c + 1)]
                at += 1


def add_core(me, keep, got, *outs):
    place = me[0] // 2
    for r, out in enumerate(outs):
        out[...] = keep[r ^ place] + got[r ^ place]


def add_plane(me, a, b, c, d, *outs):
    for r, out in enumerate(outs):
        at = r ^ me[1]
        total = a[at].astype(F32) + b[at].astype(F32) + c[at].astype(F32) + d[at].astype(F32)
        out[...] = total.astype(BF)


def fold(v):
    return jnp.sum((v * v).reshape(-1, 8, v.shape[-1]), axis=0)


def add_all(me, a, b, c, d, out, squares):
    total = a[...].astype(F32) + b[...].astype(F32) + c[...].astype(F32) + d[...].astype(F32)
    out[...] = total
    squares[...] = fold(total)


def take(me, src, *outs):
    for r, out in enumerate(outs):
        out[...] = src[r ^ me[1]]


def place_rows(me, a, b, c, d, out):
    for r, ref in enumerate((a, b, c, d)):
        out[r ^ me[1]] = ref[...]


def time_grad(me, *refs):
    rows, (grad, gain_grad, squares), (long, across) = refs[:-5], refs[-5:-2], refs[-2:]
    whole = jnp.concatenate([r[...].reshape(-1, 8, D) for r in rows], axis=0)
    cols = grad.shape[1]
    sums = whole[:, 0, :]
    signal = whole[:, 4, :]
    long[...] = lax.dot_general(
        signal, sums, (((0,), (0,)), ((), ())), preferred_element_type=F32, precision=lax.Precision.HIGHEST
    )
    n = grad.shape[0]
    mine = long[pl.ds(pl.multiple_of(me[0] * n, n), n), pl.ds(pl.multiple_of(me[1] * cols, cols), cols)]
    grad[...] = mine
    gains = jnp.sum(whole, axis=0)
    kind = lax.broadcasted_iota(jnp.int32, gains.shape, 0)
    gains = jnp.where((kind >= 1) & (kind <= 3), gains, 0.0)
    across[...] = jnp.concatenate([gains] * (128 // 8), axis=0).T
    gain_grad[...] = across[pl.ds(pl.multiple_of(me[0] * n, n), n), :]
    total = gains * gains
    count = sum(math.prod(r.shape) for r in rows) // (8 * D)
    shared = sum(total[:, 128 * t : 128 * (t + 1)] for t in range(D // 128)) * (1.0 / count)
    squares[...] = fold(mine) + shared


def scale_all(me, s0, s1, s2, s3, d_time, d_gains, a1, a2, a3, *outs):
    squares = jnp.sum(s0[...] + s1[...] + s2[...] + s3[...])
    limit = math.sqrt(9 * D * D + 2 * D * FF + 3 * D)
    factor = jnp.minimum(1.0, limit * lax.rsqrt(jnp.full((8, 128), squares, F32)))[0:1, :]
    o_time, o_q, o_k, o_v, o_out, o_cq, o_ck, o_cv, o_cout, o_in, o_fout, o_gains = outs
    o_time[...] = d_time[...] * factor
    rows = d_time.shape[0]
    for src, dsts in ((a1, (o_q, o_k, o_v)), (a2, (o_cout, o_cq, o_ck, o_cv, o_out))):
        for t, dst in enumerate(dsts):
            dst[...] = src[rows * t : rows * (t + 1), :] * factor
    for t in range(CHUNKS):
        o_in[:, 128 * t : 128 * (t + 1)] = a3[rows * t : rows * (t + 1), :].astype(F32) * factor
    o_fout[...] = a3[rows * CHUNKS :, :].astype(F32) * factor
    o_gains[...] = (d_gains[...] * factor)[:, 1:4]


def full(shape):
    return pl.BlockSpec(shape, lambda i: (0,) * len(shape), pipeline_mode=pl.Buffered(1))


def call(body, name, args, outs, scratch=(), steps=1, flops=0, limit=48):
    in_specs = [pl.BlockSpec(memory_space=pltpu.SMEM)]
    arrays = [args[0]]
    groups = [None]

    def take_in(a):
        if isinstance(a, tuple):
            arrays.append(a[0])
            in_specs.append(a[1])
        else:
            arrays.append(a)
            in_specs.append(full(a.shape))

    for a in args[1:]:
        groups.append(len(a) if isinstance(a, list) else None)
        for one in a if isinstance(a, list) else [a]:
            take_in(one)
    flat = []
    out_groups = []
    for o in outs:
        out_groups.append(len(o) if isinstance(o, list) else None)
        flat += o if isinstance(o, list) else [o]

    def grouped(refs, sizes):
        got, at = [], 0
        for size in sizes:
            got.append(refs[at] if size is None else list(refs[at : at + size]))
            at += size or 1
        return got

    def run(*refs):
        n_in, n_out = len(arrays), len(flat)
        body(
            *grouped(refs[:n_in], groups), *grouped(refs[n_in : n_in + n_out], out_groups), *refs[n_in + n_out :]
        )

    size = sum(math.prod(a.shape) * a.dtype.itemsize for a in arrays)
    size += sum(math.prod(s) * jnp.dtype(t).itemsize for s, t, _ in flat)
    got = pl.pallas_call(
        run,
        grid=(steps,),
        in_specs=in_specs,
        out_specs=tuple(full(s) if b is None else b for s, _, b in flat),
        out_shape=tuple(jax.ShapeDtypeStruct(s, t) for s, t, _ in flat),
        scratch_shapes=list(scratch),
        compiler_params=pltpu.CompilerParams(vmem_limit_bytes=limit * 2**20),
        cost_estimate=pl.CostEstimate(flops=int(flops), bytes_accessed=size, transcendentals=0),
        name=name,
    )(*arrays)
    return grouped(got, out_groups)


def step_signal(step_ids, feat_width):
    half_width = feat_width // 2
    frequency = jnp.exp(-math.log(10000.0) * jnp.arange(half_width, dtype=F32) / half_width)
    angles = step_ids.astype(F32)[:, None] * frequency[None, :]
    return jnp.concatenate([jnp.sin(angles), jnp.cos(angles)], axis=1)


def sds(shape, dtype=BF, block=None):
    return (tuple(shape), dtype, block)


def per_device(
    decoder_input, timesteps, memory, cotangent, time_weight, attn_query, attn_key, attn_value, attn_out,
    cross_query, cross_key, cross_value, cross_out, ffn_in, ffn_out, norm_gains,
):
    dp = lax.axis_size("dp")
    mem_count = lax.axis_size("mem")
    rows = D // dp
    cols = D // mem_count
    by_hand = dp == 8 and mem_count == 4
    x = decoder_input[0]
    cot = cotangent[0]
    n = x.shape[0]
    r = memory.shape[0] * memory.shape[1]
    gains = norm_gains.T
    my_dp, my_mem = lax.axis_index("dp"), lax.axis_index("mem")
    me = jnp.stack([my_dp, my_mem]).astype(jnp.int32)

    def to(value, axis, bit):
        size = lax.axis_size(axis)
        return lax.ppermute(value, axis, [(i, i ^ bit) for i in range(size)])

    def after(value, *others):
        return lax.optimization_barrier((value,) + others)[0]

    def plane(own):
        return [own] + [to(own, "dp", 2 * bit) for bit in (1, 2, 3)]

    def swap(parts):
        both = []
        for part in parts:
            both += [part, to(part, "dp", 1)]
        return both

    in_parts = [ffn_in[:, D * c : D * (c + 1)] for c in range(CHUNKS)]
    if by_hand:
        first = (time_weight, attn_query, attn_key, attn_value)
        second = (attn_out, cross_query, cross_key, cross_value, cross_out)
        (own1,) = call(pack, "pack_one", (me,) + first, [sds((4, rows, D))], limit=4)
        plane1 = plane(own1)
        mem_parts = call(take, "take_memory", (me, memory), [sds(memory.shape[1:])] * mem_count, limit=8)
        mem_rows = [mem_parts[0]] + [to(mem_parts[b], "mem", b) for b in range(1, mem_count)]
        (own2,) = call(pack, "pack_two", (me,) + second, [sds((5, rows, D))], limit=4)
        (own3,) = call(pack, "pack_three", (me, ffn_in, ffn_out), [sds((2 * CHUNKS, rows, D))], limit=8)
        g1 = swap(plane1)
        own2 = after(own2, *plane1)
        own3 = after(own3, *plane1)
        g2 = swap(plane(own2))
        g3 = lax.all_gather(own3, "dp", axis=0, tiled=False)
    else:

        def gather(parts):
            got = lax.all_gather(jnp.stack(parts, 0), "dp", axis=0, tiled=False)
            return got.transpose(1, 0, 2, 3).reshape(1, len(parts), D, D)

        g1 = [gather((time_weight, attn_query, attn_key, attn_value))]
        g2 = [gather((attn_out, cross_query, cross_key, cross_value, cross_out))]
        whole_out = lax.all_gather(ffn_out, "dp", axis=0, tiled=True).reshape(1, CHUNKS, D, D)
        g3 = jnp.concatenate([gather(in_parts), whole_out], axis=1)
        mem_rows = [lax.all_to_all(memory, "mem", split_axis=0, concat_axis=1, tiled=True)[0]]
    signal = step_signal(timesteps, D).astype(BF)
    sig = jnp.broadcast_to(signal, (8, D))

    nat = pl.BlockSpec((n, PAIR), lambda i: (0, i))
    nat_r = pl.BlockSpec((r, PAIR), lambda i: (0, i))
    rows2 = pl.BlockSpec((1, 2, n), lambda i: (i, 0, 0))
    wide = lambda m: pltpu.VMEM((PAIRS, m, PAIR), BF)
    tall = lambda m: pltpu.VMEM((PAIRS, PAIR, m), BF)
    weight = pltpu.VMEM((D, D), BF)
    weights = lambda count: pltpu.VMEM((count, D, D), BF)
    proj = 2 * n * D * D * 1.5
    att_cost = 2 * n * r * D * 5
    lse_out = sds((PAIRS, 2, n), F32, rows2)
    emb, n1, q, k, v, lse1, attended = call(
        self_forward, "self_forward", (me, x, sig, gains, g1),
        [sds((1, D), F32)] + [sds((n, D), BF, nat)] * 4 + [lse_out, sds((n, D), BF, nat)],
        [weights(4), wide(n), wide(n), wide(n), wide(n), tall(n), tall(n), tall(n)],
        PAIRS, 3 * proj + 2 * att_cost, 40,
    )
    mid, n2, cq, ck, cv, lse2, crossed = call(
        cross_forward, "cross_forward", (me, x, emb, attended, mem_rows, gains, g2),
        [sds((n, D), F32, nat)] + [sds((n, D), BF, nat)] * 2 + [sds((r, D), BF, nat_r)] * 2
        + [lse_out, sds((n, D), BF, nat)],
        [weights(4), pltpu.VMEM((PAIRS, n, PAIR), F32), wide(n), wide(n), wide(r), wide(r), tall(n), tall(r), tall(n)],
        PAIRS, 4 * proj + 2 * att_cost, 44,
    )
    if by_hand:
        cross_out_parts = [(p, pl.BlockSpec((1, rows, D), lambda i: (4, 0, 0))) for p in g2]
        fin = (g3, pl.BlockSpec((dp, 1, rows, D), lambda i: (0, i, 0, 0)))
        fout = (g3, pl.BlockSpec((dp // CHUNKS, CHUNKS, rows, D), lambda i: (i, 1, 0, 0)))
        raw_of = lambda count: [sds((dp // 2, mem_count, count * rows, cols))] * 2
        raw3_of = sds((dp, mem_count, 2 * CHUNKS * rows, cols))
    else:
        cross_out_parts = [(g2[0], pl.BlockSpec((1, 1, D, D), lambda i: (0, 4, 0, 0)))]
        fin = (g3, pl.BlockSpec((1, 1, D, D), lambda i: (0, i, 0, 0)))
        fout = (g3, pl.BlockSpec((1, 1, D, D), lambda i: (0, CHUNKS + i, 0, 0)))
        raw_of = lambda count: [sds((count, D, D))]
        raw3_of = sds((2 * CHUNKS, D, D))
    out, gl, bt, gain3, raw3 = call(
        feed_forward, "feed_forward", (me, mid, crossed, cot, gains, cross_out_parts, fin, fout),
        [sds((n, D)), sds((n, D), F32), sds((n, D)), sds((1, D), F32), raw3_of],
        [weights(1), weight, weight, pltpu.VMEM((n, D), BF), pltpu.VMEM((D, n), BF)] + [pltpu.VMEM((n, D), F32)] * 3,
        CHUNKS, 25 * proj, 48,
    )
    back_scratch = lambda m: [
        weights(5), wide(n), tall(n), wide(m), tall(m), wide(m), wide(n), tall(n),
        pltpu.VMEM((PAIRS, 2, n), F32), tall(n), wide(m), wide(m),
    ]
    raw2, mem_grad, gm, b1, gain2 = call(
        cross_back, "cross_back",
        (me, bt, gl, crossed, cq, ck, cv, (lse2, rows2), mem_rows, n2, mid, gains, g2, attended),
        [raw_of(5), [sds(m.shape) for m in mem_rows], sds((n, D), F32), sds((n, D)), sds((1, D), F32)],
        back_scratch(r), PAIRS, 9 * proj + 5 * att_cost, 56,
    )
    raw1, gn = call(
        self_back, "self_back", (me, b1, attended, q, k, v, (lse1, rows2), n1, g1, g2),
        [raw_of(3), sds((n, D), F32)],
        back_scratch(n), PAIRS, 7 * proj + 5 * att_cost, 48,
    )
    input_grad, sums = call(
        finish_back, "finish_back", (me, x, emb, gm, gn, gains, sig, gain2, gain3),
        [sds((n, D)), sds((8, D), F32)], flops=1000 * n * D, limit=24,
    )

    limit = math.sqrt(9 * D * D + 2 * D * FF + 3 * D)
    if not by_hand:
        memory_grad = lax.all_to_all(mem_grad[0][None], "mem", split_axis=1, concat_axis=0, tiled=True)

        def scatter(raw):
            part = lax.psum_scatter(raw, "dp", scatter_dimension=1, tiled=True)
            part = lax.psum_scatter(part, "mem", scatter_dimension=2, tiled=True)
            return [part[t].astype(F32) for t in range(raw.shape[0])]

        d_in = scatter(raw3[:CHUNKS].transpose(1, 0, 2).reshape(1, D, FF))[0]
        d_fout = scatter(raw3[CHUNKS:].reshape(1, FF, D))[0]
        d_query, d_key, d_value = scatter(raw1[0])
        d_cout, d_cquery, d_ckey, d_cvalue, d_out = scatter(raw2[0])
        everyone = lax.all_gather(sums, ("dp", "mem"), axis=0, tiled=False)
        my_signal = lax.dynamic_slice_in_dim(everyone[:, 4], my_dp * rows, rows, axis=1)
        my_sums = lax.dynamic_slice_in_dim(everyone[:, 0], my_mem * cols, cols, axis=1)
        d_time = jnp.dot(my_signal.T, my_sums, precision=lax.Precision.HIGHEST)
        all_gains = jnp.sum(everyone[:, 1:4], axis=0)
        d_gains = lax.dynamic_slice_in_dim(all_gains, my_dp * rows, rows, axis=1).T
        weights = [d_time, d_query, d_key, d_value, d_out, d_cquery, d_ckey, d_cvalue, d_cout, d_in, d_fout]
        local = sum(jnp.sum(w * w) for w in weights)
        squares = lax.psum(local, ("dp", "mem")) + jnp.sum(all_gains * all_gains)
        factor = jnp.minimum(1.0, limit * lax.rsqrt(squares))
        return (
            (out[None], input_grad[None], memory_grad) + tuple(w * factor for w in weights) + (d_gains * factor,)
        )

    done3 = lax.psum_scatter(raw3, "dp", scatter_dimension=0, tiled=False)
    done3 = lax.psum_scatter(done3, "mem", scatter_dimension=0, tiled=False)
    back = [mem_grad[0]] + [to(mem_grad[b], "mem", b) for b in range(1, mem_count)]

    def reduce(raw, name):
        keep, send = raw
        size = keep.shape[2]
        parts = call(
            add_core, name + "_core", (me, keep, to(send, "dp", 1)), [sds((mem_count, size, cols))] * 4, limit=16
        )
        parts = [parts[0]] + [to(parts[b], "dp", 2 * b) for b in (1, 2, 3)]
        parts = call(add_plane, name + "_plane", [me] + parts, [sds((size, cols))] * mem_count, limit=16)
        parts = [parts[0]] + [to(parts[b], "mem", b) for b in (1, 2, 3)]
        return call(add_all, name + "_all", [me] + parts, [sds((size, cols), F32), sds((8, cols), F32)], limit=16)

    done2, squares2 = reduce(raw2, "cross")
    done1, squares1 = reduce(raw1, "attn")
    two = jnp.stack([sums, to(sums, "dp", 1)])
    eight = jnp.stack([two] + [to(two, "dp", 2 * b) for b in (1, 2, 3)])
    everyone = [eight] + [to(eight, "mem", b) for b in (1, 2, 3)]
    d_time, d_gains, squares0 = call(
        time_grad, "time_grad", [me] + everyone,
        [sds((rows, cols), F32), sds((rows, 128), F32), sds((8, cols), F32)],
        [pltpu.VMEM((D, D), F32), pltpu.VMEM((D, 128), F32)], limit=16,
    )
    wide3 = done3.astype(F32)
    squares3 = jnp.sum((wide3 * wide3).reshape(-1, 8, cols), axis=0)
    local = squares0 + squares1 + squares2 + squares3
    local = local + to(local, "dp", 1)
    local = local + to(local, "dp", 2) + to(local, "dp", 4) + to(local, "dp", 6)
    planes = [local] + [to(local, "mem", b) for b in (1, 2, 3)]
    (memory_grad,) = call(place_rows, "place_rows", [me] + back, [sds(memory.shape)], limit=8)
    shapes = [(rows, cols)] * 9 + [(rows, FF // mem_count), (FF // dp, cols), (rows, 3)]
    scaled = call(
        scale_all, "scale_all", [me] + planes + [d_time, d_gains, done1, done2, done3],
        [sds(s, F32) for s in shapes], limit=16,
    )
    return (out[None], input_grad[None], memory_grad) + tuple(scaled)


def solution(mesh):
    tokens = P(("dp", "mem"), None, None)
    weight = P("dp", None)
    in_specs = (tokens, P(("dp", "mem")), P("dp", "mem", None), tokens) + (weight,) * 11 + (P(),)
    out_specs = (tokens, tokens, P("dp", "mem", None)) + (P("dp", "mem"),) * 11 + (P("dp", None),)
    return jax.shard_map(per_device, mesh=mesh, in_specs=in_specs, out_specs=out_specs, check_vma=False)
```

```python
import functools
import math

import jax
import jax.numpy as jnp
from jax import lax
from jax.experimental import pallas as pl
from jax.experimental.pallas import tpu as pltpu
from jax.sharding import PartitionSpec as P

D = 512
HEADS = 8
HEAD = 64
FF = 2048
PAIRS = HEADS // 2
PAIR = 2 * HEAD
CHUNKS = FF // D
BF = jnp.bfloat16
F32 = jnp.float32
SCALE = 1.0 / math.sqrt(HEAD)
ROOT_HALF = math.sqrt(0.5)
BELL = 1.0 / math.sqrt(2.0 * math.pi)


def dot(a, b, ca=1, cb=0):
    return lax.dot_general(a, b, (((ca,), (cb,)), ((), ())), preferred_element_type=F32)


def row_mean(v):
    return jnp.sum(v, axis=-1, keepdims=True) * (1.0 / v.shape[-1])


def norm_parts(v):
    centred = v - row_mean(v)
    scale = lax.rsqrt(row_mean(centred * centred) + 1e-05)
    return centred * scale, scale


def norm_back(v, gain, grad):
    normed, scale = norm_parts(v)
    c = grad * gain
    gain_part = jnp.sum(grad * normed, axis=0, keepdims=True)
    return scale * (c - row_mean(c) - normed * row_mean(c * normed)), gain_part


def build(w, slot, parts, which, me):
    dst = w.at[slot]
    if len(parts) == 1:
        blocks, _, rows, _ = parts[0].shape
        for b in range(blocks):
            dst[rows * b : rows * (b + 1), :] = parts[0][b, which]
        return
    rows = parts[0].shape[1]
    for r, part in enumerate(parts):
        lo = pl.multiple_of((r ^ me) * rows, rows)
        dst[pl.ds(lo, rows), :] = part[which]


def put(refs, at, mat, core):
    mat = mat.astype(refs[0].dtype)
    if len(refs) == 1:
        refs[0][at] = mat
        return
    half, cb, _, cols = refs[0].shape
    rows = D // (2 * half)

    def cut(own, other):
        for a in range(2 * half):
            ref = own if a % 2 == 0 else other
            for j in range(cb):
                ref[a // 2, j, rows * at : rows * (at + 1), :] = mat[
                    rows * a : rows * (a + 1), cols * j : cols * (j + 1)
                ]

    @pl.when(core == 0)
    def _():
        cut(refs[0], refs[1])

    @pl.when(core == 1)
    def _():
        cut(refs[1], refs[0])


ROWS = 256


def each_block(total, step, body):
    def run(b, carry):
        body(pl.ds(pl.multiple_of(b * step, step), step))
        return carry

    lax.fori_loop(0, total // step, run, 0)


def attend(i, qT, k, vT, oT, lse):
    n = qT.shape[2]
    row = lax.broadcasted_iota(jnp.int32, (PAIR, n), 0)
    zero = jnp.zeros((), BF)

    scores = [dot(k[i], jnp.where((row // HEAD) == h, qT[i], zero)) for h in range(2)]
    for h in range(2):
        own = slice(HEAD * h, HEAD * (h + 1))
        top = jnp.max(scores[h], axis=0, keepdims=True)
        e = jnp.exp(scores[h] - top)
        total = jnp.sum(e, axis=0, keepdims=True)
        out = dot(vT[i, own, :], e.astype(BF))
        oT[i, own, :] = (out * (1.0 / total)).astype(BF)
        lse[0, h : h + 1, :] = top + jnp.log(total)


def attend_back(i, q, qT, k, kT, v, g, gT, lse, delta, dqT, dk, dv):
    n = qT.shape[2]
    block = min(n, 512)
    row = lax.broadcasted_iota(jnp.int32, (PAIR, block), 0)
    lane = lax.broadcasted_iota(jnp.int32, (block, PAIR), 1)
    zero = jnp.zeros((), BF)
    total_k = total_v = None
    for t in range(2 * (n // block)):
        h = t % 2
        at = slice((t // 2) * block, (t // 2 + 1) * block)
        own = slice(HEAD * h, HEAD * (h + 1))
        s = dot(k[i], jnp.where((row // HEAD) == h, qT[i, :, at], zero))
        dp = dot(v[i], jnp.where((row // HEAD) == h, gT[i, :, at], zero))
        p = jnp.exp(s - lse[0, h : h + 1, at])
        ds = (p * (dp - delta[i, h : h + 1, at])).astype(BF)
        one_v = dot(p.astype(BF), jnp.where((lane // HEAD) == h, g[i, at, :], zero))
        one_k = dot(ds, jnp.where((lane // HEAD) == h, q[i, at, :], zero))
        dqT[i, own, at] = (dot(kT[i, own, :], ds) * SCALE).astype(BF)
        total_v = one_v if total_v is None else total_v + one_v
        total_k = one_k if total_k is None else total_k + one_k
    dk[i] = (total_k * SCALE).astype(BF)
    dv[i] = total_v.astype(BF)


def pairs_at(dst, rows, src):
    for p in range(PAIRS):
        dst[p, rows, :] = src[:, PAIR * p : PAIR * (p + 1)]


def pairs_at_T(dst, rows, src, scale=None):
    for p in range(PAIRS):
        t = src[:, PAIR * p : PAIR * (p + 1)].T
        dst[p, :, rows] = t if scale is None else t * jnp.asarray(scale, BF)


def joined(src, rows):
    return jnp.concatenate([src[p, rows, :] for p in range(PAIRS)], axis=1)


def joined_T(src, rows):
    return jnp.concatenate([src[p, :, rows].T for p in range(PAIRS)], axis=1)


def pairs_in(dst, src):
    for p in range(PAIRS):
        dst[p] = src[:, PAIR * p : PAIR * (p + 1)]


def pairs_in_T(dst, src, scale=None):
    for p in range(PAIRS):
        t = src[:, PAIR * p : PAIR * (p + 1)].T
        dst[p] = t if scale is None else t * jnp.asarray(scale, BF)


def from_pairs(src):
    return jnp.concatenate([src[p] for p in range(PAIRS)], axis=1)


def from_pairs_T(src):
    return jnp.concatenate([src[p].T for p in range(PAIRS)], axis=1)


def rows_of(mem):
    parts = [m[t] for m in mem for t in range(m.shape[0])]
    return jnp.concatenate(parts, axis=0) if len(parts) > 1 else parts[0]


def start_back_all(branch, weight, joined, g, gT, delta):
    grad = dot(branch, weight, 1, 1).astype(BF)
    pairs_in(g, grad)
    for p in range(PAIRS):
        gT[p] = g[p].T
        other = joined[:, PAIR * p : PAIR * (p + 1)].T
        both = gT[p].astype(F32) * other.astype(F32)
        for h in range(2):
            delta[p, h : h + 1, :] = jnp.sum(both[HEAD * h : HEAD * (h + 1), :], axis=0, keepdims=True)


def hold_rows(dst, mem):
    at = 0
    for m in mem:
        for t in range(m.shape[0]):
            dst[at : at + m.shape[1], :] = m[t]
            at += m.shape[1]


def self_forward(me, x, sig, gains, g1, emb, n1, q, k, v, lse, att, w, n1s, qs, ks, vs, qT, vT, oT):
    i = pl.program_id(0)

    @pl.when(i == 0)
    def _():
        build(w, 0, g1, 0, me[0])
        embedded = dot(sig[...], w[0])[0:1, :]
        emb[...] = embedded
        resid = x[...].astype(F32) + embedded
        normed = (norm_parts(resid)[0] * gains[0:1, :]).astype(BF)
        pairs_in(n1s, normed)
        for t, dst in ((1, qs), (2, ks), (3, vs)):
            build(w, t, g1, t, me[0])
            pairs_in(dst, dot(normed, w[t]).astype(BF))
        for p in range(PAIRS):
            qT[p] = qs[p].T * jnp.asarray(SCALE, BF)
            vT[p] = vs[p].T

    attend(i, qT, ks, vT, oT, lse)
    n1[...] = n1s[i]
    q[...] = qs[i]
    k[...] = ks[i]
    v[...] = vs[i]
    att[...] = oT[i].T


def cross_forward(
    me, x, emb, att, mem, gains, g2, mid, n2, cq, k, v, lse, crossed, w, mids, n2s, qs, ks, vs, qT, vT, oT
):
    i = pl.program_id(0)

    @pl.when(i == 0)
    def _():
        build(w, 0, g2, 0, me[0])
        new = x[...].astype(F32) + emb[...] + dot(att[...], w[0])
        pairs_in(mids, new)
        normed = (norm_parts(new)[0] * gains[1:2, :]).astype(BF)
        pairs_in(n2s, normed)
        build(w, 1, g2, 1, me[0])
        pairs_in(qs, dot(normed, w[1]).astype(BF))
        rows = rows_of(mem)
        for t, dst in ((2, ks), (3, vs)):
            build(w, t, g2, t, me[0])
            pairs_in(dst, dot(rows, w[t]).astype(BF))
        for p in range(PAIRS):
            qT[p] = qs[p].T * jnp.asarray(SCALE, BF)
            vT[p] = vs[p].T

    attend(i, qT, ks, vT, oT, lse)
    mid[...] = mids[i]
    n2[...] = n2s[i]
    cq[...] = qs[i]
    k[...] = ks[i]
    v[...] = vs[i]
    crossed[...] = oT[i].T


def feed_forward(
    me, mid, crossed, cot, gains, g2, g3,
    out, gl, bt, gain3, raw_out_ref,
    wlate, win, wout, n3, n3T, late, acc, gacc, active, grad_inner, raw, sems,
):
    i = pl.program_id(0)
    blocks, _, rows, _ = g3.shape
    n = mid.shape[0]
    each = max(blocks // CHUNKS, 1)
    now, before = i % 2, (i + 1) % 2
    piece = D // (n // ROWS)

    @pl.when(i == 0)
    def _():
        build(wlate, 0, g2, 0, me[0])

        def enter(at):
            new = mid[at, :] + dot(crossed[at, :], wlate[0])
            late[at, :] = new
            normed = (norm_parts(new)[0] * gains[2:3, :]).astype(BF)
            n3[at, :] = normed
            n3T[:, at] = normed.T
            acc[at, :] = new
            gacc[at, :] = jnp.zeros((ROWS, D), F32)

        each_block(n, ROWS, enter)

    @pl.when(i < CHUNKS)
    def _():
        for b in range(blocks):
            win[rows * b : rows * (b + 1), :] = g3[b, i]
        if blocks == 1:
            wout[...] = g3[0, CHUNKS + i]
        else:
            for u in range(each):
                for t in range(CHUNKS):
                    lo = rows * (CHUNKS * u + t)
                    wout[lo : lo + rows, :] = g3[each * i + u, CHUNKS + t]

    def hidden(at):
        inner = dot(n3[at, :], win[...])
        grad_active = dot(cot[at, :], wout[...], 1, 1)
        share = 0.5 * (1.0 + lax.erf(inner * ROOT_HALF))
        act = (inner * share).astype(BF)
        active[now, at, :] = act
        acc[at, :] += dot(act, wout[...])
        slope = share + inner * (jnp.exp(-0.5 * inner * inner) * BELL)
        grad = (slope * grad_active).astype(BF)
        grad_inner[now, at, :] = grad
        gacc[at, :] += dot(grad, win[...], 1, 1)

    def weights(b):
        c = i - 1
        at = pl.ds(pl.multiple_of(b * piece, piece), piece)
        raw_in = dot(n3T[at, :], grad_inner[before]).astype(BF)
        raw_out = dot(active[before, :, at], cot[...], 0, 0).astype(BF)
        if blocks == 1:
            raw[c, at, :] = raw_in
            raw[CHUNKS + c, at, :] = raw_out
            return
        cols = D // CHUNKS
        for a in range(piece // rows):
            for t in range(CHUNKS):
                raw[(piece // rows) * b + a, c, rows * t : rows * (t + 1), :] = raw_in[
                    rows * a : rows * (a + 1), cols * t : cols * (t + 1)
                ]
        tall = D // each
        split = tall // piece
        lo = tall + (b % split) * piece
        for j in range(CHUNKS):
            raw[each * c + b // split, j, pl.ds(pl.multiple_of(lo, piece), piece), :] = raw_out[
                :, cols * j : cols * (j + 1)
            ]

    @pl.when(i == 0)
    def _():
        each_block(n, ROWS, hidden)

    @pl.when((i > 0) & (i < CHUNKS))
    def _():
        def both(b, carry):
            weights(b)
            hidden(pl.ds(pl.multiple_of(b * ROWS, ROWS), ROWS))
            return carry

        lax.fori_loop(0, n // ROWS, both, 0)

    @pl.when(i == CHUNKS)
    def _():
        def only(b, carry):
            weights(b)
            return carry

        lax.fori_loop(0, n // ROWS, only, 0)

    def copies(c):
        if blocks == 1:
            return [
                pltpu.make_async_copy(raw.at[at], raw_out_ref.at[at], sems.at[c, k])
                for k, at in enumerate((c, CHUNKS + c))
            ]
        tall = D // each
        first = (slice(None), c, pl.ds(0, tall))
        second = (pl.ds(each * c, each), slice(None), pl.ds(tall, tall))
        return [
            pltpu.make_async_copy(raw.at[at], raw_out_ref.at[at], sems.at[c, k])
            for k, at in enumerate((first, second))
        ]

    @pl.when(i > 0)
    def _():
        for copy in copies(i - 1):
            copy.start()

    @pl.when(i == CHUNKS)
    def _():
        gain3[...] = jnp.zeros_like(gain3)

        def leave(at):
            out[at, :] = acc[at, :].astype(BF)
            part, gain_part = norm_back(late[at, :], gains[2:3, :], gacc[at, :])
            gain3[...] += gain_part
            total = cot[at, :].astype(F32) + part
            gl[at, :] = total
            bt[at, :] = total.astype(BF)

        each_block(n, ROWS, leave)
        for c in range(CHUNKS):
            for copy in copies(c):
                copy.wait()


def start_back(branch, weight, heads, g, gT, delta):
    def enter(rows):
        grad = dot(branch[rows, :], weight[...], 1, 1).astype(BF)
        pairs_at(g, rows, grad)
        for p in range(PAIRS):
            at = slice(PAIR * p, PAIR * (p + 1))
            turned = grad[:, at].T
            gT[p, :, rows] = turned
            both = turned.astype(F32) * heads[rows, at].T.astype(F32)
            for h in range(2):
                delta[p, h : h + 1, rows] = jnp.sum(both[HEAD * h : HEAD * (h + 1), :], axis=0, keepdims=True)

    each_block(branch.shape[0], ROWS, enter)


def hold_heads(src, dst, dstT, scale=None):
    def enter(rows):
        pairs_at(dst, rows, src[rows, :])
        if dstT is not None:
            pairs_at_T(dstT, rows, src[rows, :], scale)

    each_block(src.shape[0], ROWS, enter)


def put_product(refs, at, left, right, core, whole):
    def run(b, carry):
        rows = pl.ds(pl.multiple_of(b * ROWS, ROWS), ROWS)
        whole[rows, :] = dot(left[:, rows], right[...], 0, 0).astype(BF)
        return carry

    lax.fori_loop(0, D // ROWS, run, 0)
    put(refs, at, whole[...], core)


def cross_back(
    me, bt, gl, crossed, cq, k, v, lse, mem, n2, mid, gains, g2, att,
    raw, gm, b1, gain2, gk, gv,
    w, q, qT, ks, kT, vs, g, gT, delta, dqT, dk, dv, whole, held, grads,
):
    i = pl.program_id(0)
    core = me[0] % 2

    @pl.when(i == 0)
    def _():
        build(w, 0, g2, 4, me[0])
        build(w, 1, g2, 1, me[0])
        start_back(bt, w.at[0], crossed, g, gT, delta)
        put_product(raw, 0, crossed, bt, core, whole.at[0])
        hold_heads(cq, q, qT, SCALE)
        hold_heads(k, ks, kT)
        hold_heads(v, vs, None)
        hold_rows(held, mem)

    attend_back(i, q, qT, ks, kT, vs, g, gT, lse, delta, dqT, dk, dv)
    gk[...] = dk[i]
    gv[...] = dv[i]

    @pl.when(i == PAIRS - 1)
    def _():
        gain2[...] = jnp.zeros_like(gain2)

        def leave(rows):
            grad_q = joined_T(dqT, rows)
            grads[0, rows, :] = grad_q
            part, gain_part = norm_back(mid[rows, :], gains[1:2, :], dot(grad_q, w[1], 1, 1))
            gain2[...] += gain_part
            total = gl[rows, :] + part
            gm[rows, :] = total
            b1[rows, :] = total.astype(BF)

        each_block(bt.shape[0], ROWS, leave)

        def gather(rows):
            grads[1, rows, :] = joined(dk, rows)
            grads[2, rows, :] = joined(dv, rows)

        each_block(held.shape[0], ROWS, gather)
        put_product(raw, 1, n2, grads.at[0], core, whole.at[1])
        put_product(raw, 2, held, grads.at[1], core, whole.at[2])
        put_product(raw, 3, held, grads.at[2], core, whole.at[3])
        put_product(raw, 4, att, b1, core, whole.at[4])


def memory_back(me, gk, gv, g2, outs, w):
    build(w, 0, g2[0], 0, me[0])
    build(w, 1, g2[1], 0, me[0])
    back = (dot(gk[...], w[0], 1, 1) + dot(gv[...], w[1], 1, 1)).astype(BF)
    if len(outs) == 1:
        outs[0][...] = back
        return
    size = back.shape[0] // 4
    parts = [back[size * t : size * (t + 1)] for t in range(4)]
    outs[0][...], outs[1][...] = parts[0], parts[1]
    outs[2][0], outs[2][1] = parts[2], parts[3]


def self_back(
    me, b1, att, qn, k, v, lse, n1, g1, g2,
    raw, gn,
    w, q, qT, ks, kT, vs, g, gT, delta, dqT, dk, dv,
):
    i = pl.program_id(0)
    core = me[0] % 2

    @pl.when(i == 0)
    def _():
        build(w, 0, g2, 0, me[0])
        start_back_all(b1[...], w[0], att, g, gT, delta)
        pairs_in(q, qn)
        pairs_in_T(qT, qn, SCALE)
        pairs_in(ks, k)
        pairs_in_T(kT, k)
        pairs_in(vs, v)

    attend_back(i, q, qT, ks, kT, vs, g, gT, lse, delta, dqT, dk, dv)

    @pl.when(i == PAIRS - 1)
    def _():
        nT = n1[...].T
        grads = (from_pairs_T(dqT), from_pairs(dk), from_pairs(dv))
        for t in range(3):
            put(raw, t, dot(nT, grads[t]), core)
        total = None
        for t in range(3):
            build(w, t + 1, g1, t + 1, me[0])
            one = dot(grads[t], w[t + 1], 1, 1)
            total = one if total is None else total + one
        gn[...] = total


SMALL = 32


def finish_back(me, x, emb, gm, gn, gains, sig, gain2, gain3, grad, outs, sums):
    i = pl.program_id(0)
    part, gain_part = norm_back(x[...].astype(F32) + emb[...], gains[0:1, :], gn[...])
    total = gm[...] + part
    grad[...] = total.astype(BF)
    both = jnp.concatenate([jnp.sum(total, axis=0, keepdims=True), gain_part], axis=0)

    @pl.when(i == 0)
    def _():
        sums[...] = both

    @pl.when(i > 0)
    def _():
        sums[...] += both

    @pl.when(i == pl.num_programs(0) - 1)
    def _():
        rows = [sums[0:1, :], sig[0:1, :].astype(F32), sums[1:2, :], gain2[...], gain3[...]]
        if outs.shape[1] == D:
            for t, row in enumerate(rows):
                outs[t : t + 1, :] = row
            outs[5:8, :] = jnp.zeros((3, D), F32)
            return
        tile = jnp.concatenate([row[:, 128 * c : 128 * (c + 1)] for row in rows for c in range(D // 128)], axis=0)
        outs[...] = jnp.concatenate([tile, jnp.zeros((SMALL - tile.shape[0], 128), F32)], axis=0).astype(BF)


def pack(me, *refs):
    out = refs[-1]
    rows = out.shape[1]
    at = 0
    for ref in refs[:-1]:
        for c in range(ref.shape[1] // D):
            for r in range(ref.shape[0] // rows):
                out[at] = ref[rows * r : rows * (r + 1), D * c : D * (c + 1)]
                at += 1


def add_core(me, keep, got, outs):
    place = me[0] // 2
    for r, out in enumerate(outs):
        out[...] = keep[r ^ place] + got[r ^ place]


def add_core_small(me, keep, got, mine, other, *outs):
    place = me[0] // 2
    cb, size, cols = keep.shape[1:]
    a, b = mine[...].astype(F32), other[...].astype(F32)
    small = jnp.concatenate([a[0:4], b[0:4], a[4:8], b[4:8], a[8:20] + b[8:20], a[28:32]], axis=0).astype(BF)
    for r, out in enumerate(outs):
        out[0 : cb * size, :] = (keep[r ^ place] + got[r ^ place]).reshape(cb * size, cols)
        out[cb * size :, :] = small


def add_plane(me, parts, *outs):
    size = outs[0].shape[0] - SMALL
    cb = (parts[0].shape[0] - SMALL) // size
    small = [p[cb * size :, :].astype(F32) for p in parts]
    gains = small[0][16:28] + small[1][16:28] + small[2][16:28] + small[3][16:28]
    line = lax.broadcasted_iota(jnp.int32, (4, 128), 0)

    def pick(rows, which):
        return jnp.sum(jnp.where(line == which, rows, 0.0), axis=0, keepdims=True)

    signals = []
    for p in small:
        for core in range(2):
            row = pick(p[8 + 4 * core : 12 + 4 * core], me[0] // 2)
            turned = jnp.concatenate([row[:, 64:], row[:, :64]], axis=1)
            signals.append(jnp.where(me[0] % 2 == 1, turned, row))
    for r, out in enumerate(outs):
        at = r ^ me[1]
        spot = pl.ds(pl.multiple_of(at * size, size), size)
        total = sum(p[spot, :].astype(F32) for p in parts)
        out[0:size, :] = total.astype(BF)
        sums = [pick(p[4 * core : 4 * (core + 1)], at) for p in small for core in range(2)]
        rows = jnp.concatenate(sums + signals + [gains, jnp.zeros((4, 128), F32)], axis=0)
        out[size:, :] = rows.astype(BF)


def add_four(me, parts, keep, send):
    for r in range(4):
        at = r ^ me[1]
        total = sum(p[at].astype(F32) for p in parts).astype(BF)
        if r < 2:
            keep[r] = total
        else:
            send[r - 2] = total


def add_pair(me, keep, got, own, send):
    own[...] = keep[0] + got[0]
    send[...] = keep[1] + got[1]


def fold(v):
    return jnp.sum((v * v).reshape(-1, 8, v.shape[-1]), axis=0)


def add_all(me, attn, cross, feed, done1, done2, d_time, d_gains, squares):
    size = done1.shape[0]
    total1 = sum(p[0:size, :].astype(F32) for p in attn)
    done1[...] = total1
    total2 = sum(p[...].astype(F32) for p in cross)
    done2[...] = total2
    small = [p[size:, :].astype(F32) for p in attn]
    sums = jnp.concatenate([p[0:8] for p in small], axis=0).astype(BF)
    signals = jnp.concatenate([p[8:16] for p in small], axis=0).astype(BF)
    rows = d_time.shape[0]
    of_time = dot(signals, sums, 0, 0)[0:rows, :]
    d_time[...] = of_time
    gains = small[0][16:28] + small[1][16:28] + small[2][16:28] + small[3][16:28]
    line = lax.broadcasted_iota(jnp.int32, (4, 128), 0)
    lane = lax.broadcasted_iota(jnp.int32, (1, 128), 1)
    mine = []
    for t in range(3):
        row = jnp.sum(jnp.where(line == me[0] // 2, gains[4 * t : 4 * (t + 1)], 0.0), axis=0, keepdims=True)
        row = jnp.where(me[0] % 2 == 1, jnp.concatenate([row[:, 64:], row[:, :64]], axis=1), row)
        mine.append(jnp.where(lane < 64, row, 0.0))
    block = jnp.concatenate(mine + [jnp.zeros((125, 128), F32)], axis=0)
    d_gains[...] = block.T[0:rows, :]
    wide = feed[...].astype(F32)
    squares[...] = fold(total1) + fold(total2) + fold(wide) + fold(of_time) + fold(block) * 0.25


def take(me, src, keep, send):
    for t in range(2):
        keep[t] = src[(2 * t) ^ me[1]]
        send[t] = src[(2 * t + 1) ^ me[1]]


def join(me, first, second, out):
    out[0] = first[...] if len(first.shape) == 2 else first[1]
    out[1] = second[1]


def place_rows(me, own, across, near, out):
    out[me[1]] = own[...]
    out[2 ^ me[1]] = across[0]
    out[1 ^ me[1]] = near[0]
    out[3 ^ me[1]] = near[1]


def scale_all(me, s0, s1, s2, s3, d_time, d_gains, a1, a2, a3, *outs):
    squares = jnp.sum(s0[...] + s1[...] + s2[...] + s3[...])
    limit = math.sqrt(9 * D * D + 2 * D * FF + 3 * D)
    factor = jnp.minimum(1.0, limit * lax.rsqrt(jnp.full((8, 128), squares, F32)))[0:1, :]
    o_time, o_q, o_k, o_v, o_out, o_cq, o_ck, o_cv, o_cout, o_in, o_fout, o_gains = outs
    o_time[...] = d_time[...] * factor
    rows = d_time.shape[0]
    for src, dsts in ((a1, (o_q, o_k, o_v)), (a2, (o_cout, o_cq, o_ck, o_cv, o_out))):
        for t, dst in enumerate(dsts):
            dst[...] = src[rows * t : rows * (t + 1), :] * factor
    for t in range(CHUNKS):
        o_in[:, 128 * t : 128 * (t + 1)] = a3[rows * t : rows * (t + 1), :].astype(F32) * factor
    o_fout[...] = a3[rows * CHUNKS :, :].astype(F32) * factor
    o_gains[...] = (d_gains[...] * factor)[:, 0:3]


def full(shape):
    return pl.BlockSpec(shape, lambda i: (0,) * len(shape), pipeline_mode=pl.Buffered(1))


def call(body, name, args, outs, scratch=(), steps=1, flops=0, limit=48, hbm=False):
    in_specs = [pl.BlockSpec(memory_space=pltpu.SMEM)]
    arrays = [args[0]]
    groups = [None]

    def take_in(a):
        if isinstance(a, tuple):
            arrays.append(a[0])
            in_specs.append(a[1])
        else:
            arrays.append(a)
            in_specs.append(full(a.shape))

    for a in args[1:]:
        nested = isinstance(a, list) and isinstance(a[0], list)
        groups.append([len(b) for b in a] if nested else len(a) if isinstance(a, list) else None)
        for one in sum(a, []) if nested else a if isinstance(a, list) else [a]:
            take_in(one)
    flat = []
    out_groups = []
    for o in outs:
        out_groups.append(len(o) if isinstance(o, list) else None)
        flat += o if isinstance(o, list) else [o]

    def grouped(refs, sizes):
        got, at = [], 0
        for size in sizes:
            if isinstance(size, list):
                got.append(grouped(refs[at : at + sum(size)], size))
                at += sum(size)
            else:
                got.append(refs[at] if size is None else list(refs[at : at + size]))
                at += size or 1
        return got

    def run(*refs):
        n_in, n_out = len(arrays), len(flat)
        body(
            *grouped(refs[:n_in], groups), *grouped(refs[n_in : n_in + n_out], out_groups), *refs[n_in + n_out :]
        )

    if hbm or body in (pack, take, memory_back, finish_back):
        arrays = [
            pltpu.with_memory_space_constraint(a, pltpu.HBM) if math.prod(a.shape) >= 2**14 else a for a in arrays
        ]
    made = lambda s, t: pltpu.HBM(s, t) if hbm and math.prod(s) >= 2**14 and name != "self_back" else jax.ShapeDtypeStruct(s, t)
    size = sum(math.prod(a.shape) * a.dtype.itemsize for a in arrays)
    size += sum(math.prod(s) * jnp.dtype(t).itemsize for s, t, _ in flat)
    size = size if flops else 0
    got = pl.pallas_call(
        run,
        grid=(steps,),
        in_specs=in_specs,
        out_specs=tuple(full(s) if b is None else b for s, _, b in flat),
        out_shape=tuple(made(s, t) for s, t, _ in flat),
        scratch_shapes=list(scratch),
        compiler_params=pltpu.CompilerParams(vmem_limit_bytes=limit * 2**20),
        cost_estimate=pl.CostEstimate(flops=int(flops), bytes_accessed=size, transcendentals=0),
        name=name,
    )(*arrays)
    return grouped(got, out_groups)


def step_signal(step_ids, feat_width):
    half_width = feat_width // 2
    frequency = jnp.exp(-math.log(10000.0) * jnp.arange(half_width, dtype=F32) / half_width)
    angles = step_ids.astype(F32)[:, None] * frequency[None, :]
    return jnp.concatenate([jnp.sin(angles), jnp.cos(angles)], axis=1)


def sds(shape, dtype=BF, block=None):
    return (tuple(shape), dtype, block)


def per_device(
    decoder_input, timesteps, memory, cotangent, time_weight, attn_query, attn_key, attn_value, attn_out,
    cross_query, cross_key, cross_value, cross_out, ffn_in, ffn_out, norm_gains,
):
    dp = lax.axis_size("dp")
    mem_count = lax.axis_size("mem")
    rows = D // dp
    cols = D // mem_count
    by_hand = dp == 8 and mem_count == 4
    x = decoder_input[0]
    cot = cotangent[0]
    n = x.shape[0]
    r = memory.shape[0] * memory.shape[1]
    gains = norm_gains.T
    my_dp, my_mem = lax.axis_index("dp"), lax.axis_index("mem")
    me = jnp.stack([my_dp, my_mem]).astype(jnp.int32)

    def to(value, axis, bit):
        size = lax.axis_size(axis)
        return lax.ppermute(value, axis, [(i, i ^ bit) for i in range(size)])

    def after(value, *others):
        return lax.optimization_barrier((value,) + others)[0]

    def plane(own):
        return [own] + [to(own, "dp", 2 * bit) for bit in (1, 2, 3)]

    def swap(parts):
        both = []
        for part in parts:
            both += [part, to(part, "dp", 1)]
        return both

    in_parts = [ffn_in[:, D * c : D * (c + 1)] for c in range(CHUNKS)]
    if by_hand:
        first = (time_weight, attn_query, attn_key, attn_value)
        second = (attn_out, cross_query, cross_key, cross_value, cross_out)
        (own1,) = call(pack, "pack_one", (me,) + first, [sds((4, rows, D))], limit=4)
        plane1 = plane(own1)
        mem_keep, mem_send = call(take, "take_memory", (me, after(memory, own1)), [sds((2,) + memory.shape[1:])] * 2, limit=8)
        near = to(mem_send, "mem", 1)
        (own2,) = call(pack, "pack_two", (me,) + second, [sds((5, rows, D))], limit=4)
        (own3,) = call(pack, "pack_three", (me, ffn_in, ffn_out), [sds((2 * CHUNKS, rows, D))], limit=8)
        *plane1, near, own3 = lax.optimization_barrier(tuple(plane1[1:]) + (near, own3))
        (passed,) = call(join, "join_memory", (me, mem_keep, near), [sds(mem_keep.shape)], limit=8)
        across = to(passed, "mem", 2)
        g1 = [own1, to(own1, "dp", 1)]
        for part in plane1:
            g1 += [part, to(part, "dp", 1)]
        one_part = pl.BlockSpec((1,) + memory.shape[1:], lambda i: (0, 0, 0), pipeline_mode=pl.Buffered(1))
        mem_rows = [(mem_keep, one_part), (near, one_part), across]
        own2 = after(own2, *g1)
        g2 = plane(own2)
        g3 = lax.all_gather(own3, "dp", axis=0, tiled=False)
    else:

        def gather(parts):
            got = lax.all_gather(jnp.stack(parts, 0), "dp", axis=0, tiled=False)
            return got.transpose(1, 0, 2, 3).reshape(1, len(parts), D, D)

        g1 = [gather((time_weight, attn_query, attn_key, attn_value))]
        g2 = [gather((attn_out, cross_query, cross_key, cross_value, cross_out))]
        whole_out = lax.all_gather(ffn_out, "dp", axis=0, tiled=True).reshape(1, CHUNKS, D, D)
        g3 = jnp.concatenate([gather(in_parts), whole_out], axis=1)
        mem_rows = [lax.all_to_all(memory, "mem", split_axis=0, concat_axis=1, tiled=True)]
    signal = step_signal(timesteps, D).astype(BF)
    sig = jnp.broadcast_to(signal, (8, D))

    nat = pl.BlockSpec((n, PAIR), lambda i: (0, i))
    nat_r = pl.BlockSpec((r, PAIR), lambda i: (0, i))
    rows2 = pl.BlockSpec((1, 2, n), lambda i: (i, 0, 0))
    wide = lambda m: pltpu.VMEM((PAIRS, m, PAIR), BF)
    tall = lambda m: pltpu.VMEM((PAIRS, PAIR, m), BF)
    weight = pltpu.VMEM((D, D), BF)
    weights = lambda count: pltpu.VMEM((count, D, D), BF)
    proj = 2 * n * D * D * 1.5
    att_cost = 2 * n * r * D * 5
    lse_out = sds((PAIRS, 2, n), F32, rows2)
    emb, n1, q, k, v, lse1, attended = call(
        self_forward, "self_forward", (me, x, sig, gains, g1),
        [sds((1, D), F32)] + [sds((n, D), BF, nat)] * 4 + [lse_out, sds((n, D), BF, nat)],
        [weights(4), wide(n), wide(n), wide(n), wide(n), tall(n), tall(n), tall(n)],
        PAIRS, 3 * proj + 2 * att_cost, 36, True,
    )
    if by_hand:
        attended, *g2 = lax.optimization_barrier((attended,) + tuple(g2))
        g2 = swap(g2)
    mid, n2, cq, ck, cv, lse2, crossed = call(
        cross_forward, "cross_forward", (me, x, emb, attended, mem_rows, gains, g2),
        [sds((n, D), F32, nat)] + [sds((n, D), BF, nat)] * 2 + [sds((r, D), BF, nat_r)] * 2
        + [lse_out, sds((n, D), BF, nat)],
        [weights(4), pltpu.VMEM((PAIRS, n, PAIR), F32), wide(n), wide(n), wide(r), wide(r), tall(n), tall(r), tall(n)],
        PAIRS, 4 * proj + 2 * att_cost, 42, True,
    )
    if by_hand:
        weight_of = lambda t: [(p, pl.BlockSpec((1, rows, D), lambda i: (t, 0, 0))) for p in g2]
        raw_of = lambda count: [sds((dp // 2, mem_count, count * rows, cols))] * 2
        raw3_of = sds((dp, mem_count, 2 * CHUNKS * rows, cols))
    else:
        weight_of = lambda t: [(g2[0], pl.BlockSpec((1, 1, D, D), lambda i: (0, t, 0, 0)))]
        raw_of = lambda count: [sds((count, D, D))]
        raw3_of = sds((2 * CHUNKS, D, D))
    out, gl, bt, gain3, raw3 = call(
        feed_forward, "feed_forward", (me, mid, crossed, cot, gains, weight_of(4), g3),
        [sds((n, D)), sds((n, D), F32), sds((n, D)), sds((1, D), F32), sds(*raw3_of[:2], pl.BlockSpec(memory_space=pl.ANY))],
        [weights(1), weight, weight, pltpu.VMEM((n, D), BF), pltpu.VMEM((D, n), BF)] + [pltpu.VMEM((n, D), F32)] * 3
        + [pltpu.VMEM((2, n, D), BF)] * 2 + [pltpu.VMEM(raw3_of[0], BF), pltpu.SemaphoreType.DMA((CHUNKS, 2))],
        CHUNKS + 1, 25 * proj, 44, True,
    )
    back_scratch = lambda m: [
        weights(5), wide(n), tall(n), wide(m), tall(m), wide(m), wide(n), tall(n),
        pltpu.VMEM((PAIRS, 2, n), F32), tall(n), wide(m), wide(m),
    ]
    raw2, gm, b1, gain2, gk, gv = call(
        cross_back, "cross_back",
        (me, bt, gl, crossed, cq, ck, cv, (lse2, rows2), mem_rows, n2, mid, gains, g2, attended),
        [raw_of(5), sds((n, D), F32), sds((n, D)), sds((1, D), F32), sds((r, D), BF, nat_r), sds((r, D), BF, nat_r)],
        back_scratch(r) + [weights(5), pltpu.VMEM((r, D), BF), pltpu.VMEM((3, max(n, r), D), BF)], PAIRS, 8 * proj + 5 * att_cost, 58, True,
    )
    if by_hand:
        got2 = to(raw2[1], "dp", 1)
        grad_of = [sds(memory.shape[1:]), sds(memory.shape[1:]), sds((2,) + memory.shape[1:])]
    else:
        grad_of = [sds((r, D))]
    (mem_grad,) = call(
        memory_back, "memory_back", (me, gk, gv, [weight_of(2), weight_of(3)]), [grad_of], [weights(2)], 1, 0, 32,
    )
    if by_hand:
        got2 = after(got2, mem_grad[2])
        (parts2,) = call(add_core, "cross_core", (me, raw2[0], got2), [[sds((mem_count, 5 * rows, cols))] * 4], limit=24)
        b1, mem_grad[2], *parts2 = lax.optimization_barrier((b1, mem_grad[2]) + tuple(parts2))
        parts2 = [parts2[0]] + [to(parts2[b], "dp", 2 * b) for b in (1, 2, 3)]
        across = to(mem_grad[2], "mem", 2)
    raw1, gn = call(
        self_back, "self_back", (me, b1, attended, q, k, v, (lse1, rows2), n1, g1, g2),
        [raw_of(3), sds((n, D), F32)],
        back_scratch(n), PAIRS, 7 * proj + 5 * att_cost, 44, True,
    )
    if by_hand:
        two = sds((2, 5 * rows, cols))
        keep, send = raw1
        got1 = to(send, "dp", 1)
        gn, *parts2 = lax.optimization_barrier((gn,) + tuple(parts2))
        keep2, send2 = call(add_four, "cross_plane", (me, parts2), [two, two], limit=24)
        (passed,) = call(join, "join_grad", (me, mem_grad[1], across), [sds(across.shape)], limit=8)
        gn, keep2, send2, passed = lax.optimization_barrier((gn, keep2, send2, passed))
        across2 = to(send2, "mem", 2)
        near = to(passed, "mem", 1)
    quarter = pl.BlockSpec((n // 4, D), lambda i: (i, 0))
    input_grad, sums = call(
        finish_back, "finish_back",
        (me, (x, quarter), emb, (gm, quarter), (gn, quarter), gains, sig, gain2, gain3),
        [sds((n, D), BF, quarter), sds((SMALL, 128)) if by_hand else sds((8, D), F32)], [pltpu.VMEM((2, D), F32)], 4,
        6e9, 16, True,
    )

    limit = math.sqrt(9 * D * D + 2 * D * FF + 3 * D)
    if not by_hand:
        memory_grad = lax.all_to_all(mem_grad[0][None], "mem", split_axis=1, concat_axis=0, tiled=True)

        def scatter(raw):
            part = lax.psum_scatter(raw, "dp", scatter_dimension=1, tiled=True)
            part = lax.psum_scatter(part, "mem", scatter_dimension=2, tiled=True)
            return [part[t].astype(F32) for t in range(raw.shape[0])]

        d_in = scatter(raw3[:CHUNKS].transpose(1, 0, 2).reshape(1, D, FF))[0]
        d_fout = scatter(raw3[CHUNKS:].reshape(1, FF, D))[0]
        d_query, d_key, d_value = scatter(raw1[0])
        d_cout, d_cquery, d_ckey, d_cvalue, d_out = scatter(raw2[0])
        everyone = lax.all_gather(sums, ("dp", "mem"), axis=0, tiled=False)
        my_signal = lax.dynamic_slice_in_dim(everyone[:, 1], my_dp * rows, rows, axis=1)
        my_sums = lax.dynamic_slice_in_dim(everyone[:, 0], my_mem * cols, cols, axis=1)
        d_time = jnp.dot(my_signal.T, my_sums, precision=lax.Precision.HIGHEST)
        all_gains = jnp.sum(everyone[:, 2:5], axis=0)
        d_gains = lax.dynamic_slice_in_dim(all_gains, my_dp * rows, rows, axis=1).T
        weights = [d_time, d_query, d_key, d_value, d_out, d_cquery, d_ckey, d_cvalue, d_cout, d_in, d_fout]
        local = sum(jnp.sum(w * w) for w in weights)
        squares = lax.psum(local, ("dp", "mem")) + jnp.sum(all_gains * all_gains)
        factor = jnp.minimum(1.0, limit * lax.rsqrt(squares))
        return (
            (out[None], input_grad[None], memory_grad) + tuple(w * factor for w in weights) + (d_gains * factor,)
        )

    done3 = lax.psum_scatter(raw3, "dp", scatter_dimension=0, tiled=False)
    done3 = lax.psum_scatter(done3, "mem", scatter_dimension=0, tiled=False)
    one = sds((5 * rows, cols))
    keep2, send2 = call(add_pair, "cross_across", (me, keep2, across2), [one, one], limit=8)
    keep, keep2, send2 = lax.optimization_barrier((keep, keep2, send2))
    parts2 = [keep2, to(send2, "mem", 1)]
    parts1 = call(
        add_core_small, "attn_core", (me, keep, got1, sums, to(sums, "dp", 1)),
        [sds((mem_count * 3 * rows + SMALL, cols))] * 4, limit=16,
    )
    parts1 = [parts1[0]] + [to(parts1[b], "dp", 2 * b) for b in (1, 2, 3)]
    memory_grad, *parts1 = lax.optimization_barrier(
        (call(place_rows, "place_rows", (me, mem_grad[0], across, near), [sds(memory.shape)], limit=8)[0],) + tuple(parts1)
    )
    parts1 = call(add_plane, "attn_plane", (me, parts1), [sds((3 * rows + SMALL, cols))] * mem_count, limit=16)
    parts1 = [parts1[0]] + [to(parts1[b], "mem", b) for b in (1, 2, 3)]
    done1, done2, d_time, d_gains, local = call(
        add_all, "add_all", (me, parts1, parts2, done3),
        [sds((3 * rows, cols), F32), sds((5 * rows, cols), F32), sds((rows, cols), F32), sds((rows, cols), F32),
         sds((8, cols), F32)],
        limit=16,
    )
    local = local + to(local, "dp", 1)
    local = local + to(local, "dp", 2) + to(local, "dp", 4) + to(local, "dp", 6)
    planes = [local] + [to(local, "mem", b) for b in (1, 2, 3)]
    shapes = [(rows, cols)] * 9 + [(rows, FF // mem_count), (FF // dp, cols), (rows, 3)]
    scaled = call(
        scale_all, "scale_all", [me] + planes + [d_time, d_gains, done1, done2, done3],
        [sds(s, F32) for s in shapes], limit=16,
    )
    return (out[None], input_grad[None], memory_grad) + tuple(scaled)


def solution(mesh):
    tokens = P(("dp", "mem"), None, None)
    weight = P("dp", None)
    in_specs = (tokens, P(("dp", "mem")), P("dp", "mem", None), tokens) + (weight,) * 11 + (P(),)
    out_specs = (tokens, tokens, P("dp", "mem", None)) + (P("dp", "mem"),) * 11 + (P("dp", None),)
    return jax.shard_map(per_device, mesh=mesh, in_specs=in_specs, out_specs=out_specs, check_vma=False)
```

```python
import functools
import math

import jax
import jax.numpy as jnp
from jax import lax
from jax.experimental import pallas as pl
from jax.experimental.pallas import tpu as pltpu
from jax.sharding import PartitionSpec as P

D = 512
HEADS = 8
HEAD = 64
FF = 2048
PAIRS = HEADS // 2
PAIR = 2 * HEAD
CHUNKS = FF // D
BF = jnp.bfloat16
F32 = jnp.float32
SCALE = 1.0 / math.sqrt(HEAD)
ROOT_HALF = math.sqrt(0.5)
BELL = 1.0 / math.sqrt(2.0 * math.pi)


def dot(a, b, ca=1, cb=0):
    return lax.dot_general(a, b, (((ca,), (cb,)), ((), ())), preferred_element_type=F32)


def row_mean(v):
    return jnp.sum(v, axis=-1, keepdims=True) * (1.0 / v.shape[-1])


def norm_parts(v):
    centred = v - row_mean(v)
    scale = lax.rsqrt(row_mean(centred * centred) + 1e-05)
    return centred * scale, scale


def norm_back(v, gain, grad):
    normed, scale = norm_parts(v)
    c = grad * gain
    gain_part = jnp.sum(grad * normed, axis=0, keepdims=True)
    return scale * (c - row_mean(c) - normed * row_mean(c * normed)), gain_part


def build(w, slot, parts, which, me):
    dst = w.at[slot]
    if len(parts) == 1:
        blocks, _, rows, _ = parts[0].shape
        for b in range(blocks):
            dst[rows * b : rows * (b + 1), :] = parts[0][b, which]
        return
    rows = parts[0].shape[1]
    for r, part in enumerate(parts):
        lo = pl.multiple_of((r ^ me) * rows, rows)
        dst[pl.ds(lo, rows), :] = part[which]


def put(refs, at, mat, core):
    mat = mat.astype(refs[0].dtype)
    if len(refs) == 1:
        refs[0][at] = mat
        return
    half, cb, _, cols = refs[0].shape
    rows = D // (2 * half)

    def cut(own, other):
        for a in range(2 * half):
            ref = own if a % 2 == 0 else other
            for j in range(cb):
                ref[a // 2, j, rows * at : rows * (at + 1), :] = mat[
                    rows * a : rows * (a + 1), cols * j : cols * (j + 1)
                ]

    @pl.when(core == 0)
    def _():
        cut(refs[0], refs[1])

    @pl.when(core == 1)
    def _():
        cut(refs[1], refs[0])


ROWS = 256


def each_block(total, step, body):
    def run(b, carry):
        body(pl.ds(pl.multiple_of(b * step, step), step))
        return carry

    lax.fori_loop(0, total // step, run, 0)


def attend(i, qT, k, vT, oT, lse):
    n = qT.shape[2]
    row = lax.broadcasted_iota(jnp.int32, (PAIR, n), 0)
    zero = jnp.zeros((), BF)

    scores = [dot(k[i], jnp.where((row // HEAD) == h, qT[i], zero)) for h in range(2)]
    for h in range(2):
        own = slice(HEAD * h, HEAD * (h + 1))
        top = jnp.max(scores[h], axis=0, keepdims=True)
        e = jnp.exp(scores[h] - top)
        total = jnp.sum(e, axis=0, keepdims=True)
        out = dot(vT[i, own, :], e.astype(BF))
        oT[i, own, :] = (out * (1.0 / total)).astype(BF)
        lse[0, h : h + 1, :] = top + jnp.log(total)


def attend_back(i, q, qT, k, kT, v, g, gT, lse, delta, dqT, dk, dv):
    n = qT.shape[2]
    block = min(n, 512)
    row = lax.broadcasted_iota(jnp.int32, (PAIR, block), 0)
    lane = lax.broadcasted_iota(jnp.int32, (block, PAIR), 1)
    zero = jnp.zeros((), BF)
    total_k = total_v = None
    for t in range(2 * (n // block)):
        h = t % 2
        at = slice((t // 2) * block, (t // 2 + 1) * block)
        own = slice(HEAD * h, HEAD * (h + 1))
        s = dot(k[i], jnp.where((row // HEAD) == h, qT[i, :, at], zero))
        dp = dot(v[i], jnp.where((row // HEAD) == h, gT[i, :, at], zero))
        p = jnp.exp(s - lse[0, h : h + 1, at])
        ds = (p * (dp - delta[i, h : h + 1, at])).astype(BF)
        one_v = dot(p.astype(BF), jnp.where((lane // HEAD) == h, g[i, at, :], zero))
        one_k = dot(ds, jnp.where((lane // HEAD) == h, q[i, at, :], zero))
        dqT[i, own, at] = (dot(kT[i, own, :], ds) * SCALE).astype(BF)
        total_v = one_v if total_v is None else total_v + one_v
        total_k = one_k if total_k is None else total_k + one_k
    dk[i] = (total_k * SCALE).astype(BF)
    dv[i] = total_v.astype(BF)


def pairs_at(dst, rows, src):
    for p in range(PAIRS):
        dst[p, rows, :] = src[:, PAIR * p : PAIR * (p + 1)]


def pairs_at_T(dst, rows, src, scale=None):
    for p in range(PAIRS):
        t = src[:, PAIR * p : PAIR * (p + 1)].T
        dst[p, :, rows] = t if scale is None else t * jnp.asarray(scale, BF)


def joined(src, rows):
    return jnp.concatenate([src[p, rows, :] for p in range(PAIRS)], axis=1)


def joined_T(src, rows):
    return jnp.concatenate([src[p, :, rows].T for p in range(PAIRS)], axis=1)


def pairs_in(dst, src):
    for p in range(PAIRS):
        dst[p] = src[:, PAIR * p : PAIR * (p + 1)]


def pairs_in_T(dst, src, scale=None):
    for p in range(PAIRS):
        t = src[:, PAIR * p : PAIR * (p + 1)].T
        dst[p] = t if scale is None else t * jnp.asarray(scale, BF)


def from_pairs(src):
    return jnp.concatenate([src[p] for p in range(PAIRS)], axis=1)


def from_pairs_T(src):
    return jnp.concatenate([src[p].T for p in range(PAIRS)], axis=1)


def rows_of(mem):
    parts = [m[t] for m in mem for t in range(m.shape[0])]
    return jnp.concatenate(parts, axis=0) if len(parts) > 1 else parts[0]


def start_back_all(branch, weight, joined, g, gT, delta):
    grad = dot(branch, weight, 1, 1).astype(BF)
    pairs_in(g, grad)
    for p in range(PAIRS):
        gT[p] = g[p].T
        other = joined[:, PAIR * p : PAIR * (p + 1)].T
        both = gT[p].astype(F32) * other.astype(F32)
        for h in range(2):
            delta[p, h : h + 1, :] = jnp.sum(both[HEAD * h : HEAD * (h + 1), :], axis=0, keepdims=True)


def hold_rows(dst, mem):
    at = 0
    for m in mem:
        for t in range(m.shape[0]):
            dst[at : at + m.shape[1], :] = m[t]
            at += m.shape[1]


def self_forward(me, x, sig, gains, g1, emb, n1, q, k, v, lse, att, w, n1s, qs, ks, vs, qT, vT, oT):
    i = pl.program_id(0)

    @pl.when(i == 0)
    def _():
        build(w, 0, g1, 0, me[0])
        embedded = dot(sig[...], w[0])[0:1, :]
        emb[...] = embedded
        resid = x[...].astype(F32) + embedded
        normed = (norm_parts(resid)[0] * gains[0:1, :]).astype(BF)
        pairs_in(n1s, normed)
        for t, dst in ((1, qs), (2, ks), (3, vs)):
            build(w, t, g1, t, me[0])
            pairs_in(dst, dot(normed, w[t]).astype(BF))
        for p in range(PAIRS):
            qT[p] = qs[p].T * jnp.asarray(SCALE, BF)
            vT[p] = vs[p].T

    attend(i, qT, ks, vT, oT, lse)
    n1[...] = n1s[i]
    q[...] = qs[i]
    k[...] = ks[i]
    v[...] = vs[i]
    att[...] = oT[i].T


def cross_forward(
    me, x, emb, att, mem, gains, g2, mid, n2, cq, k, v, lse, crossed, w, mids, n2s, qs, ks, vs, qT, vT, oT
):
    i = pl.program_id(0)

    @pl.when(i == 0)
    def _():
        build(w, 0, g2, 0, me[0])
        new = x[...].astype(F32) + emb[...] + dot(att[...], w[0])
        pairs_in(mids, new)
        normed = (norm_parts(new)[0] * gains[1:2, :]).astype(BF)
        pairs_in(n2s, normed)
        build(w, 1, g2, 1, me[0])
        pairs_in(qs, dot(normed, w[1]).astype(BF))
        rows = rows_of(mem)
        for t, dst in ((2, ks), (3, vs)):
            build(w, t, g2, t, me[0])
            pairs_in(dst, dot(rows, w[t]).astype(BF))
        for p in range(PAIRS):
            qT[p] = qs[p].T * jnp.asarray(SCALE, BF)
            vT[p] = vs[p].T

    attend(i, qT, ks, vT, oT, lse)
    mid[...] = mids[i]
    n2[...] = n2s[i]
    cq[...] = qs[i]
    k[...] = ks[i]
    v[...] = vs[i]
    crossed[...] = oT[i].T


def feed_forward(
    me, mid, crossed, cot, gains, g2, g3,
    out, gl, bt, gain3, raw_out_ref,
    wlate, win, wout, n3, n3T, late, acc, gacc, active, grad_inner, raw, sems,
):
    i = pl.program_id(0)
    blocks, _, rows, _ = g3.shape
    n = mid.shape[0]
    each = max(blocks // CHUNKS, 1)
    now, before = i % 2, (i + 1) % 2
    piece = D // (n // ROWS)

    @pl.when(i == 0)
    def _():
        build(wlate, 0, g2, 0, me[0])

        def enter(at):
            new = mid[at, :] + dot(crossed[at, :], wlate[0])
            late[at, :] = new
            normed = (norm_parts(new)[0] * gains[2:3, :]).astype(BF)
            n3[at, :] = normed
            n3T[:, at] = normed.T
            acc[at, :] = new
            gacc[at, :] = jnp.zeros((ROWS, D), F32)

        each_block(n, ROWS, enter)

    @pl.when(i < CHUNKS)
    def _():
        for b in range(blocks):
            win[rows * b : rows * (b + 1), :] = g3[b, i]
        if blocks == 1:
            wout[...] = g3[0, CHUNKS + i]
        else:
            for u in range(each):
                for t in range(CHUNKS):
                    lo = rows * (CHUNKS * u + t)
                    wout[lo : lo + rows, :] = g3[each * i + u, CHUNKS + t]

    def hidden(at):
        inner = dot(n3[at, :], win[...])
        grad_active = dot(cot[at, :], wout[...], 1, 1)
        share = 0.5 * (1.0 + lax.erf(inner * ROOT_HALF))
        act = (inner * share).astype(BF)
        active[now, at, :] = act
        acc[at, :] += dot(act, wout[...])
        slope = share + inner * (jnp.exp(-0.5 * inner * inner) * BELL)
        grad = (slope * grad_active).astype(BF)
        grad_inner[now, at, :] = grad
        gacc[at, :] += dot(grad, win[...], 1, 1)

    def weights(b):
        c = i - 1
        at = pl.ds(pl.multiple_of(b * piece, piece), piece)
        raw_in = dot(n3T[at, :], grad_inner[before]).astype(BF)
        raw_out = dot(active[before, :, at], cot[...], 0, 0).astype(BF)
        if blocks == 1:
            raw[c, at, :] = raw_in
            raw[CHUNKS + c, at, :] = raw_out
            return
        cols = D // CHUNKS
        for a in range(piece // rows):
            for t in range(CHUNKS):
                raw[(piece // rows) * b + a, c, rows * t : rows * (t + 1), :] = raw_in[
                    rows * a : rows * (a + 1), cols * t : cols * (t + 1)
                ]
        tall = D // each
        split = tall // piece
        lo = tall + (b % split) * piece
        for j in range(CHUNKS):
            raw[each * c + b // split, j, pl.ds(pl.multiple_of(lo, piece), piece), :] = raw_out[
                :, cols * j : cols * (j + 1)
            ]

    @pl.when(i == 0)
    def _():
        each_block(n, ROWS, hidden)

    @pl.when((i > 0) & (i < CHUNKS))
    def _():
        def both(b, carry):
            weights(b)
            hidden(pl.ds(pl.multiple_of(b * ROWS, ROWS), ROWS))
            return carry

        lax.fori_loop(0, n // ROWS, both, 0)

    @pl.when(i == CHUNKS)
    def _():
        def only(b, carry):
            weights(b)
            return carry

        lax.fori_loop(0, n // ROWS, only, 0)

    def copies(c):
        if blocks == 1:
            return [
                pltpu.make_async_copy(raw.at[at], raw_out_ref.at[at], sems.at[c, k])
                for k, at in enumerate((c, CHUNKS + c))
            ]
        tall = D // each
        first = (slice(None), c, pl.ds(0, tall))
        second = (pl.ds(each * c, each), slice(None), pl.ds(tall, tall))
        return [
            pltpu.make_async_copy(raw.at[at], raw_out_ref.at[at], sems.at[c, k])
            for k, at in enumerate((first, second))
        ]

    @pl.when(i > 0)
    def _():
        for copy in copies(i - 1):
            copy.start()

    @pl.when(i == CHUNKS)
    def _():
        gain3[...] = jnp.zeros_like(gain3)

        def leave(at):
            out[at, :] = acc[at, :].astype(BF)
            part, gain_part = norm_back(late[at, :], gains[2:3, :], gacc[at, :])
            gain3[...] += gain_part
            total = cot[at, :].astype(F32) + part
            gl[at, :] = total
            bt[at, :] = total.astype(BF)

        each_block(n, ROWS, leave)
        for c in range(CHUNKS):
            for copy in copies(c):
                copy.wait()


def start_back(branch, weight, heads, g, gT, delta):
    def enter(rows):
        grad = dot(branch[rows, :], weight[...], 1, 1).astype(BF)
        pairs_at(g, rows, grad)
        for p in range(PAIRS):
            at = slice(PAIR * p, PAIR * (p + 1))
            turned = grad[:, at].T
            gT[p, :, rows] = turned
            both = turned.astype(F32) * heads[rows, at].T.astype(F32)
            for h in range(2):
                delta[p, h : h + 1, rows] = jnp.sum(both[HEAD * h : HEAD * (h + 1), :], axis=0, keepdims=True)

    each_block(branch.shape[0], ROWS, enter)


def hold_heads(src, dst, dstT, scale=None):
    def enter(rows):
        pairs_at(dst, rows, src[rows, :])
        if dstT is not None:
            pairs_at_T(dstT, rows, src[rows, :], scale)

    each_block(src.shape[0], ROWS, enter)


def put_product(refs, at, left, right, core, whole):
    def run(b, carry):
        rows = pl.ds(pl.multiple_of(b * ROWS, ROWS), ROWS)
        whole[rows, :] = dot(left[:, rows], right[...], 0, 0).astype(BF)
        return carry

    lax.fori_loop(0, D // ROWS, run, 0)
    put(refs, at, whole[...], core)


def cross_back(
    me, bt, gl, crossed, cq, k, v, lse, mem, n2, mid, gains, g2, att,
    raw, gm, b1, gain2, gk, gv,
    w, q, qT, ks, kT, vs, g, gT, delta, dqT, dk, dv, whole, held, grads,
):
    i = pl.program_id(0)
    core = me[0] % 2

    @pl.when(i == 0)
    def _():
        build(w, 0, g2, 4, me[0])
        build(w, 1, g2, 1, me[0])
        start_back(bt, w.at[0], crossed, g, gT, delta)
        put_product(raw, 0, crossed, bt, core, whole.at[0])
        hold_heads(cq, q, qT, SCALE)
        hold_heads(k, ks, kT)
        hold_heads(v, vs, None)
        hold_rows(held, mem)

    attend_back(i, q, qT, ks, kT, vs, g, gT, lse, delta, dqT, dk, dv)
    gk[...] = dk[i]
    gv[...] = dv[i]

    @pl.when(i == PAIRS - 1)
    def _():
        gain2[...] = jnp.zeros_like(gain2)

        def leave(rows):
            grad_q = joined_T(dqT, rows)
            grads[0, rows, :] = grad_q
            part, gain_part = norm_back(mid[rows, :], gains[1:2, :], dot(grad_q, w[1], 1, 1))
            gain2[...] += gain_part
            total = gl[rows, :] + part
            gm[rows, :] = total
            b1[rows, :] = total.astype(BF)

        each_block(bt.shape[0], ROWS, leave)

        def gather(rows):
            grads[1, rows, :] = joined(dk, rows)
            grads[2, rows, :] = joined(dv, rows)

        each_block(held.shape[0], ROWS, gather)
        put_product(raw, 1, n2, grads.at[0], core, whole.at[1])
        put_product(raw, 2, held, grads.at[1], core, whole.at[2])
        put_product(raw, 3, held, grads.at[2], core, whole.at[3])
        put_product(raw, 4, att, b1, core, whole.at[4])


def memory_back(me, gk, gv, g2, outs, w):
    build(w, 0, g2[0], 0, me[0])
    build(w, 1, g2[1], 0, me[0])
    back = (dot(gk[...], w[0], 1, 1) + dot(gv[...], w[1], 1, 1)).astype(BF)
    if len(outs) == 1:
        outs[0][...] = back
        return
    size = back.shape[0] // 4
    parts = [back[size * t : size * (t + 1)] for t in range(4)]
    outs[0][...], outs[1][...] = parts[0], parts[1]
    outs[2][0], outs[2][1] = parts[2], parts[3]


def self_back(
    me, b1, att, qn, k, v, lse, n1, g1, g2, x, emb, gm, gains, sig, gain2, gain3,
    raw, grad, outs,
    w, q, qT, ks, kT, vs, g, gT, delta, dqT, dk, dv, sums,
):
    i = pl.program_id(0)
    core = me[0] % 2

    @pl.when(i == 0)
    def _():
        fetch(n1, x, gm)
        build(w, 0, g2, 0, me[0])
        start_back_all(b1[...], w[0], att, g, gT, delta)
        pairs_in(q, qn)
        pairs_in_T(qT, qn, SCALE)
        pairs_in(ks, k)
        pairs_in_T(kT, k)
        pairs_in(vs, v)

    attend_back(i, q, qT, ks, kT, vs, g, gT, lse, delta, dqT, dk, dv)

    @pl.when(i == PAIRS - 1)
    def _():
        for t in range(3):
            build(w, t + 1, g1, t + 1, me[0])
        wait(n1, x, gm)
        nT = n1.ref[...].T
        grads = (from_pairs_T(dqT), from_pairs(dk), from_pairs(dv))
        for t in range(3):
            put(raw, t, dot(nT, grads[t]), core)
        sums[...] = jnp.zeros_like(sums)

        def leave(rows):
            parts = (joined_T(dqT, rows), joined(dk, rows), joined(dv, rows))
            back = sum(dot(part, w[t + 1], 1, 1) for t, part in enumerate(parts))
            resid = x.ref[rows, :].astype(F32) + emb[...]
            part, gain_part = norm_back(resid, gains[0:1, :], back)
            total = gm.ref[rows, :] + part
            grad[rows, :] = total.astype(BF)
            sums[0:1, :] += jnp.sum(total, axis=0, keepdims=True)
            sums[1:2, :] += gain_part

        each_block(b1.shape[0], ROWS, leave)
        small_rows(outs, [sums[0:1, :], sig[0:1, :].astype(F32), sums[1:2, :], gain2[...], gain3[...]])


SMALL = 32


def small_rows(outs, rows):
    if outs.shape[1] == D:
        for t, row in enumerate(rows):
            outs[t : t + 1, :] = row
        outs[5:8, :] = jnp.zeros((3, D), F32)
        return
    tile = jnp.concatenate([row[:, 128 * c : 128 * (c + 1)] for row in rows for c in range(D // 128)], axis=0)
    outs[...] = jnp.concatenate([tile, jnp.zeros((SMALL - tile.shape[0], 128), F32)], axis=0).astype(BF)


def pack(me, *refs):
    out = refs[-1]
    rows = out.shape[1]
    at = 0
    for ref in refs[:-1]:
        for c in range(ref.shape[1] // D):
            for r in range(ref.shape[0] // rows):
                out[at] = ref[rows * r : rows * (r + 1), D * c : D * (c + 1)]
                at += 1


def add_core(me, keep, got, outs):
    place = me[0] // 2
    for r, out in enumerate(outs):
        out[...] = keep[r ^ place] + got[r ^ place]


def add_core_small(me, keep, got, mine, other, *outs):
    place = me[0] // 2
    cb, size, cols = keep.shape[1:]
    a, b = mine[...].astype(F32), other[...].astype(F32)
    small = jnp.concatenate([a[0:4], b[0:4], a[4:8], b[4:8], a[8:20] + b[8:20], a[28:32]], axis=0).astype(BF)
    for r, out in enumerate(outs):
        out[0 : cb * size, :] = (keep[r ^ place] + got[r ^ place]).reshape(cb * size, cols)
        out[cb * size :, :] = small


def add_plane(me, parts, *outs):
    size = outs[0].shape[0] - SMALL
    cb = (parts[0].shape[0] - SMALL) // size
    small = [p[cb * size :, :].astype(F32) for p in parts]
    gains = small[0][16:28] + small[1][16:28] + small[2][16:28] + small[3][16:28]
    line = lax.broadcasted_iota(jnp.int32, (4, 128), 0)

    def pick(rows, which):
        return jnp.sum(jnp.where(line == which, rows, 0.0), axis=0, keepdims=True)

    signals = []
    for p in small:
        for core in range(2):
            row = pick(p[8 + 4 * core : 12 + 4 * core], me[0] // 2)
            turned = jnp.concatenate([row[:, 64:], row[:, :64]], axis=1)
            signals.append(jnp.where(me[0] % 2 == 1, turned, row))
    for r, out in enumerate(outs):
        at = r ^ me[1]
        spot = pl.ds(pl.multiple_of(at * size, size), size)
        total = sum(p[spot, :].astype(F32) for p in parts)
        out[0:size, :] = total.astype(BF)
        sums = [pick(p[4 * core : 4 * (core + 1)], at) for p in small for core in range(2)]
        rows = jnp.concatenate(sums + signals + [gains, jnp.zeros((4, 128), F32)], axis=0)
        out[size:, :] = rows.astype(BF)


def add_four(me, parts, keep, send):
    for r in range(4):
        at = r ^ me[1]
        total = sum(p[at].astype(F32) for p in parts).astype(BF)
        if r < 2:
            keep[r] = total
        else:
            send[r - 2] = total


def add_pair(me, keep, got, own, send):
    own[...] = keep[0] + got[0]
    send[...] = keep[1] + got[1]


def fold(v):
    return jnp.sum((v * v).reshape(-1, 8, v.shape[-1]), axis=0)


def add_all(me, attn, cross, feed, done1, done2, d_time, d_gains, squares):
    size = done1.shape[0]
    total1 = sum(p[0:size, :].astype(F32) for p in attn)
    done1[...] = total1
    total2 = sum(p[...].astype(F32) for p in cross)
    done2[...] = total2
    small = [p[size:, :].astype(F32) for p in attn]
    sums = jnp.concatenate([p[0:8] for p in small], axis=0).astype(BF)
    signals = jnp.concatenate([p[8:16] for p in small], axis=0).astype(BF)
    rows = d_time.shape[0]
    of_time = dot(signals, sums, 0, 0)[0:rows, :]
    d_time[...] = of_time
    gains = small[0][16:28] + small[1][16:28] + small[2][16:28] + small[3][16:28]
    line = lax.broadcasted_iota(jnp.int32, (4, 128), 0)
    lane = lax.broadcasted_iota(jnp.int32, (1, 128), 1)
    mine = []
    for t in range(3):
        row = jnp.sum(jnp.where(line == me[0] // 2, gains[4 * t : 4 * (t + 1)], 0.0), axis=0, keepdims=True)
        row = jnp.where(me[0] % 2 == 1, jnp.concatenate([row[:, 64:], row[:, :64]], axis=1), row)
        mine.append(jnp.where(lane < 64, row, 0.0))
    block = jnp.concatenate(mine + [jnp.zeros((5, 128), F32)], axis=0)
    d_gains[...] = block[0:8, :]
    wide = feed[...].astype(F32)
    squares[...] = fold(total1) + fold(total2) + fold(wide) + fold(of_time) + fold(block) * 0.25


def take(me, src, keep, send):
    for t in range(2):
        keep[t] = src[(2 * t) ^ me[1]]
        send[t] = src[(2 * t + 1) ^ me[1]]


def join(me, first, second, out):
    out[0] = first[...] if len(first.shape) == 2 else first[1]
    out[1] = second[1]


def place_rows(me, own, across, near, out):
    out[me[1]] = own[...]
    out[2 ^ me[1]] = across[0]
    out[1 ^ me[1]] = near[0]
    out[3 ^ me[1]] = near[1]


def scale_all(me, s0, s1, s2, s3, d_time, d_gains, a1, a2, a3, *outs):
    squares = jnp.sum(s0[...] + s1[...] + s2[...] + s3[...])
    limit = math.sqrt(9 * D * D + 2 * D * FF + 3 * D)
    factor = jnp.minimum(1.0, limit * lax.rsqrt(jnp.full((8, 128), squares, F32)))[0:1, :]
    o_time, o_q, o_k, o_v, o_out, o_cq, o_ck, o_cv, o_cout, o_in, o_fout, o_gains = outs
    o_time[...] = d_time[...] * factor
    rows = d_time.shape[0]
    for src, dsts in ((a1, (o_q, o_k, o_v)), (a2, (o_cout, o_cq, o_ck, o_cv, o_out))):
        for t, dst in enumerate(dsts):
            dst[...] = src[rows * t : rows * (t + 1), :] * factor
    for t in range(CHUNKS):
        o_in[:, 128 * t : 128 * (t + 1)] = a3[rows * t : rows * (t + 1), :].astype(F32) * factor
    o_fout[...] = a3[rows * CHUNKS :, :].astype(F32) * factor
    o_gains[...] = (d_gains[...] * factor)[0:3, 0 : o_gains.shape[1]]


class Late:
    def __init__(self, src, dst, sem):
        self.src, self.ref, self.sem = src, dst, sem

    def copy(self):
        return pltpu.make_async_copy(self.src, self.ref, self.sem)


def fetch(*operands):
    for one in operands:
        one.copy().start()


def wait(*operands):
    for one in operands:
        one.copy().wait()


def late(array):
    return (array, None)


def full(shape):
    return pl.BlockSpec(shape, lambda i: (0,) * len(shape), pipeline_mode=pl.Buffered(1))


def call(body, name, args, outs, scratch=(), steps=1, flops=0, limit=48, hbm=False, free=()):
    in_specs = [pl.BlockSpec(memory_space=pltpu.SMEM)]
    arrays = [args[0]]
    groups = [None]

    later = []

    def take_in(a):
        if isinstance(a, tuple) and a[1] is None:
            later.append(len(arrays))
            arrays.append(a[0])
            in_specs.append(pl.BlockSpec(memory_space=pl.ANY))
        elif isinstance(a, tuple):
            arrays.append(a[0])
            in_specs.append(a[1])
        else:
            arrays.append(a)
            in_specs.append(full(a.shape))

    for a in args[1:]:
        nested = isinstance(a, list) and isinstance(a[0], list)
        groups.append([len(b) for b in a] if nested else len(a) if isinstance(a, list) else None)
        for one in sum(a, []) if nested else a if isinstance(a, list) else [a]:
            take_in(one)
    flat = []
    out_groups = []
    for o in outs:
        out_groups.append(len(o) if isinstance(o, list) else None)
        flat += o if isinstance(o, list) else [o]

    def grouped(refs, sizes):
        got, at = [], 0
        for size in sizes:
            if isinstance(size, list):
                got.append(grouped(refs[at : at + sum(size)], size))
                at += sum(size)
            else:
                got.append(refs[at] if size is None else list(refs[at : at + size]))
                at += size or 1
        return got

    def run(*refs):
        n_in, n_out = len(arrays), len(flat)
        refs = list(refs)
        for k in reversed(range(len(later))):
            sem, held = refs.pop(), refs.pop()
            refs[later[k]] = Late(refs[later[k]], held, sem)
        body(
            *grouped(refs[:n_in], groups), *grouped(refs[n_in : n_in + n_out], out_groups), *refs[n_in + n_out :]
        )

    if hbm or body in (pack, take):
        arrays = [
            pltpu.with_memory_space_constraint(a, pltpu.HBM) if math.prod(a.shape) >= 2**14 else a for a in arrays
        ]
    made = lambda s, t, k: (
        pltpu.HBM(s, t) if hbm and math.prod(s) >= 2**14 and k not in free else jax.ShapeDtypeStruct(s, t)
    )
    size = sum(math.prod(a.shape) * a.dtype.itemsize for a in arrays)
    size += sum(math.prod(s) * jnp.dtype(t).itemsize for s, t, _ in flat)
    size = size if flops else 0
    got = pl.pallas_call(
        run,
        grid=(steps,),
        in_specs=in_specs,
        out_specs=tuple(full(s) if b is None else b for s, _, b in flat),
        out_shape=tuple(made(s, t, k) for k, (s, t, _) in enumerate(flat)),
        scratch_shapes=list(scratch)
        + [one for k in later for one in (pltpu.VMEM(arrays[k].shape, arrays[k].dtype), pltpu.SemaphoreType.DMA(()))],
        compiler_params=pltpu.CompilerParams(vmem_limit_bytes=limit * 2**20),
        cost_estimate=pl.CostEstimate(flops=int(flops), bytes_accessed=size, transcendentals=0),
        name=name,
    )(*arrays)
    return grouped(got, out_groups)


def step_signal(step_ids, feat_width):
    half_width = feat_width // 2
    frequency = jnp.exp(-math.log(10000.0) * jnp.arange(half_width, dtype=F32) / half_width)
    angles = step_ids.astype(F32)[:, None] * frequency[None, :]
    return jnp.concatenate([jnp.sin(angles), jnp.cos(angles)], axis=1)


def sds(shape, dtype=BF, block=None):
    return (tuple(shape), dtype, block)


def per_device(
    decoder_input, timesteps, memory, cotangent, time_weight, attn_query, attn_key, attn_value, attn_out,
    cross_query, cross_key, cross_value, cross_out, ffn_in, ffn_out, norm_gains,
):
    dp = lax.axis_size("dp")
    mem_count = lax.axis_size("mem")
    rows = D // dp
    cols = D // mem_count
    by_hand = dp == 8 and mem_count == 4
    x = decoder_input[0]
    cot = cotangent[0]
    n = x.shape[0]
    r = memory.shape[0] * memory.shape[1]
    gains = norm_gains.T
    my_dp, my_mem = lax.axis_index("dp"), lax.axis_index("mem")
    me = jnp.stack([my_dp, my_mem]).astype(jnp.int32)

    def to(value, axis, bit):
        size = lax.axis_size(axis)
        return lax.ppermute(value, axis, [(i, i ^ bit) for i in range(size)])

    def after(value, *others):
        return lax.optimization_barrier((value,) + others)[0]

    def plane(own):
        return [own] + [to(own, "dp", 2 * bit) for bit in (1, 2, 3)]

    def swap(parts):
        both = []
        for part in parts:
            both += [part, to(part, "dp", 1)]
        return both

    in_parts = [ffn_in[:, D * c : D * (c + 1)] for c in range(CHUNKS)]
    if by_hand:
        first = (time_weight, attn_query, attn_key, attn_value)
        second = (attn_out, cross_query, cross_key, cross_value, cross_out)
        (own1,) = call(pack, "pack_one", (me,) + first, [sds((4, rows, D))], limit=4)
        plane1 = plane(own1)
        mem_keep, mem_send = call(
            take, "take_memory", (me, after(memory, own1)), [sds((2,) + memory.shape[1:])] * 2, limit=8
        )
        (own2,) = call(pack, "pack_two", (me,) + second, [sds((5, rows, D))], limit=4)
        (own3,) = call(pack, "pack_three", (me, ffn_in, ffn_out), [sds((2 * CHUNKS, rows, D))], limit=8)
        near = to(mem_send, "mem", 1)
        *plane1, near, own2, own3 = lax.optimization_barrier(tuple(plane1[1:]) + (near, own2, own3))
        (passed,) = call(join, "join_memory", (me, mem_keep, near), [sds(mem_keep.shape)], limit=8)
        across = to(passed, "mem", 2)
        g1 = [own1, to(own1, "dp", 1)]
        for part in plane1:
            g1 += [part, to(part, "dp", 1)]
        one_part = pl.BlockSpec((1,) + memory.shape[1:], lambda i: (0, 0, 0), pipeline_mode=pl.Buffered(1))
        mem_rows = [(mem_keep, one_part), (near, one_part), across]
        own2 = after(own2, *g1)
        g2 = plane(own2)
        g3 = lax.all_gather(own3, "dp", axis=0, tiled=False)
    else:

        def gather(parts):
            got = lax.all_gather(jnp.stack(parts, 0), "dp", axis=0, tiled=False)
            return got.transpose(1, 0, 2, 3).reshape(1, len(parts), D, D)

        g1 = [gather((time_weight, attn_query, attn_key, attn_value))]
        g2 = [gather((attn_out, cross_query, cross_key, cross_value, cross_out))]
        whole_out = lax.all_gather(ffn_out, "dp", axis=0, tiled=True).reshape(1, CHUNKS, D, D)
        g3 = jnp.concatenate([gather(in_parts), whole_out], axis=1)
        mem_rows = [lax.all_to_all(memory, "mem", split_axis=0, concat_axis=1, tiled=True)]
    signal = step_signal(timesteps, D).astype(BF)
    sig = jnp.broadcast_to(signal, (8, D))

    nat = pl.BlockSpec((n, PAIR), lambda i: (0, i))
    nat_r = pl.BlockSpec((r, PAIR), lambda i: (0, i))
    rows2 = pl.BlockSpec((1, 2, n), lambda i: (i, 0, 0))
    wide = lambda m: pltpu.VMEM((PAIRS, m, PAIR), BF)
    tall = lambda m: pltpu.VMEM((PAIRS, PAIR, m), BF)
    weight = pltpu.VMEM((D, D), BF)
    weights = lambda count: pltpu.VMEM((count, D, D), BF)
    proj = 2 * n * D * D * 1.5
    att_cost = 2 * n * r * D * 5
    lse_out = sds((PAIRS, 2, n), F32, rows2)
    emb, n1, q, k, v, lse1, attended = call(
        self_forward, "self_forward", (me, x, sig, gains, g1),
        [sds((1, D), F32)] + [sds((n, D), BF, nat)] * 4 + [lse_out, sds((n, D), BF, nat)],
        [weights(4), wide(n), wide(n), wide(n), wide(n), tall(n), tall(n), tall(n)],
        PAIRS, 3 * proj + 2 * att_cost, 36, True,
    )
    if by_hand:
        attended, *g2 = lax.optimization_barrier((attended,) + tuple(g2))
        g2 = swap(g2)
    mid, n2, cq, ck, cv, lse2, crossed = call(
        cross_forward, "cross_forward", (me, x, emb, attended, mem_rows, gains, g2),
        [sds((n, D), F32, nat)] + [sds((n, D), BF, nat)] * 2 + [sds((r, D), BF, nat_r)] * 2
        + [lse_out, sds((n, D), BF, nat)],
        [weights(4), pltpu.VMEM((PAIRS, n, PAIR), F32), wide(n), wide(n), wide(r), wide(r), tall(n), tall(r), tall(n)],
        PAIRS, 4 * proj + 2 * att_cost, 42, True,
    )
    if by_hand:
        weight_of = lambda t: [(p, pl.BlockSpec((1, rows, D), lambda i: (t, 0, 0))) for p in g2]
        raw_of = lambda count: [sds((dp // 2, mem_count, count * rows, cols))] * 2
        raw3_of = sds((dp, mem_count, 2 * CHUNKS * rows, cols))
    else:
        weight_of = lambda t: [(g2[0], pl.BlockSpec((1, 1, D, D), lambda i: (0, t, 0, 0)))]
        raw_of = lambda count: [sds((count, D, D))]
        raw3_of = sds((2 * CHUNKS, D, D))
    out, gl, bt, gain3, raw3 = call(
        feed_forward, "feed_forward", (me, mid, crossed, cot, gains, weight_of(4), g3),
        [sds((n, D)), sds((n, D), F32), sds((n, D)), sds((1, D), F32), sds(*raw3_of[:2], pl.BlockSpec(memory_space=pl.ANY))],
        [weights(1), weight, weight, pltpu.VMEM((n, D), BF), pltpu.VMEM((D, n), BF)] + [pltpu.VMEM((n, D), F32)] * 3
        + [pltpu.VMEM((2, n, D), BF)] * 2 + [pltpu.VMEM(raw3_of[0], BF), pltpu.SemaphoreType.DMA((CHUNKS, 2))],
        CHUNKS + 1, 25 * proj, 44, True,
    )
    back_scratch = lambda m: [
        weights(5), wide(n), tall(n), wide(m), tall(m), wide(m), wide(n), tall(n),
        pltpu.VMEM((PAIRS, 2, n), F32), tall(n), wide(m), wide(m),
    ]
    raw2, gm, b1, gain2, gk, gv = call(
        cross_back, "cross_back",
        (me, bt, gl, crossed, cq, ck, cv, (lse2, rows2), mem_rows, n2, mid, gains, g2, attended),
        [raw_of(5), sds((n, D), F32), sds((n, D)), sds((1, D), F32), sds((r, D), BF, nat_r), sds((r, D), BF, nat_r)],
        back_scratch(r) + [weights(5), pltpu.VMEM((r, D), BF), pltpu.VMEM((3, max(n, r), D), BF)], PAIRS, 8 * proj + 5 * att_cost, 58, True,
    )
    if by_hand:
        got2 = to(raw2[1], "dp", 1)
        grad_of = [sds(memory.shape[1:]), sds(memory.shape[1:]), sds((2,) + memory.shape[1:])]
    else:
        grad_of = [sds((r, D))]
    (mem_grad,) = call(
        memory_back, "memory_back", (me, gk, gv, [weight_of(2), weight_of(3)]), [grad_of], [weights(2)], 1, 0, 32,
    )
    if by_hand:
        got2 = after(got2, mem_grad[2])
        (parts2,) = call(add_core, "cross_core", (me, raw2[0], got2), [[sds((mem_count, 5 * rows, cols))] * 4], limit=24)
        b1, mem_grad[2], *parts2 = lax.optimization_barrier((b1, mem_grad[2]) + tuple(parts2))
        parts2 = [parts2[0]] + [to(parts2[b], "dp", 2 * b) for b in (1, 2, 3)]
        across = to(mem_grad[2], "mem", 2)
    raw1, input_grad, sums = call(
        self_back, "self_back",
        (me, b1, attended, q, k, v, (lse1, rows2), late(n1), g1, g2, late(x), emb, late(gm), gains, sig, gain2, gain3),
        [raw_of(3), sds((n, D)), sds((SMALL, 128)) if by_hand else sds((8, D), F32)],
        back_scratch(n) + [pltpu.VMEM((2, D), F32)], PAIRS, 7 * proj + 5 * att_cost, 48, True,
    )
    if by_hand:
        two = sds((2, 5 * rows, cols))
        keep, send = raw1
        got1, small1 = to(send, "dp", 1), to(sums, "dp", 1)
        done3 = lax.psum_scatter(raw3, "dp", scatter_dimension=0, tiled=False)
        done3 = lax.psum_scatter(done3, "mem", scatter_dimension=0, tiled=False)
        done3 = pltpu.with_memory_space_constraint(done3, pltpu.HBM)
        sums, done3, *parts2 = lax.optimization_barrier((sums, done3) + tuple(parts2))
        keep2, send2 = call(add_four, "cross_plane", (me, parts2), [two, two], limit=24, hbm=True, free=(0, 1))
        (passed,) = call(join, "join_grad", (me, mem_grad[1], after(across, keep2)), [sds(across.shape)], limit=8, flops=6e9)
        sums, keep, keep2, send2, passed = lax.optimization_barrier((sums, keep, keep2, send2, passed))
        across2 = to(send2, "mem", 2)

    limit = math.sqrt(9 * D * D + 2 * D * FF + 3 * D)
    if not by_hand:
        memory_grad = lax.all_to_all(mem_grad[0][None], "mem", split_axis=1, concat_axis=0, tiled=True)

        def scatter(raw):
            part = lax.psum_scatter(raw, "dp", scatter_dimension=1, tiled=True)
            part = lax.psum_scatter(part, "mem", scatter_dimension=2, tiled=True)
            return [part[t].astype(F32) for t in range(raw.shape[0])]

        d_in = scatter(raw3[:CHUNKS].transpose(1, 0, 2).reshape(1, D, FF))[0]
        d_fout = scatter(raw3[CHUNKS:].reshape(1, FF, D))[0]
        d_query, d_key, d_value = scatter(raw1[0])
        d_cout, d_cquery, d_ckey, d_cvalue, d_out = scatter(raw2[0])
        everyone = lax.all_gather(sums, ("dp", "mem"), axis=0, tiled=False)
        my_signal = lax.dynamic_slice_in_dim(everyone[:, 1], my_dp * rows, rows, axis=1)
        my_sums = lax.dynamic_slice_in_dim(everyone[:, 0], my_mem * cols, cols, axis=1)
        d_time = jnp.dot(my_signal.T, my_sums, precision=lax.Precision.HIGHEST)
        all_gains = jnp.sum(everyone[:, 2:5], axis=0)
        d_gains = lax.dynamic_slice_in_dim(all_gains, my_dp * rows, rows, axis=1).T
        weights = [d_time, d_query, d_key, d_value, d_out, d_cquery, d_ckey, d_cvalue, d_cout, d_in, d_fout]
        local = sum(jnp.sum(w * w) for w in weights)
        squares = lax.psum(local, ("dp", "mem")) + jnp.sum(all_gains * all_gains)
        factor = jnp.minimum(1.0, limit * lax.rsqrt(squares))
        return (
            (out[None], input_grad[None], memory_grad) + tuple(w * factor for w in weights) + (d_gains * factor,)
        )

    parts1 = call(
        add_core_small, "attn_core", (me, keep, got1, sums, small1),
        [sds((mem_count * 3 * rows + SMALL, cols))] * 4, limit=16,
    )
    parts1 = [parts1[0]] + [to(parts1[b], "dp", 2 * b) for b in (1, 2, 3)]
    one = sds((5 * rows, cols))
    keep2, send2 = call(add_pair, "cross_across", (me, keep2, across2), [one, one], limit=8)
    send2, *parts1 = lax.optimization_barrier((send2,) + tuple(parts1))
    parts2 = [keep2, to(send2, "mem", 1)]
    parts1 = call(add_plane, "attn_plane", (me, parts1), [sds((3 * rows + SMALL, cols))] * mem_count, limit=16)
    parts1 = [parts1[0]] + [to(parts1[b], "mem", b) for b in (1, 2, 3)]
    done1, done2, d_time, d_gains, local = call(
        add_all, "add_all", (me, parts1, parts2, done3),
        [sds((3 * rows, cols), F32), sds((5 * rows, cols), F32), sds((rows, cols), F32), sds((8, cols), F32),
         sds((8, cols), F32)],
        limit=16,
    )
    near = to(after(passed, local), "mem", 1)
    (memory_grad,) = call(place_rows, "place_rows", (me, mem_grad[0], across, near), [sds(memory.shape)], limit=8)
    local = local + to(local, "dp", 1)
    local = local + to(local, "dp", 2) + to(local, "dp", 4) + to(local, "dp", 6)
    planes = [local] + [to(local, "mem", b) for b in (1, 2, 3)]
    shapes = [(rows, cols)] * 9 + [(rows, FF // mem_count), (FF // dp, cols), (3, rows)]
    scaled = call(
        scale_all, "scale_all", [me] + planes + [d_time, d_gains, done1, done2, done3],
        [sds(s, F32) for s in shapes], limit=16,
    )
    return (out[None], input_grad[None], memory_grad) + tuple(scaled[:-1]) + (scaled[-1].T,)


def solution(mesh):
    tokens = P(("dp", "mem"), None, None)
    weight = P("dp", None)
    in_specs = (tokens, P(("dp", "mem")), P("dp", "mem", None), tokens) + (weight,) * 11 + (P(),)
    out_specs = (tokens, tokens, P("dp", "mem", None)) + (P("dp", "mem"),) * 11 + (P("dp", None),)
    return jax.shard_map(per_device, mesh=mesh, in_specs=in_specs, out_specs=out_specs, check_vma=False)
```

```python
import functools
import math

import jax
import jax.numpy as jnp
from jax import lax
from jax.experimental import pallas as pl
from jax.experimental.pallas import tpu as pltpu
from jax.sharding import PartitionSpec as P

D = 512
HEADS = 8
HEAD = 64
FF = 2048
PAIRS = HEADS // 2
PAIR = 2 * HEAD
CHUNKS = FF // D
BF = jnp.bfloat16
F32 = jnp.float32
SCALE = 1.0 / math.sqrt(HEAD)
ROOT_HALF = math.sqrt(0.5)
BELL = 1.0 / math.sqrt(2.0 * math.pi)


def dot(a, b, ca=1, cb=0):
    return lax.dot_general(a, b, (((ca,), (cb,)), ((), ())), preferred_element_type=F32)


def row_mean(v):
    return jnp.sum(v, axis=-1, keepdims=True) * (1.0 / v.shape[-1])


def norm_parts(v):
    centred = v - row_mean(v)
    scale = lax.rsqrt(row_mean(centred * centred) + 1e-05)
    return centred * scale, scale


def norm_back(v, gain, grad):
    normed, scale = norm_parts(v)
    c = grad * gain
    gain_part = jnp.sum(grad * normed, axis=0, keepdims=True)
    return scale * (c - row_mean(c) - normed * row_mean(c * normed)), gain_part


def build(w, slot, parts, which, me):
    dst = w.at[slot]
    if len(parts) == 1:
        blocks, _, rows, _ = parts[0].shape
        for b in range(blocks):
            dst[rows * b : rows * (b + 1), :] = parts[0][b, which]
        return
    rows = parts[0].shape[1]
    for r, part in enumerate(parts):
        lo = pl.multiple_of((r ^ me) * rows, rows)
        dst[pl.ds(lo, rows), :] = part[which]


def put(refs, at, mat, core):
    mat = mat.astype(refs[0].dtype)
    if len(refs) == 1:
        refs[0][at] = mat
        return
    half, cb, _, cols = refs[0].shape
    rows = D // (2 * half)

    def cut(own, other):
        for a in range(2 * half):
            ref = own if a % 2 == 0 else other
            for j in range(cb):
                ref[a // 2, j, rows * at : rows * (at + 1), :] = mat[
                    rows * a : rows * (a + 1), cols * j : cols * (j + 1)
                ]

    @pl.when(core == 0)
    def _():
        cut(refs[0], refs[1])

    @pl.when(core == 1)
    def _():
        cut(refs[1], refs[0])


ROWS = 512


def each_block(total, step, body):
    def run(b, carry):
        body(pl.ds(pl.multiple_of(b * step, step), step))
        return carry

    lax.fori_loop(0, total // step, run, 0)


SAFE = 1444.0


def judge(flags, qT, k):
    line = lax.broadcasted_iota(jnp.int32, (8, PAIR), 0)
    lane = lax.broadcasted_iota(jnp.int32, (8, PAIR), 1)
    mine = jnp.where((lane // HEAD) == line, 1.0, 0.0).astype(BF)
    for p in range(PAIRS):
        of_q = jnp.max(dot(mine, qT[p] * qT[p]), axis=1, keepdims=True)
        of_k = jnp.max(dot(mine, k[p] * k[p], 1, 1), axis=1, keepdims=True)
        flags[p] = jnp.where(jnp.max(of_q * of_k) <= SAFE, 1, 0)


def attend(i, flags, qT, k, vT, oT, lse):
    n = qT.shape[2]
    row = lax.broadcasted_iota(jnp.int32, (PAIR, n), 0)
    zero = jnp.zeros((), BF)

    def run(shifted):
        scores = [dot(k[i], jnp.where((row // HEAD) == h, qT[i], zero)) for h in range(2)]
        for h in range(2):
            own = slice(HEAD * h, HEAD * (h + 1))
            score = scores[h]
            top = jnp.max(score, axis=0, keepdims=True) if shifted else None
            e = jnp.exp(score - top if shifted else score)
            total = jnp.sum(e, axis=0, keepdims=True)
            out = dot(vT[i, own, :], e.astype(BF))
            oT[i, own, :] = (out * (1.0 / total)).astype(BF)
            lse[0, h : h + 1, :] = top + jnp.log(total) if shifted else jnp.log(total)

    @pl.when(flags[i] == 1)
    def _():
        run(False)

    @pl.when(flags[i] == 0)
    def _():
        run(True)


def attend_back(i, q, qT, k, kT, v, g, gT, lse, delta, dq, dk, dv):
    n = qT.shape[2]
    block = min(n, 512)
    row = lax.broadcasted_iota(jnp.int32, (PAIR, block), 0)
    lane = lax.broadcasted_iota(jnp.int32, (block, PAIR), 1)
    zero = jnp.zeros((), BF)
    total_k = total_v = None
    for j in range(n // block):
        at = slice(j * block, (j + 1) * block)
        turned = []
        for h in range(2):
            own = slice(HEAD * h, HEAD * (h + 1))
            s = dot(k[i], jnp.where((row // HEAD) == h, qT[i, :, at], zero))
            dp = dot(v[i], jnp.where((row // HEAD) == h, gT[i, :, at], zero))
            p = jnp.exp(s - lse[0, h : h + 1, at])
            ds = (p * (dp - delta[i, h : h + 1, at])).astype(BF)
            one_v = dot(p.astype(BF), jnp.where((lane // HEAD) == h, g[i, at, :], zero))
            one_k = dot(ds, jnp.where((lane // HEAD) == h, q[i, at, :], zero))
            turned.append((dot(kT[i, own, :], ds) * SCALE).astype(BF))
            total_v = one_v if total_v is None else total_v + one_v
            total_k = one_k if total_k is None else total_k + one_k
        dq[i, at, :] = jnp.concatenate(turned, axis=0).T
    dk[i] = (total_k * SCALE).astype(BF)
    dv[i] = total_v.astype(BF)


def prepare(p, q, k, g, heads, qT, kT, gT, delta):
    qT[p] = q[p].T * jnp.asarray(SCALE, BF)
    kT[p] = k[p].T
    gT[p] = g[p].T
    both = gT[p].astype(F32) * heads[p].T.astype(F32)
    for h in range(2):
        delta[p, h : h + 1, :] = jnp.sum(both[HEAD * h : HEAD * (h + 1), :], axis=0, keepdims=True)


def products(refs, first, leftT, rights, core, whole):
    def run(b, carry):
        rows = pl.ds(pl.multiple_of(b * ROWS, ROWS), ROWS)
        for t, right in enumerate(rights):
            whole[first + t, rows, :] = dot(leftT[rows, :], from_pairs(right)).astype(BF)
        return carry

    lax.fori_loop(0, D // ROWS, run, 0)
    for t in range(len(rights)):
        put(refs, first + t, whole[first + t], core)


def turn_pairs(dst, src):
    for p in range(PAIRS):
        dst[PAIR * p : PAIR * (p + 1), :] = src[p].T


def pairs_at(dst, rows, src):
    for p in range(PAIRS):
        dst[p, rows, :] = src[:, PAIR * p : PAIR * (p + 1)]


def joined(src, rows):
    return jnp.concatenate([src[p, rows, :] for p in range(PAIRS)], axis=1)


def pairs_in(dst, src):
    for p in range(PAIRS):
        dst[p] = src[:, PAIR * p : PAIR * (p + 1)]


def from_pairs(src):
    return jnp.concatenate([src[p] for p in range(PAIRS)], axis=1)


def from_pairs_T(src):
    return jnp.concatenate([src[p].T for p in range(PAIRS)], axis=1)


def rows_of(mem):
    parts = [m[t] for m in mem for t in range(m.shape[0])]
    return jnp.concatenate(parts, axis=0) if len(parts) > 1 else parts[0]


def self_forward(me, x, sig, gains, g1, emb, n1, q, k, v, lse, att, w, n1s, qs, ks, vs, qT, vT, oT, flags):
    i = pl.program_id(0)

    @pl.when(i == 0)
    def _():
        build(w, 0, g1, 0, me[0])
        embedded = dot(sig[...], w[0])[0:1, :]
        emb[...] = embedded
        resid = x[...].astype(F32) + embedded
        normed = (norm_parts(resid)[0] * gains[0:1, :]).astype(BF)
        pairs_in(n1s, normed)
        for t, dst in ((1, qs), (2, ks), (3, vs)):
            build(w, t, g1, t, me[0])
            pairs_in(dst, dot(normed, w[t]).astype(BF))
        for p in range(PAIRS):
            qT[p] = qs[p].T * jnp.asarray(SCALE, BF)
            vT[p] = vs[p].T
        judge(flags, qT, ks)

    attend(i, flags, qT, ks, vT, oT, lse)
    n1[0] = n1s[i]
    q[0] = qs[i]
    k[0] = ks[i]
    v[0] = vs[i]
    att[0] = oT[i].T


def cross_forward(
    me, x, emb, att, mem, gains, g2, mid, n2, cq, k, v, lse, crossed, w, mids, n2s, qs, ks, vs, qT, vT, oT, flags
):
    i = pl.program_id(0)

    @pl.when(i == 0)
    def _():
        fetch(*mem)
        build(w, 0, g2, 0, me[0])
        new = x[...].astype(F32) + emb[...] + dot(from_pairs(att), w[0])
        pairs_in(mids, new)
        normed = (norm_parts(new)[0] * gains[1:2, :]).astype(BF)
        pairs_in(n2s, normed)
        build(w, 1, g2, 1, me[0])
        pairs_in(qs, dot(normed, w[1]).astype(BF))
        wait(*mem)
        rows = rows_of([m.ref for m in mem])
        for t, dst in ((2, ks), (3, vs)):
            build(w, t, g2, t, me[0])
            pairs_in(dst, dot(rows, w[t]).astype(BF))
        for p in range(PAIRS):
            qT[p] = qs[p].T * jnp.asarray(SCALE, BF)
            vT[p] = vs[p].T
        judge(flags, qT, ks)

    attend(i, flags, qT, ks, vT, oT, lse)
    mid[...] = mids[i]
    n2[0] = n2s[i]
    cq[0] = qs[i]
    k[0] = ks[i]
    v[0] = vs[i]
    crossed[0] = oT[i].T


def feed_forward(
    me, mid, crossed, cot, gains, g2, g3,
    out, gl, bt, gain3, raw_out_ref,
    wlate, win, wout, n3, n3T, late, acc, gacc, active, grad_inner, raw, sems,
):
    i = pl.program_id(0)
    blocks, _, rows, _ = g3.ref.shape
    n = mid.shape[0]
    each = max(blocks // CHUNKS, 1)
    now, before = i % 2, (i + 1) % 2
    piece = D // (n // 512)

    @pl.when(i == 0)
    def _():
        fetch(cot, g3)
        build(wlate, 0, g2, 0, me[0])

        def enter(at):
            new = mid[at, :] + dot(joined(crossed, at), wlate[0])
            late[at, :] = new
            normed = (norm_parts(new)[0] * gains[2:3, :]).astype(BF)
            n3[at, :] = normed
            n3T[:, at] = normed.T
            acc[at, :] = new
            gacc[at, :] = jnp.zeros((ROWS, D), F32)

        each_block(n, ROWS, enter)
        wait(cot, g3)

    @pl.when(i < CHUNKS)
    def _():
        for b in range(blocks):
            win[rows * b : rows * (b + 1), :] = g3.ref[b, i]
        if blocks == 1:
            wout[...] = g3.ref[0, CHUNKS + i]
        else:
            for u in range(each):
                for t in range(CHUNKS):
                    lo = rows * (CHUNKS * u + t)
                    wout[lo : lo + rows, :] = g3.ref[each * i + u, CHUNKS + t]

    def hidden(at):
        inner = dot(n3[at, :], win[...])
        grad_active = dot(cot.ref[at, :], wout[...], 1, 1)
        share = 0.5 * (1.0 + lax.erf(inner * ROOT_HALF))
        act = (inner * share).astype(BF)
        active[now, at, :] = act
        acc[at, :] += dot(act, wout[...])
        slope = share + inner * (jnp.exp(-0.5 * inner * inner) * BELL)
        grad = (slope * grad_active).astype(BF)
        grad_inner[now, at, :] = grad
        gacc[at, :] += dot(grad, win[...], 1, 1)

    def weights(b):
        c = i - 1
        at = pl.ds(pl.multiple_of(b * piece, piece), piece)
        raw_in = dot(n3T[at, :], grad_inner[before]).astype(BF)
        raw_out = dot(active[before, :, at], cot.ref[...], 0, 0).astype(BF)
        if blocks == 1:
            raw[c, at, :] = raw_in
            raw[CHUNKS + c, at, :] = raw_out
            return
        cols = D // CHUNKS
        for a in range(piece // rows):
            for t in range(CHUNKS):
                raw[(piece // rows) * b + a, c, rows * t : rows * (t + 1), :] = raw_in[
                    rows * a : rows * (a + 1), cols * t : cols * (t + 1)
                ]
        tall = D // each
        split = tall // piece
        lo = tall + (b % split) * piece
        for j in range(CHUNKS):
            raw[each * c + b // split, j, pl.ds(pl.multiple_of(lo, piece), piece), :] = raw_out[
                :, cols * j : cols * (j + 1)
            ]

    @pl.when(i == 0)
    def _():
        each_block(n, 512, hidden)

    @pl.when((i > 0) & (i < CHUNKS))
    def _():
        def both(b, carry):
            weights(b)
            hidden(pl.ds(pl.multiple_of(b * 512, 512), 512))
            return carry

        lax.fori_loop(0, n // 512, both, 0)

    @pl.when(i == CHUNKS)
    def _():
        def only(b, carry):
            weights(b)
            return carry

        lax.fori_loop(0, n // 512, only, 0)

    def copies(c):
        if blocks == 1:
            return [
                pltpu.make_async_copy(raw.at[at], raw_out_ref.at[at], sems.at[c, k])
                for k, at in enumerate((c, CHUNKS + c))
            ]
        tall = D // each
        first = (slice(None), c, pl.ds(0, tall))
        second = (pl.ds(each * c, each), slice(None), pl.ds(tall, tall))
        return [
            pltpu.make_async_copy(raw.at[at], raw_out_ref.at[at], sems.at[c, k])
            for k, at in enumerate((first, second))
        ]

    @pl.when(i > 0)
    def _():
        for copy in copies(i - 1):
            copy.start()

    @pl.when(i == CHUNKS)
    def _():
        gain3[...] = jnp.zeros_like(gain3)

        def leave(at):
            out.ref[at, :] = acc[at, :].astype(BF)
            part, gain_part = norm_back(late[at, :], gains[2:3, :], gacc[at, :])
            gain3[...] += gain_part
            total = cot.ref[at, :].astype(F32) + part
            gl.ref[at, :] = total
            bt.ref[at, :] = total.astype(BF)
            for one in (out, gl, bt):
                one.copy(at.start // ROWS).start()

        each_block(n, ROWS, leave)
        for one in (out, gl, bt):
            one.finish()
        for c in range(CHUNKS):
            for copy in copies(c):
                copy.wait()


def start_back(branch, weight, g):
    def enter(rows):
        pairs_at(g, rows, dot(branch[rows, :], weight[...], 1, 1).astype(BF))

    each_block(branch.shape[0], ROWS, enter)


def cross_back(
    me, bt, crossed, late_q, late_k, late_v, lse, mem, n2, mid, gl, gains, g2_out, g2_query, att,
    raw, gm, b1, gain2, gk, gv,
    w, qT, kT, g, gT, delta, dq, dk, dv, whole, leftT,
):
    i = pl.program_id(0)
    core = me[0] % 2
    q, k, v = late_q.ref, late_k.ref, late_v.ref
    turned = (q, k, g, crossed, qT, kT, gT, delta)

    @pl.when(i == 0)
    def _():
        fetch(late_q, late_k, late_v, *mem, n2, mid, gl, att)
        build(w, 0, g2_out, 0, me[0])
        build(w, 1, g2_query, 0, me[0])
        start_back(bt, w.at[0], g)
        turn_pairs(leftT, crossed)
        wait(late_q, late_k, late_v)
        prepare(0, *turned)

        def run(b, carry):
            rows = pl.ds(pl.multiple_of(b * ROWS, ROWS), ROWS)
            whole[0, rows, :] = dot(leftT[rows, 0 : bt.shape[0]], bt[...]).astype(BF)
            return carry

        lax.fori_loop(0, D // ROWS, run, 0)
        put(raw, 0, whole[0], core)

    attend_back(i, q, qT, k, kT, v, g, gT, lse, delta, dq, dk, dv)
    prepare(jnp.minimum(i + 1, PAIRS - 1), *turned)
    gk[...] = dk[i]
    gv[...] = dv[i]

    @pl.when(i == PAIRS - 1)
    def _():
        wait(*mem, n2, mid, gl, att)
        gain2[...] = jnp.zeros_like(gain2)

        def leave(rows):
            part, gain_part = norm_back(mid.ref[rows, :], gains[1:2, :], dot(joined(dq, rows), w[1], 1, 1))
            gain2[...] += gain_part
            total = gl.ref[rows, :] + part
            gm.ref[rows, :] = total
            b1.ref[rows, :] = total.astype(BF)
            for one in (gm, b1):
                one.copy(rows.start // ROWS).start()

        each_block(bt.shape[0], ROWS, leave)
        n, r = dq.shape[1], dk.shape[1]
        turn_pairs(leftT.at[:, 0:n], n2.ref)
        products(raw, 1, leftT.at[:, 0:n], (dq,), core, whole)
        at = 0
        for part in [m.ref[t] for m in mem for t in range(m.ref.shape[0])]:
            leftT[:, at : at + part.shape[0]] = part.T
            at += part.shape[0]
        products(raw, 2, leftT.at[:, 0:r], (dk, dv), core, whole)
        turn_pairs(leftT.at[:, 0:n], att.ref)

        def run(b, carry):
            rows = pl.ds(pl.multiple_of(b * ROWS, ROWS), ROWS)
            whole[4, rows, :] = dot(leftT[rows, 0:n], b1.ref[...]).astype(BF)
            return carry

        lax.fori_loop(0, D // ROWS, run, 0)
        put(raw, 4, whole[4], core)
        for one in (gm, b1):
            one.finish()


def memory_back(me, gk, gv, g2, outs, w):
    build(w, 0, g2[0], 0, me[0])
    build(w, 1, g2[1], 0, me[0])
    back = (dot(gk[...], w[0], 1, 1) + dot(gv[...], w[1], 1, 1)).astype(BF)
    if len(outs) == 1:
        outs[0][...] = back
        return
    size = back.shape[0] // 4
    parts = [back[size * t : size * (t + 1)] for t in range(4)]
    outs[0][...], outs[1][...] = parts[0], parts[1]
    outs[2][0], outs[2][1] = parts[2], parts[3]


def self_back(
    me, b1, att, late_q, late_k, late_v, lse, n1, g1, g2, x, emb, gm, gains, sig, gain2, gain3,
    raw, grad, outs,
    w, qT, kT, g, gT, delta, dq, dk, dv, whole, leftT, sums,
):
    i = pl.program_id(0)
    core = me[0] % 2
    q, k, v = late_q.ref, late_k.ref, late_v.ref
    turned = (q, k, g, att, qT, kT, gT, delta)

    @pl.when(i == 0)
    def _():
        fetch(late_q, late_k, late_v, n1, x, gm, *g1)
        build(w, 0, g2, 0, me[0])
        start_back(b1, w.at[0], g)
        wait(late_q, late_k, late_v)
        prepare(0, *turned)

    attend_back(i, q, qT, k, kT, v, g, gT, lse, delta, dq, dk, dv)
    prepare(jnp.minimum(i + 1, PAIRS - 1), *turned)

    @pl.when(i == PAIRS - 1)
    def _():
        wait(n1, x, gm, *g1)
        for t in range(1, 4):
            build(w, t, [one.ref for one in g1], t, me[0])
        sums[...] = jnp.zeros_like(sums)

        def leave(rows):
            parts = (joined(dq, rows), joined(dk, rows), joined(dv, rows))
            back = sum(dot(part, w[t + 1], 1, 1) for t, part in enumerate(parts))
            resid = x.ref[rows, :].astype(F32) + emb[...]
            part, gain_part = norm_back(resid, gains[0:1, :], back)
            total = gm.ref[rows, :] + part
            grad.ref[rows, :] = total.astype(BF)
            grad.copy(rows.start // ROWS).start()
            sums[0:1, :] += jnp.sum(total, axis=0, keepdims=True)
            sums[1:2, :] += gain_part

        each_block(b1.shape[0], ROWS, leave)
        turn_pairs(leftT, n1.ref)
        products(raw, 0, leftT, (dq, dk, dv), core, whole)
        small_rows(outs, [sums[0:1, :], sig[0:1, :].astype(F32), sums[1:2, :], gain2[...], gain3[...]])
        grad.finish()


SMALL = 32


def small_rows(outs, rows):
    if outs.shape[1] == D:
        for t, row in enumerate(rows):
            outs[t : t + 1, :] = row
        outs[5:8, :] = jnp.zeros((3, D), F32)
        return
    tile = jnp.concatenate([row[:, 128 * c : 128 * (c + 1)] for row in rows for c in range(D // 128)], axis=0)
    outs[...] = jnp.concatenate([tile, jnp.zeros((SMALL - tile.shape[0], 128), F32)], axis=0).astype(BF)


def pack(me, *refs):
    out = refs[-1]
    rows = out.shape[1]
    at = 0
    for ref in refs[:-1]:
        for c in range(ref.shape[1] // D):
            for r in range(ref.shape[0] // rows):
                out[at] = ref[rows * r : rows * (r + 1), D * c : D * (c + 1)]
                at += 1


def add_core(me, keep, got, outs):
    place = me[0] // 2
    for r, out in enumerate(outs):
        out[...] = keep[r ^ place] + got[r ^ place]


def add_core_small(me, keep, got, mine, other, *outs):
    place = me[0] // 2
    cb, size, cols = keep.shape[1:]
    a, b = mine[...].astype(F32), other[...].astype(F32)
    small = jnp.concatenate([a[0:4], b[0:4], a[4:8], b[4:8], a[8:20] + b[8:20], a[28:32]], axis=0).astype(BF)
    for r, out in enumerate(outs):
        out[0 : cb * size, :] = (keep[r ^ place] + got[r ^ place]).reshape(cb * size, cols)
        out[cb * size :, :] = small


def add_plane(me, parts, *outs):
    size = outs[0].shape[0] - SMALL
    cb = (parts[0].shape[0] - SMALL) // size
    small = [p[cb * size :, :].astype(F32) for p in parts]
    gains = small[0][16:28] + small[1][16:28] + small[2][16:28] + small[3][16:28]
    line = lax.broadcasted_iota(jnp.int32, (4, 128), 0)

    def pick(rows, which):
        return jnp.sum(jnp.where(line == which, rows, 0.0), axis=0, keepdims=True)

    signals = []
    for p in small:
        for core in range(2):
            row = pick(p[8 + 4 * core : 12 + 4 * core], me[0] // 2)
            turned = jnp.concatenate([row[:, 64:], row[:, :64]], axis=1)
            signals.append(jnp.where(me[0] % 2 == 1, turned, row))
    for r, out in enumerate(outs):
        at = r ^ me[1]
        spot = pl.ds(pl.multiple_of(at * size, size), size)
        total = sum(p[spot, :].astype(F32) for p in parts)
        out[0:size, :] = total.astype(BF)
        sums = [pick(p[4 * core : 4 * (core + 1)], at) for p in small for core in range(2)]
        rows = jnp.concatenate(sums + signals + [gains, jnp.zeros((4, 128), F32)], axis=0)
        out[size:, :] = rows.astype(BF)


def add_four(me, parts, keep, send):
    for r in range(4):
        at = r ^ me[1]
        total = sum(p[at].astype(F32) for p in parts).astype(BF)
        if r < 2:
            keep[r] = total
        else:
            send[r - 2] = total


def add_pair(me, keep, got, own, send):
    own[...] = keep[0] + got[0]
    send[...] = keep[1] + got[1]


def fold(v):
    return jnp.sum((v * v).reshape(-1, 8, v.shape[-1]), axis=0)


def add_all(me, attn, cross, feed, done1, done2, d_time, d_gains, squares):
    size = done1.shape[0]
    total1 = sum(p[0:size, :].astype(F32) for p in attn)
    done1[...] = total1
    total2 = sum(p[...].astype(F32) for p in cross)
    done2[...] = total2
    small = [p[size:, :].astype(F32) for p in attn]
    sums = jnp.concatenate([p[0:8] for p in small], axis=0).astype(BF)
    signals = jnp.concatenate([p[8:16] for p in small], axis=0).astype(BF)
    rows = d_time.shape[0]
    of_time = dot(signals, sums, 0, 0)[0:rows, :]
    d_time[...] = of_time
    gains = small[0][16:28] + small[1][16:28] + small[2][16:28] + small[3][16:28]
    line = lax.broadcasted_iota(jnp.int32, (4, 128), 0)
    lane = lax.broadcasted_iota(jnp.int32, (1, 128), 1)
    mine = []
    for t in range(3):
        row = jnp.sum(jnp.where(line == me[0] // 2, gains[4 * t : 4 * (t + 1)], 0.0), axis=0, keepdims=True)
        row = jnp.where(me[0] % 2 == 1, jnp.concatenate([row[:, 64:], row[:, :64]], axis=1), row)
        mine.append(jnp.where(lane < 64, row, 0.0))
    block = jnp.concatenate(mine + [jnp.zeros((5, 128), F32)], axis=0)
    d_gains[...] = block[0:8, :]
    wide = feed[...].astype(F32)
    squares[...] = fold(total1) + fold(total2) + fold(wide) + fold(of_time) + fold(block) * 0.25


def take(me, src, keep, send):
    for t in range(2):
        keep[t] = src[(2 * t) ^ me[1]]
        send[t] = src[(2 * t + 1) ^ me[1]]


def join(me, first, second, out):
    out[0] = first[...] if len(first.shape) == 2 else first[1]
    out[1] = second[1]


def place_rows(me, own, across, near, out):
    out[me[1]] = own[...]
    out[2 ^ me[1]] = across[0]
    out[1 ^ me[1]] = near[0]
    out[3 ^ me[1]] = near[1]


def scale_all(me, s0, s1, s2, s3, d_time, d_gains, a1, a2, a3, own, across, near, placed, *outs):
    place_rows(me, own, across, near, placed)
    squares = jnp.sum(s0[...] + s1[...] + s2[...] + s3[...])
    limit = math.sqrt(9 * D * D + 2 * D * FF + 3 * D)
    factor = jnp.minimum(1.0, limit * lax.rsqrt(jnp.full((8, 128), squares, F32)))[0:1, :]
    o_time, o_q, o_k, o_v, o_out, o_cq, o_ck, o_cv, o_cout, o_in, o_fout, o_gains = outs
    o_time[...] = d_time[...] * factor
    rows = d_time.shape[0]
    for src, dsts in ((a1, (o_q, o_k, o_v)), (a2, (o_cout, o_cq, o_ck, o_cv, o_out))):
        for t, dst in enumerate(dsts):
            dst[...] = src[rows * t : rows * (t + 1), :] * factor
    for t in range(CHUNKS):
        o_in[:, 128 * t : 128 * (t + 1)] = a3[rows * t : rows * (t + 1), :].astype(F32) * factor
    o_fout[...] = a3[rows * CHUNKS :, :].astype(F32) * factor
    o_gains[...] = (d_gains[...] * factor)[0:3, 0 : o_gains.shape[1]]


class Late:
    def __init__(self, src, dst, sems):
        self.src, self.ref, self.sems = src, dst, sems

    def copies(self):
        count = self.sems.shape[0]
        if count == 1:
            whole = pl.ds(0, self.ref.shape[0])
            return [pltpu.make_async_copy(self.src.at[whole], self.ref, self.sems.at[0])]
        return [pltpu.make_async_copy(self.src.at[p], self.ref.at[p], self.sems.at[p]) for p in range(count)]


class Early:
    def __init__(self, src, dst, sems):
        self.ref, self.dst, self.sems = src, dst, sems

    def copy(self, b):
        rows = pl.ds(pl.multiple_of(b * ROWS, ROWS), ROWS)
        return pltpu.make_async_copy(self.ref.at[rows, :], self.dst.at[rows, :], self.sems.at[b])

    def finish(self):
        for b in range(self.sems.shape[0]):
            self.copy(b).wait()


def fetch(*operands):
    for one in operands:
        for copy in one.copies():
            copy.start()


def wait(*operands):
    for one in operands:
        for copy in one.copies():
            copy.wait()


def late(array, parts=1, first=None):
    return (array, None, parts, first or array.shape[0])


EARLY = "early"


def full(shape):
    return pl.BlockSpec(shape, lambda i: (0,) * len(shape), pipeline_mode=pl.Buffered(1))


def call(body, name, args, outs, scratch=(), steps=1, flops=0, limit=48, hbm=False, free=()):
    in_specs = [pl.BlockSpec(memory_space=pltpu.SMEM)]
    arrays = [args[0]]
    groups = [None]

    later = []

    def take_in(a):
        if isinstance(a, tuple) and a[1] is None:
            later.append((len(arrays), a[2], a[3]))
            arrays.append(a[0])
            in_specs.append(pl.BlockSpec(memory_space=pl.ANY))
        elif isinstance(a, tuple):
            arrays.append(a[0])
            in_specs.append(a[1])
        else:
            arrays.append(a)
            in_specs.append(full(a.shape))

    for a in args[1:]:
        nested = isinstance(a, list) and isinstance(a[0], list)
        groups.append([len(b) for b in a] if nested else len(a) if isinstance(a, list) else None)
        for one in sum(a, []) if nested else a if isinstance(a, list) else [a]:
            take_in(one)
    flat = []
    out_groups = []
    for o in outs:
        out_groups.append(len(o) if isinstance(o, list) else None)
        flat += o if isinstance(o, list) else [o]

    early = [k for k, o in enumerate(flat) if o[2] is EARLY]

    def grouped(refs, sizes):
        got, at = [], 0
        for size in sizes:
            if isinstance(size, list):
                got.append(grouped(refs[at : at + sum(size)], size))
                at += sum(size)
            else:
                got.append(refs[at] if size is None else list(refs[at : at + size]))
                at += size or 1
        return got

    def run(*refs):
        n_in, n_out = len(arrays), len(flat)
        refs = list(refs)
        for k in reversed(early):
            sems, held = refs.pop(), refs.pop()
            refs[n_in + k] = Early(held, refs[n_in + k], sems)
        for k, _, _ in reversed(later):
            sems, held = refs.pop(), refs.pop()
            refs[k] = Late(refs[k], held, sems)
        body(
            *grouped(refs[:n_in], groups), *grouped(refs[n_in : n_in + n_out], out_groups), *refs[n_in + n_out :]
        )

    if hbm or body in (pack, take):
        arrays = [
            pltpu.with_memory_space_constraint(a, pltpu.HBM) if math.prod(a.shape) >= 2**14 else a for a in arrays
        ]
    made = lambda s, t, k: (
        pltpu.HBM(s, t) if hbm and math.prod(s) >= 2**14 and k not in free else jax.ShapeDtypeStruct(s, t)
    )
    size = sum(math.prod(a.shape) * a.dtype.itemsize for a in arrays)
    size += sum(math.prod(s) * jnp.dtype(t).itemsize for s, t, _ in flat)
    size = size if flops else 0
    got = pl.pallas_call(
        run,
        grid=(steps,),
        in_specs=in_specs,
        out_specs=tuple(
            full(s) if b is None else pl.BlockSpec(memory_space=pl.ANY) if b is EARLY else b for s, _, b in flat
        ),
        out_shape=tuple(made(s, t, k) for k, (s, t, _) in enumerate(flat)),
        scratch_shapes=list(scratch)
        + [
            one
            for k, parts, first in later
            for one in (pltpu.VMEM((first,) + arrays[k].shape[1:], arrays[k].dtype), pltpu.SemaphoreType.DMA((parts,)))
        ]
        + [
            one
            for k in early
            for one in (pltpu.VMEM(flat[k][0], flat[k][1]), pltpu.SemaphoreType.DMA((flat[k][0][0] // ROWS,)))
        ],
        compiler_params=pltpu.CompilerParams(vmem_limit_bytes=limit * 2**20),
        cost_estimate=pl.CostEstimate(flops=int(flops), bytes_accessed=size, transcendentals=0),
        name=name,
    )(*arrays)
    return grouped(got, out_groups)


def step_signal(step_ids, feat_width):
    half_width = feat_width // 2
    frequency = jnp.exp(-math.log(10000.0) * jnp.arange(half_width, dtype=F32) / half_width)
    angles = step_ids.astype(F32)[:, None] * frequency[None, :]
    return jnp.concatenate([jnp.sin(angles), jnp.cos(angles)], axis=1)


def sds(shape, dtype=BF, block=None):
    return (tuple(shape), dtype, block)


def per_device(
    decoder_input, timesteps, memory, cotangent, time_weight, attn_query, attn_key, attn_value, attn_out,
    cross_query, cross_key, cross_value, cross_out, ffn_in, ffn_out, norm_gains,
):
    dp = lax.axis_size("dp")
    mem_count = lax.axis_size("mem")
    rows = D // dp
    cols = D // mem_count
    by_hand = dp == 8 and mem_count == 4
    x = decoder_input[0]
    cot = cotangent[0]
    n = x.shape[0]
    r = memory.shape[0] * memory.shape[1]
    gains = norm_gains.T
    my_dp, my_mem = lax.axis_index("dp"), lax.axis_index("mem")
    me = jnp.stack([my_dp, my_mem]).astype(jnp.int32)

    def to(value, axis, bit):
        size = lax.axis_size(axis)
        return lax.ppermute(value, axis, [(i, i ^ bit) for i in range(size)])

    def after(value, *others):
        return lax.optimization_barrier((value,) + others)[0]

    def plane(own):
        return [own] + [to(own, "dp", 2 * bit) for bit in (1, 2, 3)]

    def swap(parts):
        both = []
        for part in parts:
            both += [part, to(part, "dp", 1)]
        return both

    in_parts = [ffn_in[:, D * c : D * (c + 1)] for c in range(CHUNKS)]
    if by_hand:
        first = (time_weight, attn_query, attn_key, attn_value)
        second = (attn_out, cross_query, cross_key, cross_value, cross_out)
        (own1,) = call(pack, "pack_one", (me,) + first, [sds((4, rows, D))], limit=4)
        plane1 = plane(own1)
        mem_keep, mem_send = call(
            take, "take_memory", (me, after(memory, own1)), [sds((2,) + memory.shape[1:])] * 2, limit=8
        )
        (own2,) = call(pack, "pack_two", (me,) + second, [sds((5, rows, D))], limit=4)
        (own3,) = call(pack, "pack_three", (me, ffn_in, ffn_out), [sds((2 * CHUNKS, rows, D))], limit=8)
        near = to(mem_send, "mem", 1)
        *plane1, near, own2, own3 = lax.optimization_barrier(tuple(plane1[1:]) + (near, own2, own3))
        (passed,) = call(join, "join_memory", (me, mem_keep, near), [sds(mem_keep.shape)], limit=8)
        across = to(passed, "mem", 2)
        g1 = [own1, to(own1, "dp", 1)]
        for part in plane1:
            g1 += [part, to(part, "dp", 1)]
        mem_rows = [late(mem_keep, 1, 1), late(near, 1, 1), late(across)]
        own2 = after(own2, *g1)
        g2 = plane(own2)
        g3 = lax.all_gather(own3, "dp", axis=0, tiled=False)
    else:

        def gather(parts):
            got = lax.all_gather(jnp.stack(parts, 0), "dp", axis=0, tiled=False)
            return got.transpose(1, 0, 2, 3).reshape(1, len(parts), D, D)

        g1 = [gather((time_weight, attn_query, attn_key, attn_value))]
        g2 = [gather((attn_out, cross_query, cross_key, cross_value, cross_out))]
        whole_out = lax.all_gather(ffn_out, "dp", axis=0, tiled=True).reshape(1, CHUNKS, D, D)
        g3 = jnp.concatenate([gather(in_parts), whole_out], axis=1)
        mem_rows = [late(lax.all_to_all(memory, "mem", split_axis=0, concat_axis=1, tiled=True))]
    signal = step_signal(timesteps, D).astype(BF)
    sig = jnp.broadcast_to(signal, (8, D))

    nat = pl.BlockSpec((n, PAIR), lambda i: (0, i))
    paired = lambda m: sds((PAIRS, m, PAIR), BF, pl.BlockSpec((1, m, PAIR), lambda i: (i, 0, 0)))
    nat_r = pl.BlockSpec((r, PAIR), lambda i: (0, i))
    rows2 = pl.BlockSpec((1, 2, n), lambda i: (i, 0, 0))
    wide = lambda m: pltpu.VMEM((PAIRS, m, PAIR), BF)
    tall = lambda m: pltpu.VMEM((PAIRS, PAIR, m), BF)
    weight = pltpu.VMEM((D, D), BF)
    weights = lambda count: pltpu.VMEM((count, D, D), BF)
    proj = 2 * n * D * D * 1.5
    att_cost = 2 * n * r * D * 5
    lse_out = sds((PAIRS, 2, n), F32, rows2)
    emb, n1, q, k, v, lse1, attended = call(
        self_forward, "self_forward", (me, x, sig, gains, g1),
        [sds((1, D), F32)] + [paired(n)] * 4 + [lse_out, paired(n)],
        [weights(4), wide(n), wide(n), wide(n), wide(n), tall(n), tall(n), tall(n), pltpu.SMEM((PAIRS,), jnp.int32)],
        PAIRS, 3 * proj + 2 * att_cost, 36, True,
    )
    if by_hand:
        attended, *g2 = lax.optimization_barrier((attended,) + tuple(g2))
        g2 = swap(g2)
    mid, n2, cq, ck, cv, lse2, crossed = call(
        cross_forward, "cross_forward", (me, x, emb, attended, mem_rows, gains, g2),
        [sds((n, D), F32, nat)] + [paired(n)] * 2 + [paired(r)] * 2 + [lse_out, paired(n)],
        [weights(4), pltpu.VMEM((PAIRS, n, PAIR), F32), wide(n), wide(n), wide(r), wide(r), tall(n), tall(r), tall(n),
         pltpu.SMEM((PAIRS,), jnp.int32)],
        PAIRS, 4 * proj + 2 * att_cost, 42, True,
    )
    if by_hand:
        weight_of = lambda t: [(p, pl.BlockSpec((1, rows, D), lambda i: (t, 0, 0))) for p in g2]
        raw_of = lambda count: [sds((dp // 2, mem_count, count * rows, cols))] * 2
        raw3_of = sds((dp, mem_count, 2 * CHUNKS * rows, cols))
    else:
        weight_of = lambda t: [(g2[0], pl.BlockSpec((1, 1, D, D), lambda i: (0, t, 0, 0)))]
        raw_of = lambda count: [sds((count, D, D))]
        raw3_of = sds((2 * CHUNKS, D, D))
    out, gl, bt, gain3, raw3 = call(
        feed_forward, "feed_forward", (me, mid, crossed, late(cot), gains, weight_of(4), late(g3)),
        [sds((n, D), BF, EARLY), sds((n, D), F32, EARLY), sds((n, D), BF, EARLY), sds((1, D), F32), sds(*raw3_of[:2], pl.BlockSpec(memory_space=pl.ANY))],
        [weights(1), weight, weight, pltpu.VMEM((n, D), BF), pltpu.VMEM((D, n), BF)] + [pltpu.VMEM((n, D), F32)] * 3
        + [pltpu.VMEM((2, n, D), BF)] * 2 + [pltpu.VMEM(raw3_of[0], BF), pltpu.SemaphoreType.DMA((CHUNKS, 2))],
        CHUNKS + 1, 25 * proj, 44, True,
    )
    back_scratch = lambda m, mats: [
        weights(mats), tall(n), tall(m), wide(n), tall(n), pltpu.VMEM((PAIRS, 2, n), F32),
        wide(n), wide(m), wide(m), weights(5), pltpu.VMEM((D, max(n, m)), BF),
    ]
    raw2, gm, b1, gain2, gk, gv = call(
        cross_back, "cross_back",
        (me, bt, crossed, late(cq), late(ck), late(cv), (lse2, rows2), mem_rows, late(n2), late(mid), late(gl), gains,
         weight_of(4), weight_of(1), late(attended)),
        [raw_of(5), sds((n, D), F32, EARLY), sds((n, D), BF, EARLY), sds((1, D), F32), sds((r, D), BF, nat_r),
         sds((r, D), BF, nat_r)],
        back_scratch(r, 2), PAIRS, 8 * proj + 5 * att_cost, 56, True,
    )
    if by_hand:
        got2 = to(raw2[1], "dp", 1)
        grad_of = [sds(memory.shape[1:]), sds(memory.shape[1:]), sds((2,) + memory.shape[1:])]
    else:
        grad_of = [sds((r, D))]
    (mem_grad,) = call(
        memory_back, "memory_back", (me, gk, gv, [weight_of(2), weight_of(3)]), [grad_of], [weights(2)], 1, 0, 32, True,
    )
    if by_hand:
        got2 = after(got2, mem_grad[2])
        (parts2,) = call(add_core, "cross_core", (me, raw2[0], got2), [[sds((mem_count, 5 * rows, cols))] * 4], limit=24)
        b1, mem_grad[2], *parts2 = lax.optimization_barrier((b1, mem_grad[2]) + tuple(parts2))
        parts2 = [parts2[0]] + [to(parts2[b], "dp", 2 * b) for b in (1, 2, 3)]
        across = to(mem_grad[2], "mem", 2)
    raw1, input_grad, sums = call(
        self_back, "self_back",
        (me, b1, attended, late(q), late(k), late(v), (lse1, rows2), late(n1), [late(p) for p in g1], weight_of(0),
         late(x), emb, late(gm), gains, sig, gain2, gain3),
        [raw_of(3), sds((n, D), BF, EARLY), sds((SMALL, 128)) if by_hand else sds((8, D), F32)],
        back_scratch(n, 4) + [pltpu.VMEM((2, D), F32)], PAIRS, 7 * proj + 5 * att_cost, 50, True,
    )
    if by_hand:
        two = sds((2, 5 * rows, cols))
        keep, send = raw1
        got1, small1 = to(send, "dp", 1), to(sums, "dp", 1)
        done3 = lax.psum_scatter(raw3, "dp", scatter_dimension=0, tiled=False)
        done3 = lax.psum_scatter(done3, "mem", scatter_dimension=0, tiled=False)
        done3 = pltpu.with_memory_space_constraint(done3, pltpu.HBM)
        sums, *parts2 = lax.optimization_barrier((sums,) + tuple(parts2))
        keep2, send2 = call(add_four, "cross_plane", (me, parts2), [two, two], limit=24, hbm=True, free=(0, 1))
        (passed,) = call(join, "join_grad", (me, mem_grad[1], after(across, keep2)), [sds(across.shape)], limit=8, flops=6e9)
        sums, keep, keep2, send2, passed = lax.optimization_barrier((sums, keep, keep2, send2, passed))
        across2 = to(send2, "mem", 2)

    limit = math.sqrt(9 * D * D + 2 * D * FF + 3 * D)
    if not by_hand:
        memory_grad = lax.all_to_all(mem_grad[0][None], "mem", split_axis=1, concat_axis=0, tiled=True)

        def scatter(raw):
            part = lax.psum_scatter(raw, "dp", scatter_dimension=1, tiled=True)
            part = lax.psum_scatter(part, "mem", scatter_dimension=2, tiled=True)
            return [part[t].astype(F32) for t in range(raw.shape[0])]

        d_in = scatter(raw3[:CHUNKS].transpose(1, 0, 2).reshape(1, D, FF))[0]
        d_fout = scatter(raw3[CHUNKS:].reshape(1, FF, D))[0]
        d_query, d_key, d_value = scatter(raw1[0])
        d_cout, d_cquery, d_ckey, d_cvalue, d_out = scatter(raw2[0])
        everyone = lax.all_gather(sums, ("dp", "mem"), axis=0, tiled=False)
        my_signal = lax.dynamic_slice_in_dim(everyone[:, 1], my_dp * rows, rows, axis=1)
        my_sums = lax.dynamic_slice_in_dim(everyone[:, 0], my_mem * cols, cols, axis=1)
        d_time = jnp.dot(my_signal.T, my_sums, precision=lax.Precision.HIGHEST)
        all_gains = jnp.sum(everyone[:, 2:5], axis=0)
        d_gains = lax.dynamic_slice_in_dim(all_gains, my_dp * rows, rows, axis=1).T
        weights = [d_time, d_query, d_key, d_value, d_out, d_cquery, d_ckey, d_cvalue, d_cout, d_in, d_fout]
        local = sum(jnp.sum(w * w) for w in weights)
        squares = lax.psum(local, ("dp", "mem")) + jnp.sum(all_gains * all_gains)
        factor = jnp.minimum(1.0, limit * lax.rsqrt(squares))
        return (
            (out[None], input_grad[None], memory_grad) + tuple(w * factor for w in weights) + (d_gains * factor,)
        )

    parts1 = call(
        add_core_small, "attn_core", (me, keep, got1, sums, small1),
        [sds((mem_count * 3 * rows + SMALL, cols))] * 4, limit=16,
    )
    parts1 = [parts1[0]] + [to(parts1[b], "dp", 2 * b) for b in (1, 2, 3)]
    parts1 = call(add_plane, "attn_plane", (me, parts1), [sds((3 * rows + SMALL, cols))] * mem_count, limit=16)
    one = sds((5 * rows, cols))
    keep2, send2 = call(add_pair, "cross_across", (me, keep2, after(across2, parts1[0])), [one, one], limit=8)
    parts1 = [parts1[0]] + [to(parts1[b], "mem", b) for b in (1, 2, 3)]
    parts2 = [keep2, to(send2, "mem", 1)]
    done1, done2, d_time, d_gains, local = call(
        add_all, "add_all", (me, parts1, parts2, done3),
        [sds((3 * rows, cols), F32), sds((5 * rows, cols), F32), sds((rows, cols), F32), sds((8, cols), F32),
         sds((8, cols), F32)],
        limit=16,
    )
    near = to(after(passed, local), "mem", 1)
    local = local + to(local, "dp", 1)
    local = local + to(local, "dp", 2) + to(local, "dp", 4) + to(local, "dp", 6)
    planes = [local] + [to(local, "mem", b) for b in (1, 2, 3)]
    shapes = [(rows, cols)] * 9 + [(rows, FF // mem_count), (FF // dp, cols), (3, rows)]
    memory_grad, *scaled = call(
        scale_all, "scale_all", [me] + planes + [d_time, d_gains, done1, done2, done3, mem_grad[0], across, near],
        [sds(memory.shape)] + [sds(s, F32) for s in shapes], limit=20,
    )
    return (out[None], input_grad[None], memory_grad) + tuple(scaled[:-1]) + (scaled[-1].T,)


def solution(mesh):
    tokens = P(("dp", "mem"), None, None)
    weight = P("dp", None)
    in_specs = (tokens, P(("dp", "mem")), P("dp", "mem", None), tokens) + (weight,) * 11 + (P(),)
    out_specs = (tokens, tokens, P("dp", "mem", None)) + (P("dp", "mem"),) * 11 + (P("dp", None),)
    return jax.shard_map(per_device, mesh=mesh, in_specs=in_specs, out_specs=out_specs, check_vma=False)
```

```python
import functools
import math

import jax
import jax.numpy as jnp
from jax import lax
from jax.experimental import pallas as pl
from jax.experimental.pallas import tpu as pltpu
from jax.sharding import PartitionSpec as P

D = 512
HEADS = 8
HEAD = 64
FF = 2048
PAIRS = HEADS // 2
PAIR = 2 * HEAD
CHUNKS = FF // D
BF = jnp.bfloat16
F32 = jnp.float32
SCALE = 1.0 / math.sqrt(HEAD)
ROOT_HALF = math.sqrt(0.5)
BELL = 1.0 / math.sqrt(2.0 * math.pi)


def dot(a, b, ca=1, cb=0):
    return lax.dot_general(a, b, (((ca,), (cb,)), ((), ())), preferred_element_type=F32)


def row_mean(v):
    return jnp.sum(v, axis=-1, keepdims=True) * (1.0 / v.shape[-1])


def norm_parts(v):
    centred = v - row_mean(v)
    scale = lax.rsqrt(row_mean(centred * centred) + 1e-05)
    return centred * scale, scale


def norm_back(v, gain, grad):
    normed, scale = norm_parts(v)
    c = grad * gain
    gain_part = jnp.sum(grad * normed, axis=0, keepdims=True)
    return scale * (c - row_mean(c) - normed * row_mean(c * normed)), gain_part


def build(w, slot, parts, which, me):
    dst = w.at[slot]
    if len(parts) == 1:
        blocks, _, rows, _ = parts[0].shape
        for b in range(blocks):
            dst[rows * b : rows * (b + 1), :] = parts[0][b, which]
        return
    rows = parts[0].shape[1]
    for r, part in enumerate(parts):
        lo = pl.multiple_of((r ^ me) * rows, rows)
        dst[pl.ds(lo, rows), :] = part[which]


def put(refs, at, mat, core):
    mat = mat.astype(refs[0].dtype)
    if len(refs) == 1:
        refs[0][at] = mat
        return
    half, cb, _, cols = refs[0].shape
    rows = D // (2 * half)

    def cut(own, other):
        for a in range(2 * half):
            ref = own if a % 2 == 0 else other
            for j in range(cb):
                ref[a // 2, j, rows * at : rows * (at + 1), :] = mat[
                    rows * a : rows * (a + 1), cols * j : cols * (j + 1)
                ]

    @pl.when(core == 0)
    def _():
        cut(refs[0], refs[1])

    @pl.when(core == 1)
    def _():
        cut(refs[1], refs[0])


ROWS = 512


def each_block(total, step, body):
    def run(b, carry):
        body(pl.ds(pl.multiple_of(b * step, step), step))
        return carry

    lax.fori_loop(0, total // step, run, 0)


SAFE = 1444.0


def judge(flags, qT, k):
    line = lax.broadcasted_iota(jnp.int32, (8, PAIR), 0)
    lane = lax.broadcasted_iota(jnp.int32, (8, PAIR), 1)
    mine = jnp.where((lane // HEAD) == line, 1.0, 0.0).astype(BF)
    for p in range(PAIRS):
        of_q = jnp.max(dot(mine, qT[p] * qT[p]), axis=1, keepdims=True)
        of_k = jnp.max(dot(mine, k[p] * k[p], 1, 1), axis=1, keepdims=True)
        flags[p] = jnp.where(jnp.max(of_q * of_k) <= SAFE, 1, 0)


def attend(i, flags, qT, k, vT, oT, lse):
    n = qT.shape[2]
    row = lax.broadcasted_iota(jnp.int32, (PAIR, n), 0)
    zero = jnp.zeros((), BF)

    def run(shifted):
        scores = [dot(k[i], jnp.where((row // HEAD) == h, qT[i], zero)) for h in range(2)]
        for h in range(2):
            own = slice(HEAD * h, HEAD * (h + 1))
            score = scores[h]
            top = jnp.max(score, axis=0, keepdims=True) if shifted else None
            e = jnp.exp(score - top if shifted else score)
            total = jnp.sum(e, axis=0, keepdims=True)
            out = dot(vT[i, own, :], e.astype(BF))
            oT[i, own, :] = (out * (1.0 / total)).astype(BF)
            lse[0, h : h + 1, :] = top + jnp.log(total) if shifted else jnp.log(total)

    @pl.when(flags[i] == 1)
    def _():
        run(False)

    @pl.when(flags[i] == 0)
    def _():
        run(True)


def attend_back(i, q, qT, k, kT, v, g, gT, lse, delta, dq, dk, dv):
    n = qT.shape[2]
    block = min(n, 512)
    row = lax.broadcasted_iota(jnp.int32, (PAIR, block), 0)
    lane = lax.broadcasted_iota(jnp.int32, (block, PAIR), 1)
    zero = jnp.zeros((), BF)
    total_k = total_v = None
    for j in range(n // block):
        at = slice(j * block, (j + 1) * block)
        turned = []
        for h in range(2):
            own = slice(HEAD * h, HEAD * (h + 1))
            s = dot(k[i], jnp.where((row // HEAD) == h, qT[i, :, at], zero))
            dp = dot(v[i], jnp.where((row // HEAD) == h, gT[i, :, at], zero))
            p = jnp.exp(s - lse[0, h : h + 1, at])
            ds = (p * (dp - delta[i, h : h + 1, at])).astype(BF)
            one_v = dot(p.astype(BF), jnp.where((lane // HEAD) == h, g[i, at, :], zero))
            one_k = dot(ds, jnp.where((lane // HEAD) == h, q[i, at, :], zero))
            turned.append((dot(kT[i, own, :], ds) * SCALE).astype(BF))
            total_v = one_v if total_v is None else total_v + one_v
            total_k = one_k if total_k is None else total_k + one_k
        dq[i, at, :] = jnp.concatenate(turned, axis=0).T
    dk[i] = (total_k * SCALE).astype(BF)
    dv[i] = total_v.astype(BF)


def prepare(p, q, k, g, heads, qT, kT, gT, delta):
    qT[p] = q[p].T * jnp.asarray(SCALE, BF)
    kT[p] = k[p].T
    gT[p] = g[p].T
    both = gT[p].astype(F32) * heads[p].T.astype(F32)
    for h in range(2):
        delta[p, h : h + 1, :] = jnp.sum(both[HEAD * h : HEAD * (h + 1), :], axis=0, keepdims=True)


def products(refs, first, leftT, rights, core, whole):
    def run(b, carry):
        rows = pl.ds(pl.multiple_of(b * ROWS, ROWS), ROWS)
        for t, right in enumerate(rights):
            whole[first + t, rows, :] = dot(leftT[rows, :], from_pairs(right)).astype(BF)
        return carry

    lax.fori_loop(0, D // ROWS, run, 0)
    for t in range(len(rights)):
        put(refs, first + t, whole[first + t], core)


def turn_pairs(dst, src):
    for p in range(PAIRS):
        dst[PAIR * p : PAIR * (p + 1), :] = src[p].T


def pairs_at(dst, rows, src):
    for p in range(PAIRS):
        dst[p, rows, :] = src[:, PAIR * p : PAIR * (p + 1)]


def joined(src, rows):
    return jnp.concatenate([src[p, rows, :] for p in range(PAIRS)], axis=1)


def pairs_in(dst, src):
    for p in range(PAIRS):
        dst[p] = src[:, PAIR * p : PAIR * (p + 1)]


def from_pairs(src):
    return jnp.concatenate([src[p] for p in range(PAIRS)], axis=1)


def from_pairs_T(src):
    return jnp.concatenate([src[p].T for p in range(PAIRS)], axis=1)


def rows_of(mem):
    parts = [m[t] for m in mem for t in range(m.shape[0])]
    return jnp.concatenate(parts, axis=0) if len(parts) > 1 else parts[0]


def self_forward(me, x, sig, gains, g1, emb, n1, q, k, v, lse, att, held, w, n1s, qs, ks, vs, qT, vT, oT, flags):
    i = pl.program_id(0)

    @pl.when(i == 0)
    def _():
        build(w, 0, g1, 0, me[0])
        embedded = dot(sig[...], w[0])[0:1, :]
        emb[...] = embedded
        resid = x[...].astype(F32) + embedded
        normed = (norm_parts(resid)[0] * gains[0:1, :]).astype(BF)
        pairs_in(n1s, normed)
        for t, dst in ((1, qs), (2, ks), (3, vs)):
            build(w, t, g1, t, me[0])
            pairs_in(dst, dot(normed, w[t]).astype(BF))
        for p in range(PAIRS):
            qT[p] = qs[p].T * jnp.asarray(SCALE, BF)
            vT[p] = vs[p].T
        judge(flags, qT, ks)

    attend(i, flags, qT, ks, vT, oT, lse)
    held[0] = w[i]
    n1[0] = n1s[i]
    q[0] = qs[i]
    k[0] = ks[i]
    v[0] = vs[i]
    att[0] = oT[i].T


def cross_forward(
    me, x, emb, att, mem, gains, g2, mid, n2, cq, k, v, lse, crossed, held, w, mids, n2s, qs, ks, vs, qT, vT, oT, flags
):
    i = pl.program_id(0)

    @pl.when(i == 0)
    def _():
        fetch(*mem)
        build(w, 0, g2, 0, me[0])
        new = x[...].astype(F32) + emb[...] + dot(from_pairs(att), w[0])
        pairs_in(mids, new)
        normed = (norm_parts(new)[0] * gains[1:2, :]).astype(BF)
        pairs_in(n2s, normed)
        build(w, 1, g2, 1, me[0])
        pairs_in(qs, dot(normed, w[1]).astype(BF))
        wait(*mem)
        rows = rows_of([m.ref for m in mem])
        for t, dst in ((2, ks), (3, vs)):
            build(w, t, g2, t, me[0])
            pairs_in(dst, dot(rows, w[t]).astype(BF))
        for p in range(PAIRS):
            qT[p] = qs[p].T * jnp.asarray(SCALE, BF)
            vT[p] = vs[p].T
        judge(flags, qT, ks)

    attend(i, flags, qT, ks, vT, oT, lse)
    held[0] = w[i]
    mid[...] = mids[i]
    n2[0] = n2s[i]
    cq[0] = qs[i]
    k[0] = ks[i]
    v[0] = vs[i]
    crossed[0] = oT[i].T


def feed_forward(
    me, mid, crossed, cot, gains, g2, g3,
    out, gl, bt, gain3, raw_out_ref,
    wlate, win, wout, n3, n3T, late, acc, gacc, active, grad_inner, raw, sems,
):
    i = pl.program_id(0)
    blocks, _, rows, _ = g3.ref.shape
    n = mid.shape[0]
    each = max(blocks // CHUNKS, 1)
    now, before = i % 2, (i + 1) % 2
    piece = D // (n // 512)

    @pl.when(i == 0)
    def _():
        fetch(cot, g3)
        build(wlate, 0, g2, 0, me[0])

        def enter(at):
            new = mid[at, :] + dot(joined(crossed, at), wlate[0])
            late[at, :] = new
            normed = (norm_parts(new)[0] * gains[2:3, :]).astype(BF)
            n3[at, :] = normed
            n3T[:, at] = normed.T
            acc[at, :] = new
            gacc[at, :] = jnp.zeros((ROWS, D), F32)

        each_block(n, ROWS, enter)
        wait(cot, g3)

    @pl.when(i < CHUNKS)
    def _():
        for b in range(blocks):
            win[rows * b : rows * (b + 1), :] = g3.ref[b, i]
        if blocks == 1:
            wout[...] = g3.ref[0, CHUNKS + i]
        else:
            for u in range(each):
                for t in range(CHUNKS):
                    lo = rows * (CHUNKS * u + t)
                    wout[lo : lo + rows, :] = g3.ref[each * i + u, CHUNKS + t]

    def hidden(at):
        inner = dot(n3[at, :], win[...])
        grad_active = dot(cot.ref[at, :], wout[...], 1, 1)
        share = 0.5 * (1.0 + lax.erf(inner * ROOT_HALF))
        act = (inner * share).astype(BF)
        active[now, at, :] = act
        acc[at, :] += dot(act, wout[...])
        slope = share + inner * (jnp.exp(-0.5 * inner * inner) * BELL)
        grad = (slope * grad_active).astype(BF)
        grad_inner[now, at, :] = grad
        gacc[at, :] += dot(grad, win[...], 1, 1)

    def weights(b):
        c = i - 1
        at = pl.ds(pl.multiple_of(b * piece, piece), piece)
        raw_in = dot(n3T[at, :], grad_inner[before]).astype(BF)
        raw_out = dot(active[before, :, at], cot.ref[...], 0, 0).astype(BF)
        if blocks == 1:
            raw[c, at, :] = raw_in
            raw[CHUNKS + c, at, :] = raw_out
            return
        cols = D // CHUNKS
        for a in range(piece // rows):
            for t in range(CHUNKS):
                raw[(piece // rows) * b + a, c, rows * t : rows * (t + 1), :] = raw_in[
                    rows * a : rows * (a + 1), cols * t : cols * (t + 1)
                ]
        tall = D // each
        split = tall // piece
        lo = tall + (b % split) * piece
        for j in range(CHUNKS):
            raw[each * c + b // split, j, pl.ds(pl.multiple_of(lo, piece), piece), :] = raw_out[
                :, cols * j : cols * (j + 1)
            ]

    @pl.when(i == 0)
    def _():
        each_block(n, 512, hidden)

    @pl.when((i > 0) & (i < CHUNKS))
    def _():
        def both(b, carry):
            weights(b)
            hidden(pl.ds(pl.multiple_of(b * 512, 512), 512))
            return carry

        lax.fori_loop(0, n // 512, both, 0)

    @pl.when(i == CHUNKS)
    def _():
        def only(b, carry):
            weights(b)
            return carry

        lax.fori_loop(0, n // 512, only, 0)

    def copies(c):
        if blocks == 1:
            return [
                pltpu.make_async_copy(raw.at[at], raw_out_ref.at[at], sems.at[c, k])
                for k, at in enumerate((c, CHUNKS + c))
            ]
        tall = D // each
        first = (slice(None), c, pl.ds(0, tall))
        second = (pl.ds(each * c, each), slice(None), pl.ds(tall, tall))
        return [
            pltpu.make_async_copy(raw.at[at], raw_out_ref.at[at], sems.at[c, k])
            for k, at in enumerate((first, second))
        ]

    @pl.when(i > 0)
    def _():
        for copy in copies(i - 1):
            copy.start()

    @pl.when(i == CHUNKS)
    def _():
        gain3[...] = jnp.zeros_like(gain3)

        def leave(at):
            out.ref[at, :] = acc[at, :].astype(BF)
            part, gain_part = norm_back(late[at, :], gains[2:3, :], gacc[at, :])
            gain3[...] += gain_part
            total = cot.ref[at, :].astype(F32) + part
            gl.ref[at, :] = total
            bt.ref[at, :] = total.astype(BF)
            for one in (out, gl, bt):
                one.copy(at.start // ROWS).start()

        each_block(n, ROWS, leave)
        for one in (out, gl, bt):
            one.finish()
        for c in range(CHUNKS):
            for copy in copies(c):
                copy.wait()


def start_back(branch, weight, g):
    def enter(rows):
        pairs_at(g, rows, dot(branch[rows, :], weight[...], 1, 1).astype(BF))

    each_block(branch.shape[0], ROWS, enter)


def cross_back(
    me, bt, crossed, late_q, late_k, late_v, lse, mem, n2, mid, gl, gains, g2_out, w_query, att,
    raw, gm, b1, gain2, gk, gv,
    w, qT, kT, g, gT, delta, dq, dk, dv, whole, leftT,
):
    i = pl.program_id(0)
    core = me[0] % 2
    q, k, v = late_q.ref, late_k.ref, late_v.ref
    turned = (q, k, g, crossed, qT, kT, gT, delta)

    @pl.when(i == 0)
    def _():
        fetch(late_q, late_k, late_v)
        build(w, 0, g2_out, 0, me[0])
        start_back(bt, w.at[0], g)
        turn_pairs(leftT, crossed)
        wait(late_q, late_k, late_v)
        prepare(0, *turned)

        def run(b, carry):
            rows = pl.ds(pl.multiple_of(b * ROWS, ROWS), ROWS)
            whole[0, rows, :] = dot(leftT[rows, 0 : bt.shape[0]], bt[...]).astype(BF)
            return carry

        lax.fori_loop(0, D // ROWS, run, 0)
        put(raw, 0, whole[0], core)

    @pl.when(i == 1)
    def _():
        fetch(*mem, n2, mid, gl, att)

    attend_back(i, q, qT, k, kT, v, g, gT, lse, delta, dq, dk, dv)
    prepare(jnp.minimum(i + 1, PAIRS - 1), *turned)
    gk[...] = dk[i]
    gv[...] = dv[i]

    @pl.when(i == PAIRS - 1)
    def _():
        wait(*mem, n2, mid, gl, att)
        gain2[...] = jnp.zeros_like(gain2)

        def leave(rows):
            part, gain_part = norm_back(mid.ref[rows, :], gains[1:2, :], dot(joined(dq, rows), w_query[0], 1, 1))
            gain2[...] += gain_part
            total = gl.ref[rows, :] + part
            gm.ref[rows, :] = total
            b1.ref[rows, :] = total.astype(BF)
            for one in (gm, b1):
                one.copy(rows.start // ROWS).start()

        each_block(bt.shape[0], ROWS, leave)
        n, r = dq.shape[1], dk.shape[1]
        turn_pairs(leftT.at[:, 0:n], n2.ref)
        products(raw, 1, leftT.at[:, 0:n], (dq,), core, whole)
        at = 0
        for part in [m.ref[t] for m in mem for t in range(m.ref.shape[0])]:
            leftT[:, at : at + part.shape[0]] = part.T
            at += part.shape[0]
        products(raw, 2, leftT.at[:, 0:r], (dk, dv), core, whole)
        turn_pairs(leftT.at[:, 0:n], att.ref)

        def run(b, carry):
            rows = pl.ds(pl.multiple_of(b * ROWS, ROWS), ROWS)
            whole[4, rows, :] = dot(leftT[rows, 0:n], b1.ref[...]).astype(BF)
            return carry

        lax.fori_loop(0, D // ROWS, run, 0)
        put(raw, 4, whole[4], core)
        for one in (gm, b1):
            one.finish()


def memory_back(me, gk, gv, w_key, w_value, outs):
    back = (dot(gk[...], w_key[0], 1, 1) + dot(gv[...], w_value[0], 1, 1)).astype(BF)
    if len(outs) == 1:
        outs[0][...] = back
        return
    size = back.shape[0] // 4
    parts = [back[size * t : size * (t + 1)] for t in range(4)]
    outs[0][...], outs[1][...] = parts[0], parts[1]
    outs[2][0], outs[2][1] = parts[2], parts[3]


def self_back(
    me, b1, att, late_q, late_k, late_v, lse, n1, held, w_out, x, emb, gm, gains, sig, gain2, gain3,
    raw, grad, outs,
    qT, kT, g, gT, delta, dq, dk, dv, whole, leftT, sums,
):
    i = pl.program_id(0)
    core = me[0] % 2
    q, k, v = late_q.ref, late_k.ref, late_v.ref
    turned = (q, k, g, att, qT, kT, gT, delta)

    @pl.when(i == 0)
    def _():
        fetch(late_q, late_k, late_v)
        start_back(b1, w_out.at[0], g)
        wait(late_q, late_k, late_v)
        prepare(0, *turned)

    @pl.when(i == 1)
    def _():
        fetch(n1, x, gm, held)

    attend_back(i, q, qT, k, kT, v, g, gT, lse, delta, dq, dk, dv)
    prepare(jnp.minimum(i + 1, PAIRS - 1), *turned)

    @pl.when(i == PAIRS - 1)
    def _():
        wait(n1, x, gm, held)
        sums[...] = jnp.zeros_like(sums)

        def leave(rows):
            parts = (joined(dq, rows), joined(dk, rows), joined(dv, rows))
            back = sum(dot(part, held.ref[t + 1], 1, 1) for t, part in enumerate(parts))
            resid = x.ref[rows, :].astype(F32) + emb[...]
            part, gain_part = norm_back(resid, gains[0:1, :], back)
            total = gm.ref[rows, :] + part
            grad.ref[rows, :] = total.astype(BF)
            grad.copy(rows.start // ROWS).start()
            sums[0:1, :] += jnp.sum(total, axis=0, keepdims=True)
            sums[1:2, :] += gain_part

        each_block(b1.shape[0], ROWS, leave)
        turn_pairs(leftT, n1.ref)
        products(raw, 0, leftT, (dq, dk, dv), core, whole)
        small_rows(outs, [sums[0:1, :], sig[0:1, :].astype(F32), sums[1:2, :], gain2[...], gain3[...]])
        grad.finish()


SMALL = 32


def small_rows(outs, rows):
    if outs.shape[1] == D:
        for t, row in enumerate(rows):
            outs[t : t + 1, :] = row
        outs[5:8, :] = jnp.zeros((3, D), F32)
        return
    tile = jnp.concatenate([row[:, 128 * c : 128 * (c + 1)] for row in rows for c in range(D // 128)], axis=0)
    outs[...] = jnp.concatenate([tile, jnp.zeros((SMALL - tile.shape[0], 128), F32)], axis=0).astype(BF)


def pack(me, *refs):
    out = refs[-1]
    rows = out.shape[1]
    at = 0
    for ref in refs[:-1]:
        for c in range(ref.shape[1] // D):
            for r in range(ref.shape[0] // rows):
                out[at] = ref[rows * r : rows * (r + 1), D * c : D * (c + 1)]
                at += 1


def add_core(me, keep, got, outs):
    place = me[0] // 2
    for r, out in enumerate(outs):
        out[...] = keep[r ^ place] + got[r ^ place]


def add_core_small(me, keep, got, mine, other, *outs):
    place = me[0] // 2
    cb, size, cols = keep.shape[1:]
    a, b = mine[...].astype(F32), other[...].astype(F32)
    small = jnp.concatenate([a[0:4], b[0:4], a[4:8], b[4:8], a[8:20] + b[8:20], a[28:32]], axis=0).astype(BF)
    for r, out in enumerate(outs):
        out[0 : cb * size, :] = (keep[r ^ place] + got[r ^ place]).reshape(cb * size, cols)
        out[cb * size :, :] = small


def add_plane(me, parts, cross, *outs):
    more = cross[0].shape[1]
    size = outs[0].shape[0] - SMALL - more
    cb = (parts[0].shape[0] - SMALL) // size
    small = [p[cb * size :, :].astype(F32) for p in parts]
    gains = small[0][16:28] + small[1][16:28] + small[2][16:28] + small[3][16:28]
    line = lax.broadcasted_iota(jnp.int32, (4, 128), 0)

    def pick(rows, which):
        return jnp.sum(jnp.where(line == which, rows, 0.0), axis=0, keepdims=True)

    signals = []
    for p in small:
        for core in range(2):
            row = pick(p[8 + 4 * core : 12 + 4 * core], me[0] // 2)
            turned = jnp.concatenate([row[:, 64:], row[:, :64]], axis=1)
            signals.append(jnp.where(me[0] % 2 == 1, turned, row))
    for r, out in enumerate(outs):
        at = r ^ me[1]
        spot = pl.ds(pl.multiple_of(at * size, size), size)
        total = sum(p[spot, :].astype(F32) for p in parts)
        out[0:size, :] = total.astype(BF)
        out[size : size + more, :] = sum(p[at].astype(F32) for p in cross).astype(BF)
        sums = [pick(p[4 * core : 4 * (core + 1)], at) for p in small for core in range(2)]
        rows = jnp.concatenate(sums + signals + [gains, jnp.zeros((4, 128), F32)], axis=0)
        out[size + more :, :] = rows.astype(BF)


def fold(v):
    return jnp.sum((v * v).reshape(-1, 8, v.shape[-1]), axis=0)


def add_all(me, parts, feed, done1, done2, d_time, d_gains, squares):
    size, more = done1.shape[0], done2.shape[0]
    total1 = sum(p[0:size, :].astype(F32) for p in parts)
    done1[...] = total1
    total2 = sum(p[size : size + more, :].astype(F32) for p in parts)
    done2[...] = total2
    small = [p[size + more :, :].astype(F32) for p in parts]
    sums = jnp.concatenate([p[0:8] for p in small], axis=0).astype(BF)
    signals = jnp.concatenate([p[8:16] for p in small], axis=0).astype(BF)
    rows = d_time.shape[0]
    of_time = dot(signals, sums, 0, 0)[0:rows, :]
    d_time[...] = of_time
    gains = small[0][16:28] + small[1][16:28] + small[2][16:28] + small[3][16:28]
    line = lax.broadcasted_iota(jnp.int32, (4, 128), 0)
    lane = lax.broadcasted_iota(jnp.int32, (1, 128), 1)
    mine = []
    for t in range(3):
        row = jnp.sum(jnp.where(line == me[0] // 2, gains[4 * t : 4 * (t + 1)], 0.0), axis=0, keepdims=True)
        row = jnp.where(me[0] % 2 == 1, jnp.concatenate([row[:, 64:], row[:, :64]], axis=1), row)
        mine.append(jnp.where(lane < 64, row, 0.0))
    block = jnp.concatenate(mine + [jnp.zeros((5, 128), F32)], axis=0)
    d_gains[...] = block[0:8, :]
    wide = feed[...].astype(F32)
    squares[...] = fold(total1) + fold(total2) + fold(wide) + fold(of_time) + fold(block) * 0.25


def take(me, src, keep, send):
    for t in range(2):
        keep[t] = src[(2 * t) ^ me[1]]
        send[t] = src[(2 * t + 1) ^ me[1]]


def join(me, first, second, out):
    out[0] = first[...] if len(first.shape) == 2 else first[1]
    out[1] = second[1]


def place_rows(me, own, across, near, out):
    out[me[1]] = own[...]
    out[2 ^ me[1]] = across[0]
    out[1 ^ me[1]] = near[0]
    out[3 ^ me[1]] = near[1]


def scale_all(me, s0, s1, s2, s3, d_time, d_gains, a1, a2, a3, own, across, near, placed, *outs):
    place_rows(me, own, across, near, placed)
    squares = jnp.sum(s0[...] + s1[...] + s2[...] + s3[...])
    limit = math.sqrt(9 * D * D + 2 * D * FF + 3 * D)
    factor = jnp.minimum(1.0, limit * lax.rsqrt(jnp.full((8, 128), squares, F32)))[0:1, :]
    o_time, o_q, o_k, o_v, o_out, o_cq, o_ck, o_cv, o_cout, o_in, o_fout, o_gains = outs
    o_time[...] = d_time[...] * factor
    rows = d_time.shape[0]
    for src, dsts in ((a1, (o_q, o_k, o_v)), (a2, (o_cout, o_cq, o_ck, o_cv, o_out))):
        for t, dst in enumerate(dsts):
            dst[...] = src[rows * t : rows * (t + 1), :] * factor
    for t in range(CHUNKS):
        o_in[:, 128 * t : 128 * (t + 1)] = a3[rows * t : rows * (t + 1), :].astype(F32) * factor
    o_fout[...] = a3[rows * CHUNKS :, :].astype(F32) * factor
    o_gains[...] = (d_gains[...] * factor)[0:3, 0 : o_gains.shape[1]]


class Late:
    def __init__(self, src, dst, sems):
        self.src, self.ref, self.sems = src, dst, sems

    def copies(self):
        count = self.sems.shape[0]
        if count == 1:
            whole = pl.ds(0, self.ref.shape[0])
            return [pltpu.make_async_copy(self.src.at[whole], self.ref, self.sems.at[0])]
        return [pltpu.make_async_copy(self.src.at[p], self.ref.at[p], self.sems.at[p]) for p in range(count)]


class Early:
    def __init__(self, src, dst, sems):
        self.ref, self.dst, self.sems = src, dst, sems

    def copy(self, b):
        rows = pl.ds(pl.multiple_of(b * ROWS, ROWS), ROWS)
        return pltpu.make_async_copy(self.ref.at[rows, :], self.dst.at[rows, :], self.sems.at[b])

    def finish(self):
        for b in range(self.sems.shape[0]):
            self.copy(b).wait()


def fetch(*operands):
    for one in operands:
        for copy in one.copies():
            copy.start()


def wait(*operands):
    for one in operands:
        for copy in one.copies():
            copy.wait()


def late(array, parts=1, first=None):
    return (array, None, parts, first or array.shape[0])


EARLY = "early"


def full(shape):
    return pl.BlockSpec(shape, lambda i: (0,) * len(shape), pipeline_mode=pl.Buffered(1))


def call(body, name, args, outs, scratch=(), steps=1, flops=0, limit=48, hbm=False, free=()):
    in_specs = [pl.BlockSpec(memory_space=pltpu.SMEM)]
    arrays = [args[0]]
    groups = [None]

    later = []

    def take_in(a):
        if isinstance(a, tuple) and a[1] is None:
            later.append((len(arrays), a[2], a[3]))
            arrays.append(a[0])
            in_specs.append(pl.BlockSpec(memory_space=pl.ANY))
        elif isinstance(a, tuple):
            arrays.append(a[0])
            in_specs.append(a[1])
        else:
            arrays.append(a)
            in_specs.append(full(a.shape))

    for a in args[1:]:
        nested = isinstance(a, list) and isinstance(a[0], list)
        groups.append([len(b) for b in a] if nested else len(a) if isinstance(a, list) else None)
        for one in sum(a, []) if nested else a if isinstance(a, list) else [a]:
            take_in(one)
    flat = []
    out_groups = []
    for o in outs:
        out_groups.append(len(o) if isinstance(o, list) else None)
        flat += o if isinstance(o, list) else [o]

    early = [k for k, o in enumerate(flat) if o[2] is EARLY]

    def grouped(refs, sizes):
        got, at = [], 0
        for size in sizes:
            if isinstance(size, list):
                got.append(grouped(refs[at : at + sum(size)], size))
                at += sum(size)
            else:
                got.append(refs[at] if size is None else list(refs[at : at + size]))
                at += size or 1
        return got

    def run(*refs):
        n_in, n_out = len(arrays), len(flat)
        refs = list(refs)
        for k in reversed(early):
            sems, held = refs.pop(), refs.pop()
            refs[n_in + k] = Early(held, refs[n_in + k], sems)
        for k, _, _ in reversed(later):
            sems, held = refs.pop(), refs.pop()
            refs[k] = Late(refs[k], held, sems)
        body(
            *grouped(refs[:n_in], groups), *grouped(refs[n_in : n_in + n_out], out_groups), *refs[n_in + n_out :]
        )

    if hbm or body in (pack, take):
        arrays = [
            pltpu.with_memory_space_constraint(a, pltpu.HBM) if math.prod(a.shape) >= 2**14 else a for a in arrays
        ]
    made = lambda s, t, k: (
        pltpu.HBM(s, t) if hbm and math.prod(s) >= 2**14 and k not in free else jax.ShapeDtypeStruct(s, t)
    )
    size = sum(math.prod(a.shape) * a.dtype.itemsize for a in arrays)
    size += sum(math.prod(s) * jnp.dtype(t).itemsize for s, t, _ in flat)
    size = size if flops else 0
    got = pl.pallas_call(
        run,
        grid=(steps,),
        in_specs=in_specs,
        out_specs=tuple(
            full(s) if b is None else pl.BlockSpec(memory_space=pl.ANY) if b is EARLY else b for s, _, b in flat
        ),
        out_shape=tuple(made(s, t, k) for k, (s, t, _) in enumerate(flat)),
        scratch_shapes=list(scratch)
        + [
            one
            for k, parts, first in later
            for one in (pltpu.VMEM((first,) + arrays[k].shape[1:], arrays[k].dtype), pltpu.SemaphoreType.DMA((parts,)))
        ]
        + [
            one
            for k in early
            for one in (pltpu.VMEM(flat[k][0], flat[k][1]), pltpu.SemaphoreType.DMA((flat[k][0][0] // ROWS,)))
        ],
        compiler_params=pltpu.CompilerParams(vmem_limit_bytes=limit * 2**20),
        cost_estimate=pl.CostEstimate(flops=int(flops), bytes_accessed=size, transcendentals=0),
        name=name,
    )(*arrays)
    return grouped(got, out_groups)


def step_signal(step_ids, feat_width):
    half_width = feat_width // 2
    frequency = jnp.exp(-math.log(10000.0) * jnp.arange(half_width, dtype=F32) / half_width)
    angles = step_ids.astype(F32)[:, None] * frequency[None, :]
    return jnp.concatenate([jnp.sin(angles), jnp.cos(angles)], axis=1)


def sds(shape, dtype=BF, block=None):
    return (tuple(shape), dtype, block)


def per_device(
    decoder_input, timesteps, memory, cotangent, time_weight, attn_query, attn_key, attn_value, attn_out,
    cross_query, cross_key, cross_value, cross_out, ffn_in, ffn_out, norm_gains,
):
    dp = lax.axis_size("dp")
    mem_count = lax.axis_size("mem")
    rows = D // dp
    cols = D // mem_count
    by_hand = dp == 8 and mem_count == 4
    x = decoder_input[0]
    cot = cotangent[0]
    n = x.shape[0]
    r = memory.shape[0] * memory.shape[1]
    gains = norm_gains.T
    my_dp, my_mem = lax.axis_index("dp"), lax.axis_index("mem")
    me = jnp.stack([my_dp, my_mem]).astype(jnp.int32)

    def to(value, axis, bit):
        size = lax.axis_size(axis)
        return lax.ppermute(value, axis, [(i, i ^ bit) for i in range(size)])

    def after(value, *others):
        return lax.optimization_barrier((value,) + others)[0]

    def plane(own):
        return [own] + [to(own, "dp", 2 * bit) for bit in (1, 2, 3)]

    def swap(parts):
        both = []
        for part in parts:
            both += [part, to(part, "dp", 1)]
        return both

    in_parts = [ffn_in[:, D * c : D * (c + 1)] for c in range(CHUNKS)]
    if by_hand:
        first = (time_weight, attn_query, attn_key, attn_value)
        second = (attn_out, cross_query, cross_key, cross_value, cross_out)
        (own1,) = call(pack, "pack_one", (me,) + first, [sds((4, rows, D))], limit=4)
        plane1 = plane(own1)
        mem_keep, mem_send = call(
            take, "take_memory", (me, after(memory, own1)), [sds((2,) + memory.shape[1:])] * 2, limit=8
        )
        (own2,) = call(pack, "pack_two", (me,) + second, [sds((5, rows, D))], limit=4)
        (own3,) = call(pack, "pack_three", (me, ffn_in, ffn_out), [sds((2 * CHUNKS, rows, D))], limit=8)
        near = to(mem_send, "mem", 1)
        *plane1, near, own2, own3 = lax.optimization_barrier(tuple(plane1[1:]) + (near, own2, own3))
        (passed,) = call(join, "join_memory", (me, mem_keep, near), [sds(mem_keep.shape)], limit=8)
        across = to(passed, "mem", 2)
        g1 = [own1, to(own1, "dp", 1)]
        for part in plane1:
            g1 += [part, to(part, "dp", 1)]
        mem_rows = [late(mem_keep, 1, 1), late(near, 1, 1), late(across)]
        own2 = after(own2, *g1)
        g2 = plane(own2)
        g3 = lax.all_gather(own3, "dp", axis=0, tiled=False)
    else:

        def gather(parts):
            got = lax.all_gather(jnp.stack(parts, 0), "dp", axis=0, tiled=False)
            return got.transpose(1, 0, 2, 3).reshape(1, len(parts), D, D)

        g1 = [gather((time_weight, attn_query, attn_key, attn_value))]
        g2 = [gather((attn_out, cross_query, cross_key, cross_value, cross_out))]
        whole_out = lax.all_gather(ffn_out, "dp", axis=0, tiled=True).reshape(1, CHUNKS, D, D)
        g3 = jnp.concatenate([gather(in_parts), whole_out], axis=1)
        mem_rows = [late(lax.all_to_all(memory, "mem", split_axis=0, concat_axis=1, tiled=True))]
    signal = step_signal(timesteps, D).astype(BF)
    sig = jnp.broadcast_to(signal, (8, D))

    nat = pl.BlockSpec((n, PAIR), lambda i: (0, i))
    paired = lambda m: sds((PAIRS, m, PAIR), BF, pl.BlockSpec((1, m, PAIR), lambda i: (i, 0, 0)))
    nat_r = pl.BlockSpec((r, PAIR), lambda i: (0, i))
    rows2 = pl.BlockSpec((1, 2, n), lambda i: (i, 0, 0))
    wide = lambda m: pltpu.VMEM((PAIRS, m, PAIR), BF)
    tall = lambda m: pltpu.VMEM((PAIRS, PAIR, m), BF)
    weight = pltpu.VMEM((D, D), BF)
    weights = lambda count: pltpu.VMEM((count, D, D), BF)
    proj = 2 * n * D * D * 1.5
    att_cost = 2 * n * r * D * 5
    lse_out = sds((PAIRS, 2, n), F32, rows2)
    four_weights = sds((4, D, D), BF, pl.BlockSpec((1, D, D), lambda i: (i, 0, 0)))
    emb, n1, q, k, v, lse1, attended, held1 = call(
        self_forward, "self_forward", (me, x, sig, gains, g1),
        [sds((1, D), F32)] + [paired(n)] * 4 + [lse_out, paired(n), four_weights],
        [weights(4), wide(n), wide(n), wide(n), wide(n), tall(n), tall(n), tall(n), pltpu.SMEM((PAIRS,), jnp.int32)],
        PAIRS, 3 * proj + 2 * att_cost, 36, True,
    )
    if by_hand:
        attended, *g2 = lax.optimization_barrier((attended,) + tuple(g2))
        g2 = swap(g2)
    mid, n2, cq, ck, cv, lse2, crossed, held2 = call(
        cross_forward, "cross_forward", (me, x, emb, attended, mem_rows, gains, g2),
        [sds((n, D), F32, nat)] + [paired(n)] * 2 + [paired(r)] * 2 + [lse_out, paired(n), four_weights],
        [weights(4), pltpu.VMEM((PAIRS, n, PAIR), F32), wide(n), wide(n), wide(r), wide(r), tall(n), tall(r), tall(n),
         pltpu.SMEM((PAIRS,), jnp.int32)],
        PAIRS, 4 * proj + 2 * att_cost, 42, True,
    )
    if by_hand:
        weight_of = lambda t: [(p, pl.BlockSpec((1, rows, D), lambda i: (t, 0, 0))) for p in g2]
        raw_of = lambda count: [sds((dp // 2, mem_count, count * rows, cols))] * 2
        raw3_of = sds((dp, mem_count, 2 * CHUNKS * rows, cols))
    else:
        weight_of = lambda t: [(g2[0], pl.BlockSpec((1, 1, D, D), lambda i: (0, t, 0, 0)))]
        raw_of = lambda count: [sds((count, D, D))]
        raw3_of = sds((2 * CHUNKS, D, D))
    out, gl, bt, gain3, raw3 = call(
        feed_forward, "feed_forward", (me, mid, crossed, late(cot), gains, weight_of(4), late(g3)),
        [sds((n, D), BF, EARLY), sds((n, D), F32, EARLY), sds((n, D), BF, EARLY), sds((1, D), F32), sds(*raw3_of[:2], pl.BlockSpec(memory_space=pl.ANY))],
        [weights(1), weight, weight, pltpu.VMEM((n, D), BF), pltpu.VMEM((D, n), BF)] + [pltpu.VMEM((n, D), F32)] * 3
        + [pltpu.VMEM((2, n, D), BF)] * 2 + [pltpu.VMEM(raw3_of[0], BF), pltpu.SemaphoreType.DMA((CHUNKS, 2))],
        CHUNKS + 1, 25 * proj, 44, True,
    )
    back_scratch = lambda m, mats: [
        weights(mats), tall(n), tall(m), wide(n), tall(n), pltpu.VMEM((PAIRS, 2, n), F32),
        wide(n), wide(m), wide(m), weights(5), pltpu.VMEM((D, max(n, m)), BF),
    ]
    of_held2 = lambda t: (held2, pl.BlockSpec((1, D, D), lambda i: (t, 0, 0), pipeline_mode=pl.Buffered(1)))
    raw2, gm, b1, gain2, gk, gv = call(
        cross_back, "cross_back",
        (me, bt, crossed, late(cq), late(ck), late(cv), (lse2, rows2), mem_rows, late(n2), late(mid), late(gl), gains,
         weight_of(4), of_held2(1), late(attended)),
        [raw_of(5), sds((n, D), F32, EARLY), sds((n, D), BF, EARLY), sds((1, D), F32), sds((r, D), BF, nat_r),
         sds((r, D), BF, nat_r)],
        back_scratch(r, 1), PAIRS, 8 * proj + 5 * att_cost, 56, True,
    )
    if by_hand:
        got2 = to(raw2[1], "dp", 1)
        grad_of = [sds(memory.shape[1:]), sds(memory.shape[1:]), sds((2,) + memory.shape[1:])]
    else:
        grad_of = [sds((r, D))]
    (mem_grad,) = call(
        memory_back, "memory_back", (me, gk, gv, of_held2(2), of_held2(3)), [grad_of], (), 1, 0, 32, True,
    )
    if by_hand:
        got2 = after(got2, mem_grad[2])
        (parts2,) = call(add_core, "cross_core", (me, raw2[0], got2), [[sds((mem_count, 5 * rows, cols))] * 4], limit=24)
        b1, mem_grad[2], *parts2 = lax.optimization_barrier((b1, mem_grad[2]) + tuple(parts2))
        parts2 = [parts2[0]] + [to(parts2[b], "dp", 2 * b) for b in (1, 2, 3)]
        across = to(mem_grad[2], "mem", 2)
    raw1, input_grad, sums = call(
        self_back, "self_back",
        (me, b1, attended, late(q), late(k), late(v), (lse1, rows2), late(n1), late(held1), of_held2(0),
         late(x), emb, late(gm), gains, sig, gain2, gain3),
        [raw_of(3), sds((n, D), BF, EARLY), sds((SMALL, 128)) if by_hand else sds((8, D), F32)],
        back_scratch(n, 1)[1:] + [pltpu.VMEM((2, D), F32)], PAIRS, 7 * proj + 5 * att_cost, 50, True,
    )
    if by_hand:
        keep, send = raw1
        got1, small1 = to(send, "dp", 1), to(sums, "dp", 1)
        done3 = lax.psum_scatter(raw3, "dp", scatter_dimension=0, tiled=False)
        done3 = lax.psum_scatter(done3, "mem", scatter_dimension=0, tiled=False)
        done3 = pltpu.with_memory_space_constraint(done3, pltpu.HBM)
        sums, *parts2 = lax.optimization_barrier((sums,) + tuple(parts2))
        (passed,) = call(join, "join_grad", (me, mem_grad[1], after(across, *parts2)), [sds(across.shape)], limit=8, flops=6e9)
        sums, keep, passed = lax.optimization_barrier((sums, keep, passed))

    limit = math.sqrt(9 * D * D + 2 * D * FF + 3 * D)
    if not by_hand:
        memory_grad = lax.all_to_all(mem_grad[0][None], "mem", split_axis=1, concat_axis=0, tiled=True)

        def scatter(raw):
            part = lax.psum_scatter(raw, "dp", scatter_dimension=1, tiled=True)
            part = lax.psum_scatter(part, "mem", scatter_dimension=2, tiled=True)
            return [part[t].astype(F32) for t in range(raw.shape[0])]

        d_in = scatter(raw3[:CHUNKS].transpose(1, 0, 2).reshape(1, D, FF))[0]
        d_fout = scatter(raw3[CHUNKS:].reshape(1, FF, D))[0]
        d_query, d_key, d_value = scatter(raw1[0])
        d_cout, d_cquery, d_ckey, d_cvalue, d_out = scatter(raw2[0])
        everyone = lax.all_gather(sums, ("dp", "mem"), axis=0, tiled=False)
        my_signal = lax.dynamic_slice_in_dim(everyone[:, 1], my_dp * rows, rows, axis=1)
        my_sums = lax.dynamic_slice_in_dim(everyone[:, 0], my_mem * cols, cols, axis=1)
        d_time = jnp.dot(my_signal.T, my_sums, precision=lax.Precision.HIGHEST)
        all_gains = jnp.sum(everyone[:, 2:5], axis=0)
        d_gains = lax.dynamic_slice_in_dim(all_gains, my_dp * rows, rows, axis=1).T
        weights = [d_time, d_query, d_key, d_value, d_out, d_cquery, d_ckey, d_cvalue, d_cout, d_in, d_fout]
        local = sum(jnp.sum(w * w) for w in weights)
        squares = lax.psum(local, ("dp", "mem")) + jnp.sum(all_gains * all_gains)
        factor = jnp.minimum(1.0, limit * lax.rsqrt(squares))
        return (
            (out[None], input_grad[None], memory_grad) + tuple(w * factor for w in weights) + (d_gains * factor,)
        )

    parts1 = call(
        add_core_small, "attn_core", (me, keep, got1, sums, small1),
        [sds((mem_count * 3 * rows + SMALL, cols))] * 4, limit=16,
    )
    parts1 = [parts1[0]] + [to(parts1[b], "dp", 2 * b) for b in (1, 2, 3)]
    parts = call(
        add_plane, "plane_sums", (me, parts1, parts2), [sds((8 * rows + SMALL, cols))] * mem_count, limit=24, hbm=False
    )
    parts = [parts[0]] + [to(parts[b], "mem", b) for b in (1, 2, 3)]
    done1, done2, d_time, d_gains, local = call(
        add_all, "add_all", (me, parts, done3),
        [sds((3 * rows, cols), F32), sds((5 * rows, cols), F32), sds((rows, cols), F32), sds((8, cols), F32),
         sds((8, cols), F32)],
        limit=16,
    )
    near = to(after(passed, local), "mem", 1)
    local = local + to(local, "dp", 1)
    local = local + to(local, "dp", 2) + to(local, "dp", 4) + to(local, "dp", 6)
    planes = [local] + [to(local, "mem", b) for b in (1, 2, 3)]
    shapes = [(rows, cols)] * 9 + [(rows, FF // mem_count), (FF // dp, cols), (3, rows)]
    memory_grad, *scaled = call(
        scale_all, "scale_all", [me] + planes + [d_time, d_gains, done1, done2, done3, mem_grad[0], across, near],
        [sds(memory.shape)] + [sds(s, F32) for s in shapes], limit=20,
    )
    return (out[None], input_grad[None], memory_grad) + tuple(scaled[:-1]) + (scaled[-1].T,)


def solution(mesh):
    tokens = P(("dp", "mem"), None, None)
    weight = P("dp", None)
    in_specs = (tokens, P(("dp", "mem")), P("dp", "mem", None), tokens) + (weight,) * 11 + (P(),)
    out_specs = (tokens, tokens, P("dp", "mem", None)) + (P("dp", "mem"),) * 11 + (P("dp", None),)
    return jax.shard_map(per_device, mesh=mesh, in_specs=in_specs, out_specs=out_specs, check_vma=False)
```

```python
import functools
import math

import jax
import jax.numpy as jnp
from jax import lax
from jax.experimental import pallas as pl
from jax.experimental.pallas import tpu as pltpu
from jax.sharding import PartitionSpec as P

D = 512
HEADS = 8
HEAD = 64
FF = 2048
PAIRS = HEADS // 2
PAIR = 2 * HEAD
CHUNKS = FF // D
BF = jnp.bfloat16
F32 = jnp.float32
SCALE = 1.0 / math.sqrt(HEAD)
ROOT_HALF = math.sqrt(0.5)
BELL = 1.0 / math.sqrt(2.0 * math.pi)


def dot(a, b, ca=1, cb=0):
    return lax.dot_general(a, b, (((ca,), (cb,)), ((), ())), preferred_element_type=F32)


def row_mean(v):
    return jnp.sum(v, axis=-1, keepdims=True) * (1.0 / v.shape[-1])


def norm_parts(v):
    centred = v - row_mean(v)
    scale = lax.rsqrt(row_mean(centred * centred) + 1e-05)
    return centred * scale, scale


def norm_back(v, gain, grad):
    normed, scale = norm_parts(v)
    c = grad * gain
    gain_part = jnp.sum(grad * normed, axis=0, keepdims=True)
    return scale * (c - row_mean(c) - normed * row_mean(c * normed)), gain_part


def build(w, slot, parts, which, me):
    dst = w.at[slot]
    if len(parts) == 1:
        blocks, _, rows, _ = parts[0].shape
        for b in range(blocks):
            dst[rows * b : rows * (b + 1), :] = parts[0][b, which]
        return
    rows = parts[0].shape[1]
    for r, part in enumerate(parts):
        lo = pl.multiple_of((r ^ me) * rows, rows)
        dst[pl.ds(lo, rows), :] = part[which]


def put(refs, at, mat, core):
    mat = mat.astype(refs[0].dtype)
    if len(refs) == 1:
        refs[0][at] = mat
        return
    half, cb, _, cols = refs[0].shape
    rows = D // (2 * half)

    def cut(own, other):
        for a in range(2 * half):
            ref = own if a % 2 == 0 else other
            for j in range(cb):
                ref[a // 2, j, rows * at : rows * (at + 1), :] = mat[
                    rows * a : rows * (a + 1), cols * j : cols * (j + 1)
                ]

    @pl.when(core == 0)
    def _():
        cut(refs[0], refs[1])

    @pl.when(core == 1)
    def _():
        cut(refs[1], refs[0])


ROWS = 512


def each_block(total, step, body):
    def run(b, carry):
        body(pl.ds(pl.multiple_of(b * step, step), step))
        return carry

    lax.fori_loop(0, total // step, run, 0)


SAFE = 1444.0


def judge(flags, qT, k):
    line = lax.broadcasted_iota(jnp.int32, (8, PAIR), 0)
    lane = lax.broadcasted_iota(jnp.int32, (8, PAIR), 1)
    mine = jnp.where((lane // HEAD) == line, 1.0, 0.0).astype(BF)
    for p in range(PAIRS):
        of_q = jnp.max(dot(mine, qT[p] * qT[p]), axis=1, keepdims=True)
        of_k = jnp.max(dot(mine, k[p] * k[p], 1, 1), axis=1, keepdims=True)
        flags[p] = jnp.where(jnp.max(of_q * of_k) <= SAFE, 1, 0)


def attend(i, flags, qT, k, vT, oT, lse):
    n = qT.shape[2]
    row = lax.broadcasted_iota(jnp.int32, (PAIR, n), 0)
    zero = jnp.zeros((), BF)

    def run(shifted):
        scores = [dot(k[i], jnp.where((row // HEAD) == h, qT[i], zero)) for h in range(2)]
        for h in range(2):
            own = slice(HEAD * h, HEAD * (h + 1))
            score = scores[h]
            top = jnp.max(score, axis=0, keepdims=True) if shifted else None
            e = jnp.exp(score - top if shifted else score)
            total = jnp.sum(e, axis=0, keepdims=True)
            out = dot(vT[i, own, :], e.astype(BF))
            oT[i, own, :] = (out * (1.0 / total)).astype(BF)
            lse[0, h : h + 1, :] = top + jnp.log(total) if shifted else jnp.log(total)

    @pl.when(flags[i] == 1)
    def _():
        run(False)

    @pl.when(flags[i] == 0)
    def _():
        run(True)


def attend_back(i, q, qT, k, kT, v, g, gT, lse, delta, dq, dk, dv):
    n = qT.shape[2]
    block = min(n, 512)
    row = lax.broadcasted_iota(jnp.int32, (PAIR, block), 0)
    lane = lax.broadcasted_iota(jnp.int32, (block, PAIR), 1)
    zero = jnp.zeros((), BF)
    total_k = total_v = None
    for j in range(n // block):
        at = slice(j * block, (j + 1) * block)
        turned = []
        for h in range(2):
            own = slice(HEAD * h, HEAD * (h + 1))
            s = dot(k[i], jnp.where((row // HEAD) == h, qT[i, :, at], zero))
            dp = dot(v[i], jnp.where((row // HEAD) == h, gT[i, :, at], zero))
            p = jnp.exp(s - lse[0, h : h + 1, at])
            ds = (p * (dp - delta[i, h : h + 1, at])).astype(BF)
            one_v = dot(p.astype(BF), jnp.where((lane // HEAD) == h, g[i, at, :], zero))
            one_k = dot(ds, jnp.where((lane // HEAD) == h, q[i, at, :], zero))
            turned.append((dot(kT[i, own, :], ds) * SCALE).astype(BF))
            total_v = one_v if total_v is None else total_v + one_v
            total_k = one_k if total_k is None else total_k + one_k
        dq[i, at, :] = jnp.concatenate(turned, axis=0).T
    dk[i] = (total_k * SCALE).astype(BF)
    dv[i] = total_v.astype(BF)


def prepare(p, q, k, g, heads, qT, kT, gT, delta):
    qT[p] = q[p].T * jnp.asarray(SCALE, BF)
    kT[p] = k[p].T
    gT[p] = g[p].T
    both = gT[p].astype(F32) * heads[p].T.astype(F32)
    for h in range(2):
        delta[p, h : h + 1, :] = jnp.sum(both[HEAD * h : HEAD * (h + 1), :], axis=0, keepdims=True)


def products(refs, first, leftT, rights, core, whole):
    def run(b, carry):
        rows = pl.ds(pl.multiple_of(b * ROWS, ROWS), ROWS)
        for t, right in enumerate(rights):
            whole[first + t, rows, :] = dot(leftT[rows, :], from_pairs(right)).astype(BF)
        return carry

    lax.fori_loop(0, D // ROWS, run, 0)
    for t in range(len(rights)):
        put(refs, first + t, whole[first + t], core)


def turn_pairs(dst, src):
    for p in range(PAIRS):
        dst[PAIR * p : PAIR * (p + 1), :] = src[p].T


def pairs_at(dst, rows, src):
    for p in range(PAIRS):
        dst[p, rows, :] = src[:, PAIR * p : PAIR * (p + 1)]


def joined(src, rows):
    return jnp.concatenate([src[p, rows, :] for p in range(PAIRS)], axis=1)


def pairs_in(dst, src):
    for p in range(PAIRS):
        dst[p] = src[:, PAIR * p : PAIR * (p + 1)]


def from_pairs(src):
    return jnp.concatenate([src[p] for p in range(PAIRS)], axis=1)


def from_pairs_T(src):
    return jnp.concatenate([src[p].T for p in range(PAIRS)], axis=1)


def rows_of(mem):
    parts = [m[t] for m in mem for t in range(m.shape[0])]
    return jnp.concatenate(parts, axis=0) if len(parts) > 1 else parts[0]


def self_forward(me, x, sig, gains, g1, emb, n1, q, k, v, lse, att, held, w, n1s, qs, ks, vs, qT, vT, oT, flags):
    i = pl.program_id(0)

    @pl.when(i == 0)
    def _():
        build(w, 0, g1, 0, me[0])
        embedded = dot(sig[...], w[0])[0:1, :]
        emb[...] = embedded
        resid = x[...].astype(F32) + embedded
        normed = (norm_parts(resid)[0] * gains[0:1, :]).astype(BF)
        pairs_in(n1s, normed)
        for t, dst in ((1, qs), (2, ks), (3, vs)):
            build(w, t, g1, t, me[0])
            pairs_in(dst, dot(normed, w[t]).astype(BF))
        for p in range(PAIRS):
            qT[p] = qs[p].T * jnp.asarray(SCALE, BF)
            vT[p] = vs[p].T
        judge(flags, qT, ks)

    attend(i, flags, qT, ks, vT, oT, lse)
    held[0] = w[i]
    n1[0] = n1s[i]
    q[0] = qs[i]
    k[0] = ks[i]
    v[0] = vs[i]
    att[0] = oT[i].T


def cross_forward(
    me, x, emb, att, mem, gains, g2, mid, n2, cq, k, v, lse, crossed, held, w, mids, n2s, qs, ks, vs, qT, vT, oT, flags
):
    i = pl.program_id(0)

    @pl.when(i == 0)
    def _():
        fetch(*mem)
        build(w, 0, g2, 0, me[0])
        new = x[...].astype(F32) + emb[...] + dot(from_pairs(att), w[0])
        pairs_in(mids, new)
        normed = (norm_parts(new)[0] * gains[1:2, :]).astype(BF)
        pairs_in(n2s, normed)
        build(w, 1, g2, 1, me[0])
        pairs_in(qs, dot(normed, w[1]).astype(BF))
        wait(*mem)
        rows = rows_of([m.ref for m in mem])
        for t, dst in ((2, ks), (3, vs)):
            build(w, t, g2, t, me[0])
            pairs_in(dst, dot(rows, w[t]).astype(BF))
        for p in range(PAIRS):
            qT[p] = qs[p].T * jnp.asarray(SCALE, BF)
            vT[p] = vs[p].T
        judge(flags, qT, ks)

    attend(i, flags, qT, ks, vT, oT, lse)
    held[0] = w[i]
    mid[...] = mids[i]
    n2[0] = n2s[i]
    cq[0] = qs[i]
    k[0] = ks[i]
    v[0] = vs[i]
    crossed[0] = oT[i].T


def feed_forward(
    me, mid, crossed, cot, gains, g2, g3,
    out, gl, bt, gain3, raw_out_ref,
    wlate, win, wout, n3, n3T, late, acc, gacc, active, grad_inner, raw, sems,
):
    i = pl.program_id(0)
    blocks, _, rows, _ = g3.ref.shape
    n = mid.shape[0]
    each = max(blocks // CHUNKS, 1)
    now, before = i % 2, (i + 1) % 2
    piece = D // (n // 512)

    @pl.when(i == 0)
    def _():
        fetch(cot, g3)
        build(wlate, 0, g2, 0, me[0])

        def enter(at):
            new = mid[at, :] + dot(joined(crossed, at), wlate[0])
            late[at, :] = new
            normed = (norm_parts(new)[0] * gains[2:3, :]).astype(BF)
            n3[at, :] = normed
            n3T[:, at] = normed.T
            acc[at, :] = new
            gacc[at, :] = jnp.zeros((ROWS, D), F32)

        each_block(n, ROWS, enter)
        wait(cot, g3)

    @pl.when(i < CHUNKS)
    def _():
        for b in range(blocks):
            win[rows * b : rows * (b + 1), :] = g3.ref[b, i]
        if blocks == 1:
            wout[...] = g3.ref[0, CHUNKS + i]
        else:
            for u in range(each):
                for t in range(CHUNKS):
                    lo = rows * (CHUNKS * u + t)
                    wout[lo : lo + rows, :] = g3.ref[each * i + u, CHUNKS + t]

    def hidden(at):
        inner = dot(n3[at, :], win[...])
        grad_active = dot(cot.ref[at, :], wout[...], 1, 1)
        share = 0.5 * (1.0 + lax.erf(inner * ROOT_HALF))
        act = (inner * share).astype(BF)
        active[now, at, :] = act
        acc[at, :] += dot(act, wout[...])
        slope = share + inner * (jnp.exp(-0.5 * inner * inner) * BELL)
        grad = (slope * grad_active).astype(BF)
        grad_inner[now, at, :] = grad
        gacc[at, :] += dot(grad, win[...], 1, 1)

    def weights(b):
        c = i - 1
        at = pl.ds(pl.multiple_of(b * piece, piece), piece)
        raw_in = dot(n3T[at, :], grad_inner[before]).astype(BF)
        raw_out = dot(active[before, :, at], cot.ref[...], 0, 0).astype(BF)
        if blocks == 1:
            raw[c, at, :] = raw_in
            raw[CHUNKS + c, at, :] = raw_out
            return
        cols = D // CHUNKS
        for a in range(piece // rows):
            for t in range(CHUNKS):
                raw[(piece // rows) * b + a, c, rows * t : rows * (t + 1), :] = raw_in[
                    rows * a : rows * (a + 1), cols * t : cols * (t + 1)
                ]
        tall = D // each
        split = tall // piece
        lo = tall + (b % split) * piece
        for j in range(CHUNKS):
            raw[each * c + b // split, j, pl.ds(pl.multiple_of(lo, piece), piece), :] = raw_out[
                :, cols * j : cols * (j + 1)
            ]

    @pl.when(i == 0)
    def _():
        each_block(n, 512, hidden)

    @pl.when((i > 0) & (i < CHUNKS))
    def _():
        def both(b, carry):
            weights(b)
            hidden(pl.ds(pl.multiple_of(b * 512, 512), 512))
            return carry

        lax.fori_loop(0, n // 512, both, 0)

    @pl.when(i == CHUNKS)
    def _():
        def only(b, carry):
            weights(b)
            return carry

        lax.fori_loop(0, n // 512, only, 0)

    def copies(c):
        if blocks == 1:
            return [
                pltpu.make_async_copy(raw.at[at], raw_out_ref.at[at], sems.at[c, k])
                for k, at in enumerate((c, CHUNKS + c))
            ]
        tall = D // each
        first = (slice(None), c, pl.ds(0, tall))
        second = (pl.ds(each * c, each), slice(None), pl.ds(tall, tall))
        return [
            pltpu.make_async_copy(raw.at[at], raw_out_ref.at[at], sems.at[c, k])
            for k, at in enumerate((first, second))
        ]

    @pl.when(i > 0)
    def _():
        for copy in copies(i - 1):
            copy.start()

    @pl.when(i == CHUNKS)
    def _():
        gain3[...] = jnp.zeros_like(gain3)

        def leave(at):
            out.ref[at, :] = acc[at, :].astype(BF)
            part, gain_part = norm_back(late[at, :], gains[2:3, :], gacc[at, :])
            gain3[...] += gain_part
            total = cot.ref[at, :].astype(F32) + part
            gl.ref[at, :] = total
            bt.ref[at, :] = total.astype(BF)
            for one in (out, gl, bt):
                one.copy(at.start // ROWS).start()

        each_block(n, ROWS, leave)
        for one in (out, gl, bt):
            one.finish()
        for c in range(CHUNKS):
            for copy in copies(c):
                copy.wait()


def start_back(branch, weight, g):
    def enter(rows):
        pairs_at(g, rows, dot(branch[rows, :], weight[...], 1, 1).astype(BF))

    each_block(branch.shape[0], ROWS, enter)


def cross_back(
    me, bt, crossed, late_q, late_k, late_v, lse, mem, n2, mid, gl, gains, g2_out, w_query, att,
    raw, gm, b1, gain2, gk, gv,
    w, qT, kT, g, gT, delta, dq, dk, dv, whole, leftT,
):
    i = pl.program_id(0)
    core = me[0] % 2
    q, k, v = late_q.ref, late_k.ref, late_v.ref
    turned = (q, k, g, crossed, qT, kT, gT, delta)

    @pl.when(i == 0)
    def _():
        fetch(late_q, late_k, late_v)
        build(w, 0, g2_out, 0, me[0])
        start_back(bt, w.at[0], g)
        turn_pairs(leftT, crossed)
        wait(late_q, late_k, late_v)
        prepare(0, *turned)

        def run(b, carry):
            rows = pl.ds(pl.multiple_of(b * ROWS, ROWS), ROWS)
            whole[0, rows, :] = dot(leftT[rows, 0 : bt.shape[0]], bt[...]).astype(BF)
            return carry

        lax.fori_loop(0, D // ROWS, run, 0)
        put(raw, 0, whole[0], core)

    @pl.when(i == 1)
    def _():
        fetch(*mem, n2, mid, gl, att)

    attend_back(i, q, qT, k, kT, v, g, gT, lse, delta, dq, dk, dv)
    prepare(jnp.minimum(i + 1, PAIRS - 1), *turned)
    gk[...] = dk[i]
    gv[...] = dv[i]

    @pl.when(i == PAIRS - 1)
    def _():
        wait(*mem, n2, mid, gl, att)
        gain2[...] = jnp.zeros_like(gain2)

        def leave(rows):
            part, gain_part = norm_back(mid.ref[rows, :], gains[1:2, :], dot(joined(dq, rows), w_query[0], 1, 1))
            gain2[...] += gain_part
            total = gl.ref[rows, :] + part
            gm.ref[rows, :] = total
            b1.ref[rows, :] = total.astype(BF)
            for one in (gm, b1):
                one.copy(rows.start // ROWS).start()

        each_block(bt.shape[0], ROWS, leave)
        n, r = dq.shape[1], dk.shape[1]
        turn_pairs(leftT.at[:, 0:n], n2.ref)
        products(raw, 1, leftT.at[:, 0:n], (dq,), core, whole)
        at = 0
        for part in [m.ref[t] for m in mem for t in range(m.ref.shape[0])]:
            leftT[:, at : at + part.shape[0]] = part.T
            at += part.shape[0]
        products(raw, 2, leftT.at[:, 0:r], (dk, dv), core, whole)
        turn_pairs(leftT.at[:, 0:n], att.ref)

        def run(b, carry):
            rows = pl.ds(pl.multiple_of(b * ROWS, ROWS), ROWS)
            whole[4, rows, :] = dot(leftT[rows, 0:n], b1.ref[...]).astype(BF)
            return carry

        lax.fori_loop(0, D // ROWS, run, 0)
        put(raw, 4, whole[4], core)
        for one in (gm, b1):
            one.finish()


def memory_back(me, gk, gv, w_key, w_value, outs):
    back = (dot(gk[...], w_key[0], 1, 1) + dot(gv[...], w_value[0], 1, 1)).astype(BF)
    if len(outs) == 1:
        outs[0][...] = back
        return
    size = back.shape[0] // 4
    parts = [back[size * t : size * (t + 1)] for t in range(4)]
    outs[0][...], outs[1][...] = parts[0], parts[1]
    outs[2][0], outs[2][1] = parts[2], parts[3]


def self_back(
    me, b1, att, late_q, late_k, late_v, lse, n1, held, w_out, x, emb, gm, gains, sig, gain2, gain3,
    raw, grad, outs,
    qT, kT, g, gT, delta, dq, dk, dv, whole, leftT, sums,
):
    i = pl.program_id(0)
    core = me[0] % 2
    q, k, v = late_q.ref, late_k.ref, late_v.ref
    turned = (q, k, g, att, qT, kT, gT, delta)

    @pl.when(i == 0)
    def _():
        fetch(late_q, late_k, late_v)
        start_back(b1, w_out.at[0], g)
        wait(late_q, late_k, late_v)
        prepare(0, *turned)

    @pl.when(i == 1)
    def _():
        fetch(n1, x, gm, held)

    attend_back(i, q, qT, k, kT, v, g, gT, lse, delta, dq, dk, dv)
    prepare(jnp.minimum(i + 1, PAIRS - 1), *turned)

    @pl.when(i == PAIRS - 1)
    def _():
        wait(n1, x, gm, held)
        sums[...] = jnp.zeros_like(sums)

        def leave(rows):
            parts = (joined(dq, rows), joined(dk, rows), joined(dv, rows))
            back = sum(dot(part, held.ref[t + 1], 1, 1) for t, part in enumerate(parts))
            resid = x.ref[rows, :].astype(F32) + emb[...]
            part, gain_part = norm_back(resid, gains[0:1, :], back)
            total = gm.ref[rows, :] + part
            grad.ref[rows, :] = total.astype(BF)
            grad.copy(rows.start // ROWS).start()
            sums[0:1, :] += jnp.sum(total, axis=0, keepdims=True)
            sums[1:2, :] += gain_part

        each_block(b1.shape[0], ROWS, leave)
        turn_pairs(leftT, n1.ref)
        products(raw, 0, leftT, (dq, dk, dv), core, whole)
        small_rows(outs, [sums[0:1, :], sig[0:1, :].astype(F32), sums[1:2, :], gain2[...], gain3[...]])
        grad.finish()


SMALL = 32


def small_rows(outs, rows):
    if outs.shape[1] == D:
        for t, row in enumerate(rows):
            outs[t : t + 1, :] = row
        outs[5:8, :] = jnp.zeros((3, D), F32)
        return
    tile = jnp.concatenate([row[:, 128 * c : 128 * (c + 1)] for row in rows for c in range(D // 128)], axis=0)
    outs[...] = jnp.concatenate([tile, jnp.zeros((SMALL - tile.shape[0], 128), F32)], axis=0).astype(BF)


def pack(me, *refs):
    out = refs[-1]
    rows = out.shape[1]
    at = 0
    for ref in refs[:-1]:
        for c in range(ref.shape[1] // D):
            for r in range(ref.shape[0] // rows):
                out[at] = ref[rows * r : rows * (r + 1), D * c : D * (c + 1)]
                at += 1


def add_core(me, keep, got, outs):
    place = me[0] // 2
    for r, out in enumerate(outs):
        out[...] = keep[r ^ place] + got[r ^ place]


def add_core_small(me, keep, got, mine, other, *outs):
    place = me[0] // 2
    cb, size, cols = keep.shape[1:]
    a, b = mine[...].astype(F32), other[...].astype(F32)
    small = jnp.concatenate([a[0:4], b[0:4], a[4:8], b[4:8], a[8:20] + b[8:20], a[28:32]], axis=0).astype(BF)
    for r, out in enumerate(outs):
        out[0 : cb * size, :] = (keep[r ^ place] + got[r ^ place]).reshape(cb * size, cols)
        out[cb * size :, :] = small


def add_plane(me, parts, cross, *outs):
    more = cross[0].shape[1]
    size = outs[0].shape[0] - SMALL - more
    cb = (parts[0].shape[0] - SMALL) // size
    small = [p[cb * size :, :].astype(F32) for p in parts]
    gains = small[0][16:28] + small[1][16:28] + small[2][16:28] + small[3][16:28]
    line = lax.broadcasted_iota(jnp.int32, (4, 128), 0)

    def pick(rows, which):
        return jnp.sum(jnp.where(line == which, rows, 0.0), axis=0, keepdims=True)

    signals = []
    for p in small:
        for core in range(2):
            row = pick(p[8 + 4 * core : 12 + 4 * core], me[0] // 2)
            turned = jnp.concatenate([row[:, 64:], row[:, :64]], axis=1)
            signals.append(jnp.where(me[0] % 2 == 1, turned, row))
    for r, out in enumerate(outs):
        at = r ^ me[1]
        spot = pl.ds(pl.multiple_of(at * size, size), size)
        total = sum(p[spot, :].astype(F32) for p in parts)
        out[0:size, :] = total.astype(BF)
        out[size : size + more, :] = sum(p[at].astype(F32) for p in cross).astype(BF)
        sums = [pick(p[4 * core : 4 * (core + 1)], at) for p in small for core in range(2)]
        rows = jnp.concatenate(sums + signals + [gains, jnp.zeros((4, 128), F32)], axis=0)
        out[size + more :, :] = rows.astype(BF)


def fold(v):
    return jnp.sum((v * v).reshape(-1, 8, v.shape[-1]), axis=0)


def add_all(me, parts, feed, done1, done2, d_time, d_gains, squares):
    size, more = done1.shape[0], done2.shape[0]
    total1 = sum(p[0:size, :].astype(F32) for p in parts)
    done1[...] = total1
    total2 = sum(p[size : size + more, :].astype(F32) for p in parts)
    done2[...] = total2
    small = [p[size + more :, :].astype(F32) for p in parts]
    sums = jnp.concatenate([p[0:8] for p in small], axis=0).astype(BF)
    signals = jnp.concatenate([p[8:16] for p in small], axis=0).astype(BF)
    rows = d_time.shape[0]
    of_time = dot(signals, sums, 0, 0)[0:rows, :]
    d_time[...] = of_time
    gains = small[0][16:28] + small[1][16:28] + small[2][16:28] + small[3][16:28]
    line = lax.broadcasted_iota(jnp.int32, (4, 128), 0)
    lane = lax.broadcasted_iota(jnp.int32, (1, 128), 1)
    mine = []
    for t in range(3):
        row = jnp.sum(jnp.where(line == me[0] // 2, gains[4 * t : 4 * (t + 1)], 0.0), axis=0, keepdims=True)
        row = jnp.where(me[0] % 2 == 1, jnp.concatenate([row[:, 64:], row[:, :64]], axis=1), row)
        mine.append(jnp.where(lane < 64, row, 0.0))
    block = jnp.concatenate(mine + [jnp.zeros((5, 128), F32)], axis=0)
    d_gains[...] = block[0:8, :]
    wide = feed[...].astype(F32)
    squares[...] = fold(total1) + fold(total2) + fold(wide) + fold(of_time) + fold(block) * 0.25


def take(me, src, keep, send):
    for t in range(2):
        keep[t] = src[(2 * t) ^ me[1]]
        send[t] = src[(2 * t + 1) ^ me[1]]


def join(me, first, second, out):
    out[0] = first[...] if len(first.shape) == 2 else first[1]
    out[1] = second[1]


def place_rows(me, own, across, near, out):
    out[me[1]] = own[...]
    out[2 ^ me[1]] = across[0]
    out[1 ^ me[1]] = near[0]
    out[3 ^ me[1]] = near[1]


def scale_all(me, s0, s1, s2, s3, d_time, d_gains, a1, a2, a3, own, across, near, placed, *outs):
    place_rows(me, own, across, near, placed)
    squares = jnp.sum(s0[...] + s1[...] + s2[...] + s3[...])
    limit = math.sqrt(9 * D * D + 2 * D * FF + 3 * D)
    factor = jnp.minimum(1.0, limit * lax.rsqrt(jnp.full((8, 128), squares, F32)))[0:1, :]
    o_time, o_q, o_k, o_v, o_out, o_cq, o_ck, o_cv, o_cout, o_in, o_fout, o_gains = outs
    o_time[...] = d_time[...] * factor
    rows = d_time.shape[0]
    for src, dsts in ((a1, (o_q, o_k, o_v)), (a2, (o_cout, o_cq, o_ck, o_cv, o_out))):
        for t, dst in enumerate(dsts):
            dst[...] = src[rows * t : rows * (t + 1), :] * factor
    for t in range(CHUNKS):
        o_in[:, 128 * t : 128 * (t + 1)] = a3[rows * t : rows * (t + 1), :].astype(F32) * factor
    o_fout[...] = a3[rows * CHUNKS :, :].astype(F32) * factor
    o_gains[...] = (d_gains[...] * factor)[0:3, 0 : o_gains.shape[1]]


class Late:
    def __init__(self, src, dst, sems):
        self.src, self.ref, self.sems = src, dst, sems

    def copies(self):
        count = self.sems.shape[0]
        if count == 1:
            whole = pl.ds(0, self.ref.shape[0])
            return [pltpu.make_async_copy(self.src.at[whole], self.ref, self.sems.at[0])]
        return [pltpu.make_async_copy(self.src.at[p], self.ref.at[p], self.sems.at[p]) for p in range(count)]


class Early:
    def __init__(self, src, dst, sems):
        self.ref, self.dst, self.sems = src, dst, sems

    def copy(self, b):
        rows = pl.ds(pl.multiple_of(b * ROWS, ROWS), ROWS)
        return pltpu.make_async_copy(self.ref.at[rows, :], self.dst.at[rows, :], self.sems.at[b])

    def finish(self):
        for b in range(self.sems.shape[0]):
            self.copy(b).wait()


def fetch(*operands):
    for one in operands:
        for copy in one.copies():
            copy.start()


def wait(*operands):
    for one in operands:
        for copy in one.copies():
            copy.wait()


def late(array, parts=1, first=None):
    return (array, None, parts, first or array.shape[0])


EARLY = "early"


def full(shape):
    return pl.BlockSpec(shape, lambda i: (0,) * len(shape), pipeline_mode=pl.Buffered(1))


def call(body, name, args, outs, scratch=(), steps=1, flops=0, limit=48, hbm=False, free=()):
    in_specs = [pl.BlockSpec(memory_space=pltpu.SMEM)]
    arrays = [args[0]]
    groups = [None]

    later = []

    def take_in(a):
        if isinstance(a, tuple) and a[1] is None:
            later.append((len(arrays), a[2], a[3]))
            arrays.append(a[0])
            in_specs.append(pl.BlockSpec(memory_space=pl.ANY))
        elif isinstance(a, tuple):
            arrays.append(a[0])
            in_specs.append(a[1])
        else:
            arrays.append(a)
            in_specs.append(full(a.shape))

    for a in args[1:]:
        nested = isinstance(a, list) and isinstance(a[0], list)
        groups.append([len(b) for b in a] if nested else len(a) if isinstance(a, list) else None)
        for one in sum(a, []) if nested else a if isinstance(a, list) else [a]:
            take_in(one)
    flat = []
    out_groups = []
    for o in outs:
        out_groups.append(len(o) if isinstance(o, list) else None)
        flat += o if isinstance(o, list) else [o]

    early = [k for k, o in enumerate(flat) if o[2] is EARLY]

    def grouped(refs, sizes):
        got, at = [], 0
        for size in sizes:
            if isinstance(size, list):
                got.append(grouped(refs[at : at + sum(size)], size))
                at += sum(size)
            else:
                got.append(refs[at] if size is None else list(refs[at : at + size]))
                at += size or 1
        return got

    def run(*refs):
        n_in, n_out = len(arrays), len(flat)
        refs = list(refs)
        for k in reversed(early):
            sems, held = refs.pop(), refs.pop()
            refs[n_in + k] = Early(held, refs[n_in + k], sems)
        for k, _, _ in reversed(later):
            sems, held = refs.pop(), refs.pop()
            refs[k] = Late(refs[k], held, sems)
        body(
            *grouped(refs[:n_in], groups), *grouped(refs[n_in : n_in + n_out], out_groups), *refs[n_in + n_out :]
        )

    if hbm or body in (pack, take):
        arrays = [
            pltpu.with_memory_space_constraint(a, pltpu.HBM) if math.prod(a.shape) >= 2**14 else a for a in arrays
        ]
    made = lambda s, t, k: (
        pltpu.HBM(s, t) if hbm and math.prod(s) >= 2**14 and k not in free else jax.ShapeDtypeStruct(s, t)
    )
    size = sum(math.prod(a.shape) * a.dtype.itemsize for a in arrays)
    size += sum(math.prod(s) * jnp.dtype(t).itemsize for s, t, _ in flat)
    size = size if flops else 0
    got = pl.pallas_call(
        run,
        grid=(steps,),
        in_specs=in_specs,
        out_specs=tuple(
            full(s) if b is None else pl.BlockSpec(memory_space=pl.ANY) if b is EARLY else b for s, _, b in flat
        ),
        out_shape=tuple(made(s, t, k) for k, (s, t, _) in enumerate(flat)),
        scratch_shapes=list(scratch)
        + [
            one
            for k, parts, first in later
            for one in (pltpu.VMEM((first,) + arrays[k].shape[1:], arrays[k].dtype), pltpu.SemaphoreType.DMA((parts,)))
        ]
        + [
            one
            for k in early
            for one in (pltpu.VMEM(flat[k][0], flat[k][1]), pltpu.SemaphoreType.DMA((flat[k][0][0] // ROWS,)))
        ],
        compiler_params=pltpu.CompilerParams(vmem_limit_bytes=limit * 2**20),
        cost_estimate=pl.CostEstimate(flops=int(flops), bytes_accessed=size, transcendentals=0),
        name=name,
    )(*arrays)
    return grouped(got, out_groups)


def step_signal(step_ids, feat_width):
    half_width = feat_width // 2
    frequency = jnp.exp(-math.log(10000.0) * jnp.arange(half_width, dtype=F32) / half_width)
    angles = step_ids.astype(F32)[:, None] * frequency[None, :]
    return jnp.concatenate([jnp.sin(angles), jnp.cos(angles)], axis=1)


def sds(shape, dtype=BF, block=None):
    return (tuple(shape), dtype, block)


def per_device(
    decoder_input, timesteps, memory, cotangent, time_weight, attn_query, attn_key, attn_value, attn_out,
    cross_query, cross_key, cross_value, cross_out, ffn_in, ffn_out, norm_gains,
):
    dp = lax.axis_size("dp")
    mem_count = lax.axis_size("mem")
    rows = D // dp
    cols = D // mem_count
    by_hand = dp == 8 and mem_count == 4
    x = decoder_input[0]
    cot = cotangent[0]
    n = x.shape[0]
    r = memory.shape[0] * memory.shape[1]
    gains = norm_gains.T
    my_dp, my_mem = lax.axis_index("dp"), lax.axis_index("mem")
    me = jnp.stack([my_dp, my_mem]).astype(jnp.int32)

    def to(value, axis, bit):
        size = lax.axis_size(axis)
        return lax.ppermute(value, axis, [(i, i ^ bit) for i in range(size)])

    def after(value, *others):
        return lax.optimization_barrier((value,) + others)[0]

    def plane(own):
        return [own] + [to(own, "dp", 2 * bit) for bit in (1, 2, 3)]

    def swap(parts):
        both = []
        for part in parts:
            both += [part, to(part, "dp", 1)]
        return both

    in_parts = [ffn_in[:, D * c : D * (c + 1)] for c in range(CHUNKS)]
    if by_hand:
        first = (time_weight, attn_query, attn_key, attn_value)
        second = (attn_out, cross_query, cross_key, cross_value, cross_out)
        (own1,) = call(pack, "pack_one", (me,) + first, [sds((4, rows, D))], limit=4)
        plane1 = plane(own1)
        mem_keep, mem_send = call(
            take, "take_memory", (me, after(memory, own1)), [sds((2,) + memory.shape[1:])] * 2, limit=8
        )
        (own2,) = call(pack, "pack_two", (me,) + second, [sds((5, rows, D))], limit=4)
        (own3,) = call(pack, "pack_three", (me, ffn_in, ffn_out), [sds((2 * CHUNKS, rows, D))], limit=8)
        near = to(mem_send, "mem", 1)
        *plane1, near, own2, own3 = lax.optimization_barrier(tuple(plane1[1:]) + (near, own2, own3))
        (passed,) = call(join, "join_memory", (me, mem_keep, near), [sds(mem_keep.shape)], limit=8)
        across = to(passed, "mem", 2)
        g1 = [own1, to(own1, "dp", 1)]
        for part in plane1:
            g1 += [part, to(part, "dp", 1)]
        mem_rows = [late(mem_keep, 1, 1), late(near, 1, 1), late(across)]
        own2 = after(own2, *g1)
        g2 = plane(own2)
        g3 = lax.all_gather(own3, "dp", axis=0, tiled=False)
    else:

        def gather(parts):
            got = lax.all_gather(jnp.stack(parts, 0), "dp", axis=0, tiled=False)
            return got.transpose(1, 0, 2, 3).reshape(1, len(parts), D, D)

        g1 = [gather((time_weight, attn_query, attn_key, attn_value))]
        g2 = [gather((attn_out, cross_query, cross_key, cross_value, cross_out))]
        whole_out = lax.all_gather(ffn_out, "dp", axis=0, tiled=True).reshape(1, CHUNKS, D, D)
        g3 = jnp.concatenate([gather(in_parts), whole_out], axis=1)
        mem_rows = [late(lax.all_to_all(memory, "mem", split_axis=0, concat_axis=1, tiled=True))]
    signal = step_signal(timesteps, D).astype(BF)
    sig = jnp.broadcast_to(signal, (8, D))

    nat = pl.BlockSpec((n, PAIR), lambda i: (0, i))
    paired = lambda m: sds((PAIRS, m, PAIR), BF, pl.BlockSpec((1, m, PAIR), lambda i: (i, 0, 0)))
    nat_r = pl.BlockSpec((r, PAIR), lambda i: (0, i))
    rows2 = pl.BlockSpec((1, 2, n), lambda i: (i, 0, 0))
    wide = lambda m: pltpu.VMEM((PAIRS, m, PAIR), BF)
    tall = lambda m: pltpu.VMEM((PAIRS, PAIR, m), BF)
    weight = pltpu.VMEM((D, D), BF)
    weights = lambda count: pltpu.VMEM((count, D, D), BF)
    proj = 2 * n * D * D * 1.5
    att_cost = 2 * n * r * D * 5
    lse_out = sds((PAIRS, 2, n), F32, rows2)
    four_weights = sds((4, D, D), BF, pl.BlockSpec((1, D, D), lambda i: (i, 0, 0)))
    emb, n1, q, k, v, lse1, attended, held1 = call(
        self_forward, "self_forward", (me, x, sig, gains, g1),
        [sds((1, D), F32)] + [paired(n)] * 4 + [lse_out, paired(n), four_weights],
        [weights(4), wide(n), wide(n), wide(n), wide(n), tall(n), tall(n), tall(n), pltpu.SMEM((PAIRS,), jnp.int32)],
        PAIRS, 3 * proj + 2 * att_cost, 36, True,
    )
    if by_hand:
        attended, *g2 = lax.optimization_barrier((attended,) + tuple(g2))
        g2 = swap(g2)
    mid, n2, cq, ck, cv, lse2, crossed, held2 = call(
        cross_forward, "cross_forward", (me, x, emb, attended, mem_rows, gains, g2),
        [sds((n, D), F32, nat)] + [paired(n)] * 2 + [paired(r)] * 2 + [lse_out, paired(n), four_weights],
        [weights(4), pltpu.VMEM((PAIRS, n, PAIR), F32), wide(n), wide(n), wide(r), wide(r), tall(n), tall(r), tall(n),
         pltpu.SMEM((PAIRS,), jnp.int32)],
        PAIRS, 4 * proj + 2 * att_cost, 42, True,
    )
    if by_hand:
        weight_of = lambda t: [(p, pl.BlockSpec((1, rows, D), lambda i: (t, 0, 0))) for p in g2]
        raw_of = lambda count: [sds((dp // 2, mem_count, count * rows, cols))] * 2
        raw3_of = sds((dp, mem_count, 2 * CHUNKS * rows, cols))
    else:
        weight_of = lambda t: [(g2[0], pl.BlockSpec((1, 1, D, D), lambda i: (0, t, 0, 0)))]
        raw_of = lambda count: [sds((count, D, D))]
        raw3_of = sds((2 * CHUNKS, D, D))
    out, gl, bt, gain3, raw3 = call(
        feed_forward, "feed_forward", (me, mid, crossed, late(cot), gains, weight_of(4), late(g3)),
        [sds((n, D), BF, EARLY), sds((n, D), F32, EARLY), sds((n, D), BF, EARLY), sds((1, D), F32), sds(*raw3_of[:2], pl.BlockSpec(memory_space=pl.ANY))],
        [weights(1), weight, weight, pltpu.VMEM((n, D), BF), pltpu.VMEM((D, n), BF)] + [pltpu.VMEM((n, D), F32)] * 3
        + [pltpu.VMEM((2, n, D), BF)] * 2 + [pltpu.VMEM(raw3_of[0], BF), pltpu.SemaphoreType.DMA((CHUNKS, 2))],
        CHUNKS + 1, 25 * proj, 44, True,
    )
    back_scratch = lambda m, mats: [
        weights(mats), tall(n), tall(m), wide(n), tall(n), pltpu.VMEM((PAIRS, 2, n), F32),
        wide(n), wide(m), wide(m), weights(5), pltpu.VMEM((D, max(n, m)), BF),
    ]
    of_held2 = lambda t: (held2, pl.BlockSpec((1, D, D), lambda i: (t, 0, 0), pipeline_mode=pl.Buffered(1)))
    raw2, gm, b1, gain2, gk, gv = call(
        cross_back, "cross_back",
        (me, bt, crossed, late(cq), late(ck), late(cv), (lse2, rows2), mem_rows, late(n2), late(mid), late(gl), gains,
         weight_of(4), of_held2(1), late(attended)),
        [raw_of(5), sds((n, D), F32, EARLY), sds((n, D), BF, EARLY), sds((1, D), F32), sds((r, D), BF, nat_r),
         sds((r, D), BF, nat_r)],
        back_scratch(r, 1), PAIRS, 8 * proj + 5 * att_cost, 56, True,
    )
    if by_hand:
        got2 = to(raw2[1], "dp", 1)
        grad_of = [sds(memory.shape[1:]), sds(memory.shape[1:]), sds((2,) + memory.shape[1:])]
    else:
        grad_of = [sds((r, D))]
    (mem_grad,) = call(
        memory_back, "memory_back", (me, gk, gv, of_held2(2), of_held2(3)), [grad_of], (), 1, 0, 32, True,
    )
    if by_hand:
        got2 = after(got2, mem_grad[2])
        (parts2,) = call(add_core, "cross_core", (me, raw2[0], got2), [[sds((mem_count, 5 * rows, cols))] * 4], limit=24)
        b1, mem_grad[2], *parts2 = lax.optimization_barrier((b1, mem_grad[2]) + tuple(parts2))
        parts2 = [parts2[0]] + [to(parts2[b], "dp", 2 * b) for b in (1, 2, 3)]
        across = to(mem_grad[2], "mem", 2)
    raw1, input_grad, sums = call(
        self_back, "self_back",
        (me, b1, attended, late(q), late(k), late(v), (lse1, rows2), late(n1), late(held1), of_held2(0),
         late(x), emb, late(gm), gains, sig, gain2, gain3),
        [raw_of(3), sds((n, D), BF, EARLY), sds((SMALL, 128)) if by_hand else sds((8, D), F32)],
        back_scratch(n, 1)[1:] + [pltpu.VMEM((2, D), F32)], PAIRS, 7 * proj + 5 * att_cost, 50, True,
    )
    if by_hand:
        keep, send = raw1
        got1, small1 = to(send, "dp", 1), to(sums, "dp", 1)
        done3 = lax.psum_scatter(raw3, "dp", scatter_dimension=0, tiled=False)
        done3, sums = lax.optimization_barrier((done3, sums))
        done3 = lax.psum_scatter(done3, "mem", scatter_dimension=0, tiled=False)
        done3 = pltpu.with_memory_space_constraint(done3, pltpu.HBM)
        sums, *parts2 = lax.optimization_barrier((sums,) + tuple(parts2))
        (passed,) = call(join, "join_grad", (me, mem_grad[1], after(across, *parts2)), [sds(across.shape)], limit=8, flops=6e9)
        sums, keep, passed = lax.optimization_barrier((sums, keep, passed))

    limit = math.sqrt(9 * D * D + 2 * D * FF + 3 * D)
    if not by_hand:
        memory_grad = lax.all_to_all(mem_grad[0][None], "mem", split_axis=1, concat_axis=0, tiled=True)

        def scatter(raw):
            part = lax.psum_scatter(raw, "dp", scatter_dimension=1, tiled=True)
            part = lax.psum_scatter(part, "mem", scatter_dimension=2, tiled=True)
            return [part[t].astype(F32) for t in range(raw.shape[0])]

        d_in = scatter(raw3[:CHUNKS].transpose(1, 0, 2).reshape(1, D, FF))[0]
        d_fout = scatter(raw3[CHUNKS:].reshape(1, FF, D))[0]
        d_query, d_key, d_value = scatter(raw1[0])
        d_cout, d_cquery, d_ckey, d_cvalue, d_out = scatter(raw2[0])
        everyone = lax.all_gather(sums, ("dp", "mem"), axis=0, tiled=False)
        my_signal = lax.dynamic_slice_in_dim(everyone[:, 1], my_dp * rows, rows, axis=1)
        my_sums = lax.dynamic_slice_in_dim(everyone[:, 0], my_mem * cols, cols, axis=1)
        d_time = jnp.dot(my_signal.T, my_sums, precision=lax.Precision.HIGHEST)
        all_gains = jnp.sum(everyone[:, 2:5], axis=0)
        d_gains = lax.dynamic_slice_in_dim(all_gains, my_dp * rows, rows, axis=1).T
        weights = [d_time, d_query, d_key, d_value, d_out, d_cquery, d_ckey, d_cvalue, d_cout, d_in, d_fout]
        local = sum(jnp.sum(w * w) for w in weights)
        squares = lax.psum(local, ("dp", "mem")) + jnp.sum(all_gains * all_gains)
        factor = jnp.minimum(1.0, limit * lax.rsqrt(squares))
        return (
            (out[None], input_grad[None], memory_grad) + tuple(w * factor for w in weights) + (d_gains * factor,)
        )

    parts1 = call(
        add_core_small, "attn_core", (me, keep, got1, sums, small1),
        [sds((mem_count * 3 * rows + SMALL, cols))] * 4, limit=16,
    )
    parts1 = [parts1[0]] + [to(parts1[b], "dp", 2 * b) for b in (1, 2, 3)]
    parts = call(
        add_plane, "plane_sums", (me, parts1, parts2), [sds((8 * rows + SMALL, cols))] * mem_count, limit=24, hbm=False
    )
    last, done3 = lax.optimization_barrier((parts[3], done3))
    parts = [parts[0], to(parts[1], "mem", 1), to(parts[2], "mem", 2), to(last, "mem", 3)]
    done1, done2, d_time, d_gains, local = call(
        add_all, "add_all", (me, parts, done3),
        [sds((3 * rows, cols), F32), sds((5 * rows, cols), F32), sds((rows, cols), F32), sds((8, cols), F32),
         sds((8, cols), F32)],
        limit=16,
    )
    near = to(after(passed, local), "mem", 1)
    local = local + to(local, "dp", 1)
    local = local + to(local, "dp", 2) + to(local, "dp", 4) + to(local, "dp", 6)
    planes = [local] + [to(local, "mem", b) for b in (1, 2, 3)]
    shapes = [(rows, cols)] * 9 + [(rows, FF // mem_count), (FF // dp, cols), (3, rows)]
    memory_grad, *scaled = call(
        scale_all, "scale_all", [me] + planes + [d_time, d_gains, done1, done2, done3, mem_grad[0], across, near],
        [sds(memory.shape)] + [sds(s, F32) for s in shapes], limit=20,
    )
    return (out[None], input_grad[None], memory_grad) + tuple(scaled[:-1]) + (scaled[-1].T,)


def solution(mesh):
    tokens = P(("dp", "mem"), None, None)
    weight = P("dp", None)
    in_specs = (tokens, P(("dp", "mem")), P("dp", "mem", None), tokens) + (weight,) * 11 + (P(),)
    out_specs = (tokens, tokens, P("dp", "mem", None)) + (P("dp", "mem"),) * 11 + (P("dp", None),)
    return jax.shard_map(per_device, mesh=mesh, in_specs=in_specs, out_specs=out_specs, check_vma=False)
```

```python
import functools
import math

import jax
import jax.numpy as jnp
from jax import lax
from jax.experimental import pallas as pl
from jax.experimental.pallas import tpu as pltpu
from jax.sharding import PartitionSpec as P

D = 512
HEADS = 8
HEAD = 64
FF = 2048
PAIRS = HEADS // 2
PAIR = 2 * HEAD
CHUNKS = FF // D
BF = jnp.bfloat16
F32 = jnp.float32
SCALE = 1.0 / math.sqrt(HEAD)
ROOT_HALF = math.sqrt(0.5)
BELL = 1.0 / math.sqrt(2.0 * math.pi)


def dot(a, b, ca=1, cb=0):
    return lax.dot_general(a, b, (((ca,), (cb,)), ((), ())), preferred_element_type=F32)


def row_mean(v):
    return jnp.sum(v, axis=-1, keepdims=True) * (1.0 / v.shape[-1])


def norm_parts(v):
    centred = v - row_mean(v)
    scale = lax.rsqrt(row_mean(centred * centred) + 1e-05)
    return centred * scale, scale


def norm_back(v, gain, grad):
    normed, scale = norm_parts(v)
    c = grad * gain
    gain_part = jnp.sum(grad * normed, axis=0, keepdims=True)
    return scale * (c - row_mean(c) - normed * row_mean(c * normed)), gain_part


def build(w, slot, parts, which, me):
    dst = w.at[slot]
    if len(parts) == 1:
        blocks, _, rows, _ = parts[0].shape
        for b in range(blocks):
            dst[rows * b : rows * (b + 1), :] = parts[0][b, which]
        return
    rows = parts[0].shape[1]
    for r, part in enumerate(parts):
        lo = pl.multiple_of((r ^ me) * rows, rows)
        dst[pl.ds(lo, rows), :] = part[which]


def put(refs, at, mat, core):
    mat = mat.astype(refs[0].dtype)
    if len(refs) == 1:
        refs[0][at] = mat
        return
    half, cb, _, cols = refs[0].shape
    rows = D // (2 * half)

    def cut(own, other):
        for a in range(2 * half):
            ref = own if a % 2 == 0 else other
            for j in range(cb):
                ref[a // 2, j, rows * at : rows * (at + 1), :] = mat[
                    rows * a : rows * (a + 1), cols * j : cols * (j + 1)
                ]

    @pl.when(core == 0)
    def _():
        cut(refs[0], refs[1])

    @pl.when(core == 1)
    def _():
        cut(refs[1], refs[0])


ROWS = 512


def each_block(total, step, body):
    def run(b, carry):
        body(pl.ds(pl.multiple_of(b * step, step), step))
        return carry

    lax.fori_loop(0, total // step, run, 0)


SAFE = 1444.0


def judge(flags, qT, k):
    line = lax.broadcasted_iota(jnp.int32, (8, PAIR), 0)
    lane = lax.broadcasted_iota(jnp.int32, (8, PAIR), 1)
    mine = jnp.where((lane // HEAD) == line, 1.0, 0.0).astype(BF)
    for p in range(PAIRS):
        of_q = jnp.max(dot(mine, qT[p] * qT[p]), axis=1, keepdims=True)
        of_k = jnp.max(dot(mine, k[p] * k[p], 1, 1), axis=1, keepdims=True)
        flags[p] = jnp.where(jnp.max(of_q * of_k) <= SAFE, 1, 0)


def attend(i, flags, qT, k, vT, oT, lse):
    n = qT.shape[2]
    row = lax.broadcasted_iota(jnp.int32, (PAIR, n), 0)
    zero = jnp.zeros((), BF)

    def run(shifted):
        scores = [dot(k[i], jnp.where((row // HEAD) == h, qT[i], zero)) for h in range(2)]
        for h in range(2):
            own = slice(HEAD * h, HEAD * (h + 1))
            score = scores[h]
            top = jnp.max(score, axis=0, keepdims=True) if shifted else None
            e = jnp.exp(score - top if shifted else score)
            total = jnp.sum(e, axis=0, keepdims=True)
            out = dot(vT[i, own, :], e.astype(BF))
            oT[i, own, :] = (out * (1.0 / total)).astype(BF)
            lse[0, h : h + 1, :] = top + jnp.log(total) if shifted else jnp.log(total)

    @pl.when(flags[i] == 1)
    def _():
        run(False)

    @pl.when(flags[i] == 0)
    def _():
        run(True)


def attend_back(i, q, qT, k, kT, v, g, gT, lse, delta, dq, dk, dv):
    n = qT.shape[2]
    block = min(n, 512)
    row = lax.broadcasted_iota(jnp.int32, (PAIR, block), 0)
    lane = lax.broadcasted_iota(jnp.int32, (block, PAIR), 1)
    zero = jnp.zeros((), BF)
    total_k = total_v = None
    for j in range(n // block):
        at = slice(j * block, (j + 1) * block)
        turned = []
        for h in range(2):
            own = slice(HEAD * h, HEAD * (h + 1))
            s = dot(k[i], jnp.where((row // HEAD) == h, qT[i, :, at], zero))
            dp = dot(v[i], jnp.where((row // HEAD) == h, gT[i, :, at], zero))
            p = jnp.exp(s - lse[0, h : h + 1, at])
            ds = (p * (dp - delta[i, h : h + 1, at])).astype(BF)
            one_v = dot(p.astype(BF), jnp.where((lane // HEAD) == h, g[i, at, :], zero))
            one_k = dot(ds, jnp.where((lane // HEAD) == h, q[i, at, :], zero))
            turned.append((dot(kT[i, own, :], ds) * SCALE).astype(BF))
            total_v = one_v if total_v is None else total_v + one_v
            total_k = one_k if total_k is None else total_k + one_k
        dq[i, at, :] = jnp.concatenate(turned, axis=0).T
    dk[i] = (total_k * SCALE).astype(BF)
    dv[i] = total_v.astype(BF)


def prepare(p, q, k, g, heads, qT, kT, gT, delta):
    qT[p] = q[p].T * jnp.asarray(SCALE, BF)
    kT[p] = k[p].T
    gT[p] = g[p].T
    both = gT[p].astype(F32) * heads[p].T.astype(F32)
    for h in range(2):
        delta[p, h : h + 1, :] = jnp.sum(both[HEAD * h : HEAD * (h + 1), :], axis=0, keepdims=True)


def products(refs, first, leftT, rights, core, whole):
    def run(b, carry):
        rows = pl.ds(pl.multiple_of(b * ROWS, ROWS), ROWS)
        for t, right in enumerate(rights):
            whole[first + t, rows, :] = dot(leftT[rows, :], from_pairs(right)).astype(BF)
        return carry

    lax.fori_loop(0, D // ROWS, run, 0)
    for t in range(len(rights)):
        put(refs, first + t, whole[first + t], core)


def turn_pairs(dst, src):
    for p in range(PAIRS):
        dst[PAIR * p : PAIR * (p + 1), :] = src[p].T


def pairs_at(dst, rows, src):
    for p in range(PAIRS):
        dst[p, rows, :] = src[:, PAIR * p : PAIR * (p + 1)]


def joined(src, rows):
    return jnp.concatenate([src[p, rows, :] for p in range(PAIRS)], axis=1)


def pairs_in(dst, src):
    for p in range(PAIRS):
        dst[p] = src[:, PAIR * p : PAIR * (p + 1)]


def from_pairs(src):
    return jnp.concatenate([src[p] for p in range(PAIRS)], axis=1)


def from_pairs_T(src):
    return jnp.concatenate([src[p].T for p in range(PAIRS)], axis=1)


def rows_of(mem):
    parts = [m[t] for m in mem for t in range(m.shape[0])]
    return jnp.concatenate(parts, axis=0) if len(parts) > 1 else parts[0]


def self_forward(me, x, sig, gains, g1, emb, n1, q, k, v, lse, att, held, w, n1s, qs, ks, vs, qT, vT, oT, flags):
    i = pl.program_id(0)

    @pl.when(i == 0)
    def _():
        build(w, 0, g1, 0, me[0])
        embedded = dot(sig[...], w[0])[0:1, :]
        emb[...] = embedded
        resid = x[...].astype(F32) + embedded
        normed = (norm_parts(resid)[0] * gains[0:1, :]).astype(BF)
        pairs_in(n1s, normed)
        for t, dst in ((1, qs), (2, ks), (3, vs)):
            build(w, t, g1, t, me[0])
            pairs_in(dst, dot(normed, w[t]).astype(BF))
        for p in range(PAIRS):
            qT[p] = qs[p].T * jnp.asarray(SCALE, BF)
            vT[p] = vs[p].T
        judge(flags, qT, ks)

    attend(i, flags, qT, ks, vT, oT, lse)
    held[0] = w[i]
    n1[0] = n1s[i]
    q[0] = qs[i]
    k[0] = ks[i]
    v[0] = vs[i]
    att[0] = oT[i].T


def cross_forward(
    me, x, emb, att, mem, gains, g2, mid, n2, cq, k, v, lse, crossed, held, w, mids, n2s, qs, ks, vs, qT, vT, oT, flags
):
    i = pl.program_id(0)

    @pl.when(i == 0)
    def _():
        fetch(*mem)
        build(w, 0, g2, 0, me[0])
        new = x[...].astype(F32) + emb[...] + dot(from_pairs(att), w[0])
        pairs_in(mids, new)
        normed = (norm_parts(new)[0] * gains[1:2, :]).astype(BF)
        pairs_in(n2s, normed)
        build(w, 1, g2, 1, me[0])
        pairs_in(qs, dot(normed, w[1]).astype(BF))
        wait(*mem)
        rows = rows_of([m.ref for m in mem])
        for t, dst in ((2, ks), (3, vs)):
            build(w, t, g2, t, me[0])
            pairs_in(dst, dot(rows, w[t]).astype(BF))
        for p in range(PAIRS):
            qT[p] = qs[p].T * jnp.asarray(SCALE, BF)
            vT[p] = vs[p].T
        judge(flags, qT, ks)

    attend(i, flags, qT, ks, vT, oT, lse)
    held[0] = w[i]
    mid[...] = mids[i]
    n2[0] = n2s[i]
    cq[0] = qs[i]
    k[0] = ks[i]
    v[0] = vs[i]
    crossed[0] = oT[i].T


def feed_forward(
    me, mid, crossed, cot, gains, g2, g3,
    out, gl, bt, gain3, raw_out_ref,
    wlate, win, wout, n3, n3T, late, acc, gacc, active, grad_inner, raw, sems,
):
    i = pl.program_id(0)
    blocks, _, rows, _ = g3.ref.shape
    n = mid.shape[0]
    each = max(blocks // CHUNKS, 1)
    now, before = i % 2, (i + 1) % 2
    piece = D // (n // 512)

    @pl.when(i == 0)
    def _():
        fetch(cot, g3)
        build(wlate, 0, g2, 0, me[0])

        def enter(at):
            new = mid[at, :] + dot(joined(crossed, at), wlate[0])
            late[at, :] = new
            normed = (norm_parts(new)[0] * gains[2:3, :]).astype(BF)
            n3[at, :] = normed
            n3T[:, at] = normed.T
            acc[at, :] = new
            gacc[at, :] = jnp.zeros((ROWS, D), F32)

        each_block(n, ROWS, enter)
        wait(cot, g3)

    @pl.when(i < CHUNKS)
    def _():
        for b in range(blocks):
            win[rows * b : rows * (b + 1), :] = g3.ref[b, i]
        if blocks == 1:
            wout[...] = g3.ref[0, CHUNKS + i]
        else:
            for u in range(each):
                for t in range(CHUNKS):
                    lo = rows * (CHUNKS * u + t)
                    wout[lo : lo + rows, :] = g3.ref[each * i + u, CHUNKS + t]

    def hidden(at):
        inner = dot(n3[at, :], win[...])
        grad_active = dot(cot.ref[at, :], wout[...], 1, 1)
        share = 0.5 * (1.0 + lax.erf(inner * ROOT_HALF))
        act = (inner * share).astype(BF)
        active[now, at, :] = act
        acc[at, :] += dot(act, wout[...])
        slope = share + inner * (jnp.exp(-0.5 * inner * inner) * BELL)
        grad = (slope * grad_active).astype(BF)
        grad_inner[now, at, :] = grad
        gacc[at, :] += dot(grad, win[...], 1, 1)

    def weights(b):
        c = i - 1
        at = pl.ds(pl.multiple_of(b * piece, piece), piece)
        raw_in = dot(n3T[at, :], grad_inner[before]).astype(BF)
        raw_out = dot(active[before, :, at], cot.ref[...], 0, 0).astype(BF)
        if blocks == 1:
            raw[c, at, :] = raw_in
            raw[CHUNKS + c, at, :] = raw_out
            return
        cols = D // CHUNKS
        for a in range(piece // rows):
            for t in range(CHUNKS):
                raw[(piece // rows) * b + a, c, rows * t : rows * (t + 1), :] = raw_in[
                    rows * a : rows * (a + 1), cols * t : cols * (t + 1)
                ]
        tall = D // each
        split = tall // piece
        lo = tall + (b % split) * piece
        for j in range(CHUNKS):
            raw[each * c + b // split, j, pl.ds(pl.multiple_of(lo, piece), piece), :] = raw_out[
                :, cols * j : cols * (j + 1)
            ]

    @pl.when(i == 0)
    def _():
        each_block(n, 512, hidden)

    @pl.when((i > 0) & (i < CHUNKS))
    def _():
        def both(b, carry):
            weights(b)
            hidden(pl.ds(pl.multiple_of(b * 512, 512), 512))
            return carry

        lax.fori_loop(0, n // 512, both, 0)

    @pl.when(i == CHUNKS)
    def _():
        def only(b, carry):
            weights(b)
            return carry

        lax.fori_loop(0, n // 512, only, 0)

    def copies(c):
        if blocks == 1:
            return [
                pltpu.make_async_copy(raw.at[at], raw_out_ref.at[at], sems.at[c, k])
                for k, at in enumerate((c, CHUNKS + c))
            ]
        tall = D // each
        first = (slice(None), c, pl.ds(0, tall))
        second = (pl.ds(each * c, each), slice(None), pl.ds(tall, tall))
        return [
            pltpu.make_async_copy(raw.at[at], raw_out_ref.at[at], sems.at[c, k])
            for k, at in enumerate((first, second))
        ]

    @pl.when(i > 0)
    def _():
        for copy in copies(i - 1):
            copy.start()

    @pl.when(i == CHUNKS)
    def _():
        gain3[...] = jnp.zeros_like(gain3)

        def leave(at):
            out.ref[at, :] = acc[at, :].astype(BF)
            part, gain_part = norm_back(late[at, :], gains[2:3, :], gacc[at, :])
            gain3[...] += gain_part
            total = cot.ref[at, :].astype(F32) + part
            gl.ref[at, :] = total
            bt.ref[at, :] = total.astype(BF)
            for one in (out, gl, bt):
                one.copy(at.start // ROWS).start()

        each_block(n, ROWS, leave)
        for one in (out, gl, bt):
            one.finish()
        for c in range(CHUNKS):
            for copy in copies(c):
                copy.wait()


def start_back(branch, weight, g):
    def enter(rows):
        pairs_at(g, rows, dot(branch[rows, :], weight[...], 1, 1).astype(BF))

    each_block(branch.shape[0], ROWS, enter)


def cross_back(
    me, bt, crossed, late_q, late_k, late_v, lse, mem, n2, mid, gl, gains, g2_out, w_query, att,
    raw, gm, b1, gain2, gk, gv,
    w, qT, kT, g, gT, delta, dq, dk, dv, whole, leftT,
):
    i = pl.program_id(0)
    core = me[0] % 2
    q, k, v = late_q.ref, late_k.ref, late_v.ref
    turned = (q, k, g, crossed, qT, kT, gT, delta)

    @pl.when(i == 0)
    def _():
        fetch(late_q, late_k, late_v)
        build(w, 0, g2_out, 0, me[0])
        start_back(bt, w.at[0], g)
        turn_pairs(leftT, crossed)
        wait(late_q, late_k, late_v)
        prepare(0, *turned)

        def run(b, carry):
            rows = pl.ds(pl.multiple_of(b * ROWS, ROWS), ROWS)
            whole[0, rows, :] = dot(leftT[rows, 0 : bt.shape[0]], bt[...]).astype(BF)
            return carry

        lax.fori_loop(0, D // ROWS, run, 0)
        put(raw, 0, whole[0], core)

    @pl.when(i == 1)
    def _():
        fetch(*mem, n2, mid, gl, att)

    attend_back(i, q, qT, k, kT, v, g, gT, lse, delta, dq, dk, dv)
    prepare(jnp.minimum(i + 1, PAIRS - 1), *turned)
    gk[...] = dk[i]
    gv[...] = dv[i]

    @pl.when(i == PAIRS - 1)
    def _():
        wait(*mem, n2, mid, gl, att)
        gain2[...] = jnp.zeros_like(gain2)

        def leave(rows):
            part, gain_part = norm_back(mid.ref[rows, :], gains[1:2, :], dot(joined(dq, rows), w_query[0], 1, 1))
            gain2[...] += gain_part
            total = gl.ref[rows, :] + part
            gm.ref[rows, :] = total
            b1.ref[rows, :] = total.astype(BF)
            for one in (gm, b1):
                one.copy(rows.start // ROWS).start()

        each_block(bt.shape[0], ROWS, leave)
        n, r = dq.shape[1], dk.shape[1]
        turn_pairs(leftT.at[:, 0:n], n2.ref)
        products(raw, 1, leftT.at[:, 0:n], (dq,), core, whole)
        at = 0
        for part in [m.ref[t] for m in mem for t in range(m.ref.shape[0])]:
            leftT[:, at : at + part.shape[0]] = part.T
            at += part.shape[0]
        products(raw, 2, leftT.at[:, 0:r], (dk, dv), core, whole)
        turn_pairs(leftT.at[:, 0:n], att.ref)

        def run(b, carry):
            rows = pl.ds(pl.multiple_of(b * ROWS, ROWS), ROWS)
            whole[4, rows, :] = dot(leftT[rows, 0:n], b1.ref[...]).astype(BF)
            return carry

        lax.fori_loop(0, D // ROWS, run, 0)
        put(raw, 4, whole[4], core)
        for one in (gm, b1):
            one.finish()


def memory_back(me, gk, gv, w_key, w_value, outs):
    back = (dot(gk[...], w_key[0], 1, 1) + dot(gv[...], w_value[0], 1, 1)).astype(BF)
    if len(outs) == 1:
        outs[0][...] = back
        return
    size = back.shape[0] // 4
    parts = [back[size * t : size * (t + 1)] for t in range(4)]
    outs[0][...], outs[1][...] = parts[0], parts[1]
    outs[2][0], outs[2][1] = parts[2], parts[3]


def self_back(
    me, b1, att, late_q, late_k, late_v, lse, n1, held, w_out, x, emb, gm, gains, sig, gain2, gain3,
    raw, grad, outs,
    qT, kT, g, gT, delta, dq, dk, dv, whole, leftT, sums,
):
    i = pl.program_id(0)
    core = me[0] % 2
    q, k, v = late_q.ref, late_k.ref, late_v.ref
    turned = (q, k, g, att, qT, kT, gT, delta)

    @pl.when(i == 0)
    def _():
        fetch(late_q, late_k, late_v)
        start_back(b1, w_out.at[0], g)
        wait(late_q, late_k, late_v)
        prepare(0, *turned)

    @pl.when(i == 1)
    def _():
        fetch(n1, x, gm, held)

    attend_back(i, q, qT, k, kT, v, g, gT, lse, delta, dq, dk, dv)
    prepare(jnp.minimum(i + 1, PAIRS - 1), *turned)

    @pl.when(i == PAIRS - 1)
    def _():
        wait(n1, x, gm, held)
        sums[...] = jnp.zeros_like(sums)

        def leave(rows):
            parts = (joined(dq, rows), joined(dk, rows), joined(dv, rows))
            back = sum(dot(part, held.ref[t + 1], 1, 1) for t, part in enumerate(parts))
            resid = x.ref[rows, :].astype(F32) + emb[...]
            part, gain_part = norm_back(resid, gains[0:1, :], back)
            total = gm.ref[rows, :] + part
            grad.ref[rows, :] = total.astype(BF)
            grad.copy(rows.start // ROWS).start()
            sums[0:1, :] += jnp.sum(total, axis=0, keepdims=True)
            sums[1:2, :] += gain_part

        each_block(b1.shape[0], ROWS, leave)
        turn_pairs(leftT, n1.ref)
        products(raw, 0, leftT, (dq, dk, dv), core, whole)
        small_rows(outs, [sums[0:1, :], sig[0:1, :].astype(F32), sums[1:2, :], gain2[...], gain3[...]])
        grad.finish()


SMALL = 32


def small_rows(outs, rows):
    if outs.shape[1] == D:
        for t, row in enumerate(rows):
            outs[t : t + 1, :] = row
        outs[5:8, :] = jnp.zeros((3, D), F32)
        return
    tile = jnp.concatenate([row[:, 128 * c : 128 * (c + 1)] for row in rows for c in range(D // 128)], axis=0)
    outs[...] = jnp.concatenate([tile, jnp.zeros((SMALL - tile.shape[0], 128), F32)], axis=0).astype(BF)


def pack(me, *refs):
    out = refs[-1]
    rows = out.shape[1]
    at = 0
    for ref in refs[:-1]:
        for c in range(ref.shape[1] // D):
            for r in range(ref.shape[0] // rows):
                out[at] = ref[rows * r : rows * (r + 1), D * c : D * (c + 1)]
                at += 1


def add_core(me, keep, got, outs):
    place = me[0] // 2
    for r, out in enumerate(outs):
        out[...] = keep[r ^ place] + got[r ^ place]


def add_core_small(me, keep, got, mine, other, *outs):
    place = me[0] // 2
    cb, size, cols = keep.shape[1:]
    a, b = mine[...].astype(F32), other[...].astype(F32)
    small = jnp.concatenate([a[0:4], b[0:4], a[4:8], b[4:8], a[8:20] + b[8:20], a[28:32]], axis=0).astype(BF)
    for r, out in enumerate(outs):
        out[0 : cb * size, :] = (keep[r ^ place] + got[r ^ place]).reshape(cb * size, cols)
        out[cb * size :, :] = small


def add_plane(me, parts, cross, *outs):
    more = cross[0].shape[1]
    size = outs[0].shape[0] - SMALL - more
    cb = (parts[0].shape[0] - SMALL) // size
    small = [p[cb * size :, :].astype(F32) for p in parts]
    gains = small[0][16:28] + small[1][16:28] + small[2][16:28] + small[3][16:28]
    line = lax.broadcasted_iota(jnp.int32, (4, 128), 0)

    def pick(rows, which):
        return jnp.sum(jnp.where(line == which, rows, 0.0), axis=0, keepdims=True)

    signals = []
    for p in small:
        for core in range(2):
            row = pick(p[8 + 4 * core : 12 + 4 * core], me[0] // 2)
            turned = jnp.concatenate([row[:, 64:], row[:, :64]], axis=1)
            signals.append(jnp.where(me[0] % 2 == 1, turned, row))
    for r, out in enumerate(outs):
        at = r ^ me[1]
        spot = pl.ds(pl.multiple_of(at * size, size), size)
        total = sum(p[spot, :].astype(F32) for p in parts)
        out[0:size, :] = total.astype(BF)
        out[size : size + more, :] = sum(p[at].astype(F32) for p in cross).astype(BF)
        sums = [pick(p[4 * core : 4 * (core + 1)], at) for p in small for core in range(2)]
        rows = jnp.concatenate(sums + signals + [gains, jnp.zeros((4, 128), F32)], axis=0)
        out[size + more :, :] = rows.astype(BF)


def split(me, src, keep, send):
    for t in range(2):
        keep[t] = src[t ^ me[1]]
        send[t] = src[(2 + t) ^ me[1]]


def add_pair(me, keep, got, own, send):
    own[...] = keep[0] + got[0]
    send[...] = keep[1] + got[1]


def fold(v):
    return jnp.sum((v * v).reshape(-1, 8, v.shape[-1]), axis=0)


def add_all(me, parts, feed, done1, done2, done3, d_time, d_gains, squares):
    size, more = done1.shape[0], done2.shape[0]
    total1 = sum(p[0:size, :].astype(F32) for p in parts)
    done1[...] = total1
    total2 = sum(p[size : size + more, :].astype(F32) for p in parts)
    done2[...] = total2
    small = [p[size + more :, :].astype(F32) for p in parts]
    sums = jnp.concatenate([p[0:8] for p in small], axis=0).astype(BF)
    signals = jnp.concatenate([p[8:16] for p in small], axis=0).astype(BF)
    rows = d_time.shape[0]
    of_time = dot(signals, sums, 0, 0)[0:rows, :]
    d_time[...] = of_time
    gains = small[0][16:28] + small[1][16:28] + small[2][16:28] + small[3][16:28]
    line = lax.broadcasted_iota(jnp.int32, (4, 128), 0)
    lane = lax.broadcasted_iota(jnp.int32, (1, 128), 1)
    mine = []
    for t in range(3):
        row = jnp.sum(jnp.where(line == me[0] // 2, gains[4 * t : 4 * (t + 1)], 0.0), axis=0, keepdims=True)
        row = jnp.where(me[0] % 2 == 1, jnp.concatenate([row[:, 64:], row[:, :64]], axis=1), row)
        mine.append(jnp.where(lane < 64, row, 0.0))
    block = jnp.concatenate(mine + [jnp.zeros((5, 128), F32)], axis=0)
    d_gains[...] = block[0:8, :]
    wide = feed[0][...].astype(F32) + feed[1][...].astype(F32)
    done3[...] = wide
    squares[...] = fold(total1) + fold(total2) + fold(wide) + fold(of_time) + fold(block) * 0.25


def take(me, src, keep, send):
    for t in range(2):
        keep[t] = src[(2 * t) ^ me[1]]
        send[t] = src[(2 * t + 1) ^ me[1]]


def join(me, first, second, out):
    out[0] = first[...] if len(first.shape) == 2 else first[1]
    out[1] = second[1]


def place_rows(me, own, across, near, out):
    out[me[1]] = own[...]
    out[2 ^ me[1]] = across[0]
    out[1 ^ me[1]] = near[0]
    out[3 ^ me[1]] = near[1]


def scale_all(me, s0, s1, s2, s3, d_time, d_gains, a1, a2, a3, own, across, near, placed, *outs):
    place_rows(me, own, across, near, placed)
    squares = jnp.sum(s0[...] + s1[...] + s2[...] + s3[...])
    limit = math.sqrt(9 * D * D + 2 * D * FF + 3 * D)
    factor = jnp.minimum(1.0, limit * lax.rsqrt(jnp.full((8, 128), squares, F32)))[0:1, :]
    o_time, o_q, o_k, o_v, o_out, o_cq, o_ck, o_cv, o_cout, o_in, o_fout, o_gains = outs
    o_time[...] = d_time[...] * factor
    rows = d_time.shape[0]
    for src, dsts in ((a1, (o_q, o_k, o_v)), (a2, (o_cout, o_cq, o_ck, o_cv, o_out))):
        for t, dst in enumerate(dsts):
            dst[...] = src[rows * t : rows * (t + 1), :] * factor
    for t in range(CHUNKS):
        o_in[:, 128 * t : 128 * (t + 1)] = a3[rows * t : rows * (t + 1), :].astype(F32) * factor
    o_fout[...] = a3[rows * CHUNKS :, :].astype(F32) * factor
    o_gains[...] = (d_gains[...] * factor)[0:3, 0 : o_gains.shape[1]]


class Late:
    def __init__(self, src, dst, sems):
        self.src, self.ref, self.sems = src, dst, sems

    def copies(self):
        count = self.sems.shape[0]
        if count == 1:
            whole = pl.ds(0, self.ref.shape[0])
            return [pltpu.make_async_copy(self.src.at[whole], self.ref, self.sems.at[0])]
        return [pltpu.make_async_copy(self.src.at[p], self.ref.at[p], self.sems.at[p]) for p in range(count)]


class Early:
    def __init__(self, src, dst, sems):
        self.ref, self.dst, self.sems = src, dst, sems

    def copy(self, b):
        rows = pl.ds(pl.multiple_of(b * ROWS, ROWS), ROWS)
        return pltpu.make_async_copy(self.ref.at[rows, :], self.dst.at[rows, :], self.sems.at[b])

    def finish(self):
        for b in range(self.sems.shape[0]):
            self.copy(b).wait()


def fetch(*operands):
    for one in operands:
        for copy in one.copies():
            copy.start()


def wait(*operands):
    for one in operands:
        for copy in one.copies():
            copy.wait()


def late(array, parts=1, first=None):
    return (array, None, parts, first or array.shape[0])


EARLY = "early"


def full(shape):
    return pl.BlockSpec(shape, lambda i: (0,) * len(shape), pipeline_mode=pl.Buffered(1))


def call(body, name, args, outs, scratch=(), steps=1, flops=0, limit=48, hbm=False, free=()):
    in_specs = [pl.BlockSpec(memory_space=pltpu.SMEM)]
    arrays = [args[0]]
    groups = [None]

    later = []

    def take_in(a):
        if isinstance(a, tuple) and a[1] is None:
            later.append((len(arrays), a[2], a[3]))
            arrays.append(a[0])
            in_specs.append(pl.BlockSpec(memory_space=pl.ANY))
        elif isinstance(a, tuple):
            arrays.append(a[0])
            in_specs.append(a[1])
        else:
            arrays.append(a)
            in_specs.append(full(a.shape))

    for a in args[1:]:
        nested = isinstance(a, list) and isinstance(a[0], list)
        groups.append([len(b) for b in a] if nested else len(a) if isinstance(a, list) else None)
        for one in sum(a, []) if nested else a if isinstance(a, list) else [a]:
            take_in(one)
    flat = []
    out_groups = []
    for o in outs:
        out_groups.append(len(o) if isinstance(o, list) else None)
        flat += o if isinstance(o, list) else [o]

    early = [k for k, o in enumerate(flat) if o[2] is EARLY]

    def grouped(refs, sizes):
        got, at = [], 0
        for size in sizes:
            if isinstance(size, list):
                got.append(grouped(refs[at : at + sum(size)], size))
                at += sum(size)
            else:
                got.append(refs[at] if size is None else list(refs[at : at + size]))
                at += size or 1
        return got

    def run(*refs):
        n_in, n_out = len(arrays), len(flat)
        refs = list(refs)
        for k in reversed(early):
            sems, held = refs.pop(), refs.pop()
            refs[n_in + k] = Early(held, refs[n_in + k], sems)
        for k, _, _ in reversed(later):
            sems, held = refs.pop(), refs.pop()
            refs[k] = Late(refs[k], held, sems)
        body(
            *grouped(refs[:n_in], groups), *grouped(refs[n_in : n_in + n_out], out_groups), *refs[n_in + n_out :]
        )

    if hbm or body in (pack, take):
        arrays = [
            pltpu.with_memory_space_constraint(a, pltpu.HBM) if math.prod(a.shape) >= 2**14 else a for a in arrays
        ]
    made = lambda s, t, k: (
        pltpu.HBM(s, t) if hbm and math.prod(s) >= 2**14 and k not in free else jax.ShapeDtypeStruct(s, t)
    )
    size = sum(math.prod(a.shape) * a.dtype.itemsize for a in arrays)
    size += sum(math.prod(s) * jnp.dtype(t).itemsize for s, t, _ in flat)
    size = size if flops else 0
    got = pl.pallas_call(
        run,
        grid=(steps,),
        in_specs=in_specs,
        out_specs=tuple(
            full(s) if b is None else pl.BlockSpec(memory_space=pl.ANY) if b is EARLY else b for s, _, b in flat
        ),
        out_shape=tuple(made(s, t, k) for k, (s, t, _) in enumerate(flat)),
        scratch_shapes=list(scratch)
        + [
            one
            for k, parts, first in later
            for one in (pltpu.VMEM((first,) + arrays[k].shape[1:], arrays[k].dtype), pltpu.SemaphoreType.DMA((parts,)))
        ]
        + [
            one
            for k in early
            for one in (pltpu.VMEM(flat[k][0], flat[k][1]), pltpu.SemaphoreType.DMA((flat[k][0][0] // ROWS,)))
        ],
        compiler_params=pltpu.CompilerParams(vmem_limit_bytes=limit * 2**20),
        cost_estimate=pl.CostEstimate(flops=int(flops), bytes_accessed=size, transcendentals=0),
        name=name,
    )(*arrays)
    return grouped(got, out_groups)


def step_signal(step_ids, feat_width):
    half_width = feat_width // 2
    frequency = jnp.exp(-math.log(10000.0) * jnp.arange(half_width, dtype=F32) / half_width)
    angles = step_ids.astype(F32)[:, None] * frequency[None, :]
    return jnp.concatenate([jnp.sin(angles), jnp.cos(angles)], axis=1)


def sds(shape, dtype=BF, block=None):
    return (tuple(shape), dtype, block)


def per_device(
    decoder_input, timesteps, memory, cotangent, time_weight, attn_query, attn_key, attn_value, attn_out,
    cross_query, cross_key, cross_value, cross_out, ffn_in, ffn_out, norm_gains,
):
    dp = lax.axis_size("dp")
    mem_count = lax.axis_size("mem")
    rows = D // dp
    cols = D // mem_count
    by_hand = dp == 8 and mem_count == 4
    x = decoder_input[0]
    cot = cotangent[0]
    n = x.shape[0]
    r = memory.shape[0] * memory.shape[1]
    gains = norm_gains.T
    my_dp, my_mem = lax.axis_index("dp"), lax.axis_index("mem")
    me = jnp.stack([my_dp, my_mem]).astype(jnp.int32)

    def to(value, axis, bit):
        size = lax.axis_size(axis)
        return lax.ppermute(value, axis, [(i, i ^ bit) for i in range(size)])

    def after(value, *others):
        return lax.optimization_barrier((value,) + others)[0]

    def plane(own):
        return [own] + [to(own, "dp", 2 * bit) for bit in (1, 2, 3)]

    def swap(parts):
        both = []
        for part in parts:
            both += [part, to(part, "dp", 1)]
        return both

    in_parts = [ffn_in[:, D * c : D * (c + 1)] for c in range(CHUNKS)]
    if by_hand:
        first = (time_weight, attn_query, attn_key, attn_value)
        second = (attn_out, cross_query, cross_key, cross_value, cross_out)
        (own1,) = call(pack, "pack_one", (me,) + first, [sds((4, rows, D))], limit=4)
        plane1 = plane(own1)
        mem_keep, mem_send = call(
            take, "take_memory", (me, after(memory, own1)), [sds((2,) + memory.shape[1:])] * 2, limit=8
        )
        (own2,) = call(pack, "pack_two", (me,) + second, [sds((5, rows, D))], limit=4)
        (own3,) = call(pack, "pack_three", (me, ffn_in, ffn_out), [sds((2 * CHUNKS, rows, D))], limit=8)
        near = to(mem_send, "mem", 1)
        *plane1, near, own2, own3 = lax.optimization_barrier(tuple(plane1[1:]) + (near, own2, own3))
        (passed,) = call(join, "join_memory", (me, mem_keep, near), [sds(mem_keep.shape)], limit=8)
        across = to(passed, "mem", 2)
        g1 = [own1, to(own1, "dp", 1)]
        for part in plane1:
            g1 += [part, to(part, "dp", 1)]
        mem_rows = [late(mem_keep, 1, 1), late(near, 1, 1), late(across)]
        own2 = after(own2, *g1)
        g2 = plane(own2)
        g3 = lax.all_gather(own3, "dp", axis=0, tiled=False)
    else:

        def gather(parts):
            got = lax.all_gather(jnp.stack(parts, 0), "dp", axis=0, tiled=False)
            return got.transpose(1, 0, 2, 3).reshape(1, len(parts), D, D)

        g1 = [gather((time_weight, attn_query, attn_key, attn_value))]
        g2 = [gather((attn_out, cross_query, cross_key, cross_value, cross_out))]
        whole_out = lax.all_gather(ffn_out, "dp", axis=0, tiled=True).reshape(1, CHUNKS, D, D)
        g3 = jnp.concatenate([gather(in_parts), whole_out], axis=1)
        mem_rows = [late(lax.all_to_all(memory, "mem", split_axis=0, concat_axis=1, tiled=True))]
    signal = step_signal(timesteps, D).astype(BF)
    sig = jnp.broadcast_to(signal, (8, D))

    nat = pl.BlockSpec((n, PAIR), lambda i: (0, i))
    paired = lambda m: sds((PAIRS, m, PAIR), BF, pl.BlockSpec((1, m, PAIR), lambda i: (i, 0, 0)))
    nat_r = pl.BlockSpec((r, PAIR), lambda i: (0, i))
    rows2 = pl.BlockSpec((1, 2, n), lambda i: (i, 0, 0))
    wide = lambda m: pltpu.VMEM((PAIRS, m, PAIR), BF)
    tall = lambda m: pltpu.VMEM((PAIRS, PAIR, m), BF)
    weight = pltpu.VMEM((D, D), BF)
    weights = lambda count: pltpu.VMEM((count, D, D), BF)
    proj = 2 * n * D * D * 1.5
    att_cost = 2 * n * r * D * 5
    lse_out = sds((PAIRS, 2, n), F32, rows2)
    four_weights = sds((4, D, D), BF, pl.BlockSpec((1, D, D), lambda i: (i, 0, 0)))
    emb, n1, q, k, v, lse1, attended, held1 = call(
        self_forward, "self_forward", (me, x, sig, gains, g1),
        [sds((1, D), F32)] + [paired(n)] * 4 + [lse_out, paired(n), four_weights],
        [weights(4), wide(n), wide(n), wide(n), wide(n), tall(n), tall(n), tall(n), pltpu.SMEM((PAIRS,), jnp.int32)],
        PAIRS, 3 * proj + 2 * att_cost, 36, True,
    )
    if by_hand:
        attended, *g2 = lax.optimization_barrier((attended,) + tuple(g2))
        g2 = swap(g2)
    mid, n2, cq, ck, cv, lse2, crossed, held2 = call(
        cross_forward, "cross_forward", (me, x, emb, attended, mem_rows, gains, g2),
        [sds((n, D), F32, nat)] + [paired(n)] * 2 + [paired(r)] * 2 + [lse_out, paired(n), four_weights],
        [weights(4), pltpu.VMEM((PAIRS, n, PAIR), F32), wide(n), wide(n), wide(r), wide(r), tall(n), tall(r), tall(n),
         pltpu.SMEM((PAIRS,), jnp.int32)],
        PAIRS, 4 * proj + 2 * att_cost, 42, True,
    )
    if by_hand:
        weight_of = lambda t: [(p, pl.BlockSpec((1, rows, D), lambda i: (t, 0, 0))) for p in g2]
        raw_of = lambda count: [sds((dp // 2, mem_count, count * rows, cols))] * 2
        raw3_of = sds((dp, mem_count, 2 * CHUNKS * rows, cols))
    else:
        weight_of = lambda t: [(g2[0], pl.BlockSpec((1, 1, D, D), lambda i: (0, t, 0, 0)))]
        raw_of = lambda count: [sds((count, D, D))]
        raw3_of = sds((2 * CHUNKS, D, D))
    out, gl, bt, gain3, raw3 = call(
        feed_forward, "feed_forward", (me, mid, crossed, late(cot), gains, weight_of(4), late(g3)),
        [sds((n, D), BF, EARLY), sds((n, D), F32, EARLY), sds((n, D), BF, EARLY), sds((1, D), F32), sds(*raw3_of[:2], pl.BlockSpec(memory_space=pl.ANY))],
        [weights(1), weight, weight, pltpu.VMEM((n, D), BF), pltpu.VMEM((D, n), BF)] + [pltpu.VMEM((n, D), F32)] * 3
        + [pltpu.VMEM((2, n, D), BF)] * 2 + [pltpu.VMEM(raw3_of[0], BF), pltpu.SemaphoreType.DMA((CHUNKS, 2))],
        CHUNKS + 1, 25 * proj, 44, True,
    )
    back_scratch = lambda m, mats: [
        weights(mats), tall(n), tall(m), wide(n), tall(n), pltpu.VMEM((PAIRS, 2, n), F32),
        wide(n), wide(m), wide(m), weights(5), pltpu.VMEM((D, max(n, m)), BF),
    ]
    of_held2 = lambda t: (held2, pl.BlockSpec((1, D, D), lambda i: (t, 0, 0), pipeline_mode=pl.Buffered(1)))
    raw2, gm, b1, gain2, gk, gv = call(
        cross_back, "cross_back",
        (me, bt, crossed, late(cq), late(ck), late(cv), (lse2, rows2), mem_rows, late(n2), late(mid), late(gl), gains,
         weight_of(4), of_held2(1), late(attended)),
        [raw_of(5), sds((n, D), F32, EARLY), sds((n, D), BF, EARLY), sds((1, D), F32), sds((r, D), BF, nat_r),
         sds((r, D), BF, nat_r)],
        back_scratch(r, 1), PAIRS, 8 * proj + 5 * att_cost, 56, True,
    )
    if by_hand:
        got2 = to(raw2[1], "dp", 1)
        grad_of = [sds(memory.shape[1:]), sds(memory.shape[1:]), sds((2,) + memory.shape[1:])]
    else:
        grad_of = [sds((r, D))]
    (mem_grad,) = call(
        memory_back, "memory_back", (me, gk, gv, of_held2(2), of_held2(3)), [grad_of], (), 1, 0, 32, True,
    )
    if by_hand:
        got2 = after(got2, mem_grad[2])
        (parts2,) = call(add_core, "cross_core", (me, raw2[0], got2), [[sds((mem_count, 5 * rows, cols))] * 4], limit=24)
        b1, mem_grad[2], *parts2 = lax.optimization_barrier((b1, mem_grad[2]) + tuple(parts2))
        parts2 = [parts2[0]] + [to(parts2[b], "dp", 2 * b) for b in (1, 2, 3)]
        across = to(mem_grad[2], "mem", 2)
    raw1, input_grad, sums = call(
        self_back, "self_back",
        (me, b1, attended, late(q), late(k), late(v), (lse1, rows2), late(n1), late(held1), of_held2(0),
         late(x), emb, late(gm), gains, sig, gain2, gain3),
        [raw_of(3), sds((n, D), BF, EARLY), sds((SMALL, 128)) if by_hand else sds((8, D), F32)],
        back_scratch(n, 1)[1:] + [pltpu.VMEM((2, D), F32)], PAIRS, 7 * proj + 5 * att_cost, 50, True,
    )
    if by_hand:
        keep, send = raw1
        got1, small1 = to(send, "dp", 1), to(sums, "dp", 1)
        done3 = lax.psum_scatter(raw3, "dp", scatter_dimension=0, tiled=False)
        done3, sums = lax.optimization_barrier((done3, sums))
        sums, *parts2 = lax.optimization_barrier((sums,) + tuple(parts2))
        (passed,) = call(join, "join_grad", (me, mem_grad[1], after(across, *parts2)), [sds(across.shape)], limit=8, flops=6e9)
        sums, keep, passed = lax.optimization_barrier((sums, keep, passed))

    limit = math.sqrt(9 * D * D + 2 * D * FF + 3 * D)
    if not by_hand:
        memory_grad = lax.all_to_all(mem_grad[0][None], "mem", split_axis=1, concat_axis=0, tiled=True)

        def scatter(raw):
            part = lax.psum_scatter(raw, "dp", scatter_dimension=1, tiled=True)
            part = lax.psum_scatter(part, "mem", scatter_dimension=2, tiled=True)
            return [part[t].astype(F32) for t in range(raw.shape[0])]

        d_in = scatter(raw3[:CHUNKS].transpose(1, 0, 2).reshape(1, D, FF))[0]
        d_fout = scatter(raw3[CHUNKS:].reshape(1, FF, D))[0]
        d_query, d_key, d_value = scatter(raw1[0])
        d_cout, d_cquery, d_ckey, d_cvalue, d_out = scatter(raw2[0])
        everyone = lax.all_gather(sums, ("dp", "mem"), axis=0, tiled=False)
        my_signal = lax.dynamic_slice_in_dim(everyone[:, 1], my_dp * rows, rows, axis=1)
        my_sums = lax.dynamic_slice_in_dim(everyone[:, 0], my_mem * cols, cols, axis=1)
        d_time = jnp.dot(my_signal.T, my_sums, precision=lax.Precision.HIGHEST)
        all_gains = jnp.sum(everyone[:, 2:5], axis=0)
        d_gains = lax.dynamic_slice_in_dim(all_gains, my_dp * rows, rows, axis=1).T
        weights = [d_time, d_query, d_key, d_value, d_out, d_cquery, d_ckey, d_cvalue, d_cout, d_in, d_fout]
        local = sum(jnp.sum(w * w) for w in weights)
        squares = lax.psum(local, ("dp", "mem")) + jnp.sum(all_gains * all_gains)
        factor = jnp.minimum(1.0, limit * lax.rsqrt(squares))
        return (
            (out[None], input_grad[None], memory_grad) + tuple(w * factor for w in weights) + (d_gains * factor,)
        )

    parts1 = call(
        add_core_small, "attn_core", (me, keep, got1, sums, small1),
        [sds((mem_count * 3 * rows + SMALL, cols))] * 4, limit=16,
    )
    parts1 = [parts1[0]] + [to(parts1[b], "dp", 2 * b) for b in (1, 2, 3)]
    two = sds((2, 2 * CHUNKS * rows, cols))
    keep3, send3 = call(split, "feed_split", (me, after(done3, parts1[0])), [two, two], limit=8)
    across3 = to(send3, "mem", 2)
    parts = call(
        add_plane, "plane_sums", (me, parts1, parts2), [sds((8 * rows + SMALL, cols))] * mem_count, limit=24, hbm=False
    )
    across3, *parts = lax.optimization_barrier((across3,) + tuple(parts))
    parts = [parts[0]] + [to(parts[b], "mem", b) for b in (1, 2, 3)]
    one = sds((2 * CHUNKS * rows, cols))
    keep3, send3 = call(add_pair, "feed_across", (me, keep3, across3), [one, one], limit=8)
    feed = [keep3, to(send3, "mem", 1)]
    done1, done2, done3, d_time, d_gains, local = call(
        add_all, "add_all", (me, parts, feed),
        [sds((3 * rows, cols), F32), sds((5 * rows, cols), F32), sds((2 * CHUNKS * rows, cols), F32), sds((rows, cols), F32), sds((8, cols), F32),
         sds((8, cols), F32)],
        limit=16,
    )
    near = to(after(passed, local), "mem", 1)
    local = local + to(local, "dp", 1)
    local = local + to(local, "dp", 2) + to(local, "dp", 4) + to(local, "dp", 6)
    planes = [local] + [to(local, "mem", b) for b in (1, 2, 3)]
    shapes = [(rows, cols)] * 9 + [(rows, FF // mem_count), (FF // dp, cols), (3, rows)]
    memory_grad, *scaled = call(
        scale_all, "scale_all", [me] + planes + [d_time, d_gains, done1, done2, done3, mem_grad[0], across, near],
        [sds(memory.shape)] + [sds(s, F32) for s in shapes], limit=20,
    )
    return (out[None], input_grad[None], memory_grad) + tuple(scaled[:-1]) + (scaled[-1].T,)


def solution(mesh):
    tokens = P(("dp", "mem"), None, None)
    weight = P("dp", None)
    in_specs = (tokens, P(("dp", "mem")), P("dp", "mem", None), tokens) + (weight,) * 11 + (P(),)
    out_specs = (tokens, tokens, P("dp", "mem", None)) + (P("dp", "mem"),) * 11 + (P("dp", None),)
    return jax.shard_map(per_device, mesh=mesh, in_specs=in_specs, out_specs=out_specs, check_vma=False)
```

```python
import functools
import math

import jax
import jax.numpy as jnp
from jax import lax
from jax.experimental import pallas as pl
from jax.experimental.pallas import tpu as pltpu
from jax.sharding import PartitionSpec as P

D = 512
HEADS = 8
HEAD = 64
FF = 2048
PAIRS = HEADS // 2
PAIR = 2 * HEAD
CHUNKS = FF // D
BF = jnp.bfloat16
F32 = jnp.float32
SCALE = 1.0 / math.sqrt(HEAD)
ROOT_HALF = math.sqrt(0.5)
BELL = 1.0 / math.sqrt(2.0 * math.pi)


def dot(a, b, ca=1, cb=0):
    return lax.dot_general(a, b, (((ca,), (cb,)), ((), ())), preferred_element_type=F32)


def row_mean(v):
    return jnp.sum(v, axis=-1, keepdims=True) * (1.0 / v.shape[-1])


def norm_parts(v):
    centred = v - row_mean(v)
    scale = lax.rsqrt(row_mean(centred * centred) + 1e-05)
    return centred * scale, scale


def norm_back(v, gain, grad):
    normed, scale = norm_parts(v)
    c = grad * gain
    gain_part = jnp.sum(grad * normed, axis=0, keepdims=True)
    return scale * (c - row_mean(c) - normed * row_mean(c * normed)), gain_part


def build(w, slot, parts, which, me):
    dst = w.at[slot]
    if len(parts) == 1:
        blocks, _, rows, _ = parts[0].shape
        for b in range(blocks):
            dst[rows * b : rows * (b + 1), :] = parts[0][b, which]
        return
    rows = parts[0].shape[1]
    for r, part in enumerate(parts):
        lo = pl.multiple_of((r ^ me) * rows, rows)
        dst[pl.ds(lo, rows), :] = part[which]


def put(refs, at, mat, core):
    mat = mat.astype(refs[0].dtype)
    if len(refs) == 1:
        refs[0][at] = mat
        return
    half, cb, _, cols = refs[0].shape
    rows = D // (2 * half)

    def cut(own, other):
        for a in range(2 * half):
            ref = own if a % 2 == 0 else other
            for j in range(cb):
                ref[a // 2, j, rows * at : rows * (at + 1), :] = mat[
                    rows * a : rows * (a + 1), cols * j : cols * (j + 1)
                ]

    @pl.when(core == 0)
    def _():
        cut(refs[0], refs[1])

    @pl.when(core == 1)
    def _():
        cut(refs[1], refs[0])


ROWS = 512


def each_block(total, step, body):
    def run(b, carry):
        body(pl.ds(pl.multiple_of(b * step, step), step))
        return carry

    lax.fori_loop(0, total // step, run, 0)


SAFE = 1444.0


def judge(flags, qT, k):
    line = lax.broadcasted_iota(jnp.int32, (8, PAIR), 0)
    lane = lax.broadcasted_iota(jnp.int32, (8, PAIR), 1)
    mine = jnp.where((lane // HEAD) == line, 1.0, 0.0).astype(BF)
    for p in range(PAIRS):
        of_q = jnp.max(dot(mine, qT[p] * qT[p]), axis=1, keepdims=True)
        of_k = jnp.max(dot(mine, k[p] * k[p], 1, 1), axis=1, keepdims=True)
        flags[p] = jnp.where(jnp.max(of_q * of_k) <= SAFE, 1, 0)


def attend(i, flags, qT, k, vT, oT, lse):
    n = qT.shape[2]
    row = lax.broadcasted_iota(jnp.int32, (PAIR, n), 0)
    zero = jnp.zeros((), BF)

    def run(shifted):
        scores = [dot(k[i], jnp.where((row // HEAD) == h, qT[i], zero)) for h in range(2)]
        for h in range(2):
            own = slice(HEAD * h, HEAD * (h + 1))
            score = scores[h]
            top = jnp.max(score, axis=0, keepdims=True) if shifted else None
            e = jnp.exp(score - top if shifted else score)
            total = jnp.sum(e, axis=0, keepdims=True)
            out = dot(vT[i, own, :], e.astype(BF))
            oT[i, own, :] = (out * (1.0 / total)).astype(BF)
            lse[0, h : h + 1, :] = top + jnp.log(total) if shifted else jnp.log(total)

    @pl.when(flags[i] == 1)
    def _():
        run(False)

    @pl.when(flags[i] == 0)
    def _():
        run(True)


def attend_back(i, q, qT, k, kT, v, g, gT, lse, delta, dq, dk, dv):
    n = qT.shape[2]
    block = min(n, 512)
    row = lax.broadcasted_iota(jnp.int32, (PAIR, block), 0)
    lane = lax.broadcasted_iota(jnp.int32, (block, PAIR), 1)
    zero = jnp.zeros((), BF)
    total_k = total_v = None
    for j in range(n // block):
        at = slice(j * block, (j + 1) * block)
        turned = []
        for h in range(2):
            own = slice(HEAD * h, HEAD * (h + 1))
            s = dot(k[i], jnp.where((row // HEAD) == h, qT[i, :, at], zero))
            dp = dot(v[i], jnp.where((row // HEAD) == h, gT[i, :, at], zero))
            p = jnp.exp(s - lse[0, h : h + 1, at])
            ds = (p * (dp - delta[i, h : h + 1, at])).astype(BF)
            one_v = dot(p.astype(BF), jnp.where((lane // HEAD) == h, g[i, at, :], zero))
            one_k = dot(ds, jnp.where((lane // HEAD) == h, q[i, at, :], zero))
            turned.append((dot(kT[i, own, :], ds) * SCALE).astype(BF))
            total_v = one_v if total_v is None else total_v + one_v
            total_k = one_k if total_k is None else total_k + one_k
        dq[i, at, :] = jnp.concatenate(turned, axis=0).T
    dk[i] = (total_k * SCALE).astype(BF)
    dv[i] = total_v.astype(BF)


def prepare(p, q, k, g, heads, qT, kT, gT, delta):
    qT[p] = q[p].T * jnp.asarray(SCALE, BF)
    kT[p] = k[p].T
    gT[p] = g[p].T
    both = gT[p].astype(F32) * heads[p].T.astype(F32)
    for h in range(2):
        delta[p, h : h + 1, :] = jnp.sum(both[HEAD * h : HEAD * (h + 1), :], axis=0, keepdims=True)


def products(refs, first, leftT, rights, core, whole):
    def run(b, carry):
        rows = pl.ds(pl.multiple_of(b * ROWS, ROWS), ROWS)
        for t, right in enumerate(rights):
            whole[first + t, rows, :] = dot(leftT[rows, :], from_pairs(right)).astype(BF)
        return carry

    lax.fori_loop(0, D // ROWS, run, 0)
    for t in range(len(rights)):
        put(refs, first + t, whole[first + t], core)


def turn_pairs(dst, src):
    for p in range(PAIRS):
        dst[PAIR * p : PAIR * (p + 1), :] = src[p].T


def pairs_at(dst, rows, src):
    for p in range(PAIRS):
        dst[p, rows, :] = src[:, PAIR * p : PAIR * (p + 1)]


def joined(src, rows):
    return jnp.concatenate([src[p, rows, :] for p in range(PAIRS)], axis=1)


def pairs_in(dst, src):
    for p in range(PAIRS):
        dst[p] = src[:, PAIR * p : PAIR * (p + 1)]


def from_pairs(src):
    return jnp.concatenate([src[p] for p in range(PAIRS)], axis=1)


def from_pairs_T(src):
    return jnp.concatenate([src[p].T for p in range(PAIRS)], axis=1)


def rows_of(mem):
    parts = [m[t] for m in mem for t in range(m.shape[0])]
    return jnp.concatenate(parts, axis=0) if len(parts) > 1 else parts[0]


def self_forward(me, x, sig, gains, g1, emb, n1, q, k, v, lse, att, held, w, n1s, qs, ks, vs, qT, vT, oT, flags):
    i = pl.program_id(0)

    @pl.when(i == 0)
    def _():
        build(w, 0, g1, 0, me[0])
        embedded = dot(sig[...], w[0])[0:1, :]
        emb[...] = embedded
        resid = x[...].astype(F32) + embedded
        normed = (norm_parts(resid)[0] * gains[0:1, :]).astype(BF)
        pairs_in(n1s, normed)
        for t, dst in ((1, qs), (2, ks), (3, vs)):
            build(w, t, g1, t, me[0])
            pairs_in(dst, dot(normed, w[t]).astype(BF))
        for p in range(PAIRS):
            qT[p] = qs[p].T * jnp.asarray(SCALE, BF)
            vT[p] = vs[p].T
        judge(flags, qT, ks)

    attend(i, flags, qT, ks, vT, oT, lse)
    held[0] = w[i]
    n1[0] = n1s[i]
    q[0] = qs[i]
    k[0] = ks[i]
    v[0] = vs[i]
    att[0] = oT[i].T


def cross_forward(
    me, x, emb, att, mem, gains, g2, mid, n2, cq, k, v, lse, crossed, held, w, mids, n2s, qs, ks, vs, qT, vT, oT, flags
):
    i = pl.program_id(0)

    @pl.when(i == 0)
    def _():
        fetch(*mem)
        build(w, 0, g2, 0, me[0])
        new = x[...].astype(F32) + emb[...] + dot(from_pairs(att), w[0])
        pairs_in(mids, new)
        normed = (norm_parts(new)[0] * gains[1:2, :]).astype(BF)
        pairs_in(n2s, normed)
        build(w, 1, g2, 1, me[0])
        pairs_in(qs, dot(normed, w[1]).astype(BF))
        wait(*mem)
        rows = rows_of([m.ref for m in mem])
        for t, dst in ((2, ks), (3, vs)):
            build(w, t, g2, t, me[0])
            pairs_in(dst, dot(rows, w[t]).astype(BF))
        for p in range(PAIRS):
            qT[p] = qs[p].T * jnp.asarray(SCALE, BF)
            vT[p] = vs[p].T
        judge(flags, qT, ks)

    attend(i, flags, qT, ks, vT, oT, lse)
    held[0] = w[i]
    mid[...] = mids[i]
    n2[0] = n2s[i]
    cq[0] = qs[i]
    k[0] = ks[i]
    v[0] = vs[i]
    crossed[0] = oT[i].T


def feed_forward(
    me, mid, crossed, cot, gains, g2, g3,
    out, gl, bt, gain3, raw_out_ref,
    wlate, win, wout, n3, n3T, late, acc, gacc, active, grad_inner, raw, sems,
):
    i = pl.program_id(0)
    blocks, _, rows, _ = g3.ref.shape
    n = mid.shape[0]
    each = max(blocks // CHUNKS, 1)
    now, before = i % 2, (i + 1) % 2
    piece = D // (n // 512)

    @pl.when(i == 0)
    def _():
        fetch(cot, g3)
        build(wlate, 0, g2, 0, me[0])

        def enter(at):
            new = mid[at, :] + dot(joined(crossed, at), wlate[0])
            late[at, :] = new
            normed = (norm_parts(new)[0] * gains[2:3, :]).astype(BF)
            n3[at, :] = normed
            n3T[:, at] = normed.T
            acc[at, :] = new
            gacc[at, :] = jnp.zeros((ROWS, D), F32)

        each_block(n, ROWS, enter)
        wait(cot, g3)

    @pl.when(i < CHUNKS)
    def _():
        for b in range(blocks):
            win[rows * b : rows * (b + 1), :] = g3.ref[b, i]
        if blocks == 1:
            wout[...] = g3.ref[0, CHUNKS + i]
        else:
            for u in range(each):
                for t in range(CHUNKS):
                    lo = rows * (CHUNKS * u + t)
                    wout[lo : lo + rows, :] = g3.ref[each * i + u, CHUNKS + t]

    def hidden(at):
        inner = dot(n3[at, :], win[...])
        grad_active = dot(cot.ref[at, :], wout[...], 1, 1)
        share = 0.5 * (1.0 + lax.erf(inner * ROOT_HALF))
        act = (inner * share).astype(BF)
        active[now, at, :] = act
        acc[at, :] += dot(act, wout[...])
        slope = share + inner * (jnp.exp(-0.5 * inner * inner) * BELL)
        grad = (slope * grad_active).astype(BF)
        grad_inner[now, at, :] = grad
        gacc[at, :] += dot(grad, win[...], 1, 1)

    def weights(b):
        c = i - 1
        at = pl.ds(pl.multiple_of(b * piece, piece), piece)
        raw_in = dot(n3T[at, :], grad_inner[before]).astype(BF)
        raw_out = dot(active[before, :, at], cot.ref[...], 0, 0).astype(BF)
        if blocks == 1:
            raw[c, at, :] = raw_in
            raw[CHUNKS + c, at, :] = raw_out
            return
        cols = D // CHUNKS
        for a in range(piece // rows):
            for t in range(CHUNKS):
                raw[(piece // rows) * b + a, c, rows * t : rows * (t + 1), :] = raw_in[
                    rows * a : rows * (a + 1), cols * t : cols * (t + 1)
                ]
        tall = D // each
        split = tall // piece
        lo = tall + (b % split) * piece
        for j in range(CHUNKS):
            raw[each * c + b // split, j, pl.ds(pl.multiple_of(lo, piece), piece), :] = raw_out[
                :, cols * j : cols * (j + 1)
            ]

    @pl.when(i == 0)
    def _():
        each_block(n, 512, hidden)

    @pl.when((i > 0) & (i < CHUNKS))
    def _():
        def both(b, carry):
            weights(b)
            hidden(pl.ds(pl.multiple_of(b * 512, 512), 512))
            return carry

        lax.fori_loop(0, n // 512, both, 0)

    @pl.when(i == CHUNKS)
    def _():
        def only(b, carry):
            weights(b)
            return carry

        lax.fori_loop(0, n // 512, only, 0)

    def copies(c):
        if blocks == 1:
            return [
                pltpu.make_async_copy(raw.at[at], raw_out_ref.at[at], sems.at[c, k])
                for k, at in enumerate((c, CHUNKS + c))
            ]
        tall = D // each
        first = (slice(None), c, pl.ds(0, tall))
        second = (pl.ds(each * c, each), slice(None), pl.ds(tall, tall))
        return [
            pltpu.make_async_copy(raw.at[at], raw_out_ref.at[at], sems.at[c, k])
            for k, at in enumerate((first, second))
        ]

    @pl.when(i > 0)
    def _():
        for copy in copies(i - 1):
            copy.start()

    @pl.when(i == CHUNKS)
    def _():
        gain3[...] = jnp.zeros_like(gain3)

        def leave(at):
            out.ref[at, :] = acc[at, :].astype(BF)
            part, gain_part = norm_back(late[at, :], gains[2:3, :], gacc[at, :])
            gain3[...] += gain_part
            total = cot.ref[at, :].astype(F32) + part
            gl.ref[at, :] = total
            bt.ref[at, :] = total.astype(BF)
            for one in (out, gl, bt):
                one.copy(at.start // ROWS).start()

        each_block(n, ROWS, leave)
        for one in (out, gl, bt):
            one.finish()
        for c in range(CHUNKS):
            for copy in copies(c):
                copy.wait()


def start_back(branch, weight, g):
    def enter(rows):
        pairs_at(g, rows, dot(branch[rows, :], weight[...], 1, 1).astype(BF))

    each_block(branch.shape[0], ROWS, enter)


def cross_back(
    me, bt, crossed, late_q, late_k, late_v, lse, mem, n2, mid, gl, gains, g2_out, w_query, att,
    raw, gm, b1, gain2, gk, gv,
    w, qT, kT, g, gT, delta, dq, dk, dv, whole, leftT,
):
    i = pl.program_id(0)
    core = me[0] % 2
    q, k, v = late_q.ref, late_k.ref, late_v.ref
    turned = (q, k, g, crossed, qT, kT, gT, delta)

    @pl.when(i == 0)
    def _():
        fetch(late_q, late_k, late_v)
        build(w, 0, g2_out, 0, me[0])
        start_back(bt, w.at[0], g)
        turn_pairs(leftT, crossed)
        wait(late_q, late_k, late_v)
        prepare(0, *turned)

        def run(b, carry):
            rows = pl.ds(pl.multiple_of(b * ROWS, ROWS), ROWS)
            whole[0, rows, :] = dot(leftT[rows, 0 : bt.shape[0]], bt[...]).astype(BF)
            return carry

        lax.fori_loop(0, D // ROWS, run, 0)
        put(raw, 0, whole[0], core)

    @pl.when(i == 1)
    def _():
        fetch(*mem, n2, mid, gl, att)

    attend_back(i, q, qT, k, kT, v, g, gT, lse, delta, dq, dk, dv)
    prepare(jnp.minimum(i + 1, PAIRS - 1), *turned)
    gk[...] = dk[i]
    gv[...] = dv[i]

    @pl.when(i == PAIRS - 1)
    def _():
        wait(*mem, n2, mid, gl, att)
        gain2[...] = jnp.zeros_like(gain2)

        def leave(rows):
            part, gain_part = norm_back(mid.ref[rows, :], gains[1:2, :], dot(joined(dq, rows), w_query[0], 1, 1))
            gain2[...] += gain_part
            total = gl.ref[rows, :] + part
            gm.ref[rows, :] = total
            b1.ref[rows, :] = total.astype(BF)
            for one in (gm, b1):
                one.copy(rows.start // ROWS).start()

        each_block(bt.shape[0], ROWS, leave)
        n, r = dq.shape[1], dk.shape[1]
        turn_pairs(leftT.at[:, 0:n], n2.ref)
        products(raw, 1, leftT.at[:, 0:n], (dq,), core, whole)
        at = 0
        for part in [m.ref[t] for m in mem for t in range(m.ref.shape[0])]:
            leftT[:, at : at + part.shape[0]] = part.T
            at += part.shape[0]
        products(raw, 2, leftT.at[:, 0:r], (dk, dv), core, whole)
        turn_pairs(leftT.at[:, 0:n], att.ref)

        def run(b, carry):
            rows = pl.ds(pl.multiple_of(b * ROWS, ROWS), ROWS)
            whole[4, rows, :] = dot(leftT[rows, 0:n], b1.ref[...]).astype(BF)
            return carry

        lax.fori_loop(0, D // ROWS, run, 0)
        put(raw, 4, whole[4], core)
        for one in (gm, b1):
            one.finish()


def memory_back(me, gk, gv, w_key, w_value, outs):
    back = (dot(gk[...], w_key[0], 1, 1) + dot(gv[...], w_value[0], 1, 1)).astype(BF)
    if len(outs) == 1:
        outs[0][...] = back
        return
    size = back.shape[0] // 4
    parts = [back[size * t : size * (t + 1)] for t in range(4)]
    outs[0][...], outs[1][...] = parts[0], parts[1]
    outs[2][0], outs[2][1] = parts[2], parts[3]


def self_back(
    me, b1, att, late_q, late_k, late_v, lse, n1, held, w_out, x, emb, gm, gains, sig, gain2, gain3,
    raw, grad, outs,
    qT, kT, g, gT, delta, dq, dk, dv, whole, leftT, sums,
):
    i = pl.program_id(0)
    core = me[0] % 2
    q, k, v = late_q.ref, late_k.ref, late_v.ref
    turned = (q, k, g, att, qT, kT, gT, delta)

    @pl.when(i == 0)
    def _():
        fetch(late_q, late_k, late_v)
        start_back(b1, w_out.at[0], g)
        wait(late_q, late_k, late_v)
        prepare(0, *turned)

    @pl.when(i == 1)
    def _():
        fetch(n1, x, gm, held)

    attend_back(i, q, qT, k, kT, v, g, gT, lse, delta, dq, dk, dv)
    prepare(jnp.minimum(i + 1, PAIRS - 1), *turned)

    @pl.when(i == PAIRS - 1)
    def _():
        wait(n1, x, gm, held)
        sums[...] = jnp.zeros_like(sums)

        def leave(rows):
            parts = (joined(dq, rows), joined(dk, rows), joined(dv, rows))
            back = sum(dot(part, held.ref[t + 1], 1, 1) for t, part in enumerate(parts))
            resid = x.ref[rows, :].astype(F32) + emb[...]
            part, gain_part = norm_back(resid, gains[0:1, :], back)
            total = gm.ref[rows, :] + part
            grad.ref[rows, :] = total.astype(BF)
            grad.copy(rows.start // ROWS).start()
            sums[0:1, :] += jnp.sum(total, axis=0, keepdims=True)
            sums[1:2, :] += gain_part

        each_block(b1.shape[0], ROWS, leave)
        turn_pairs(leftT, n1.ref)
        products(raw, 0, leftT, (dq, dk, dv), core, whole)
        small_rows(outs, [sums[0:1, :], sig[0:1, :].astype(F32), sums[1:2, :], gain2[...], gain3[...]])
        grad.finish()


SMALL = 32


def small_rows(outs, rows):
    if outs.shape[1] == D:
        for t, row in enumerate(rows):
            outs[t : t + 1, :] = row
        outs[5:8, :] = jnp.zeros((3, D), F32)
        return
    tile = jnp.concatenate([row[:, 128 * c : 128 * (c + 1)] for row in rows for c in range(D // 128)], axis=0)
    outs[...] = jnp.concatenate([tile, jnp.zeros((SMALL - tile.shape[0], 128), F32)], axis=0).astype(BF)


def pack(me, *refs):
    out = refs[-1]
    rows = out.shape[1]
    at = 0
    for ref in refs[:-1]:
        for c in range(ref.shape[1] // D):
            for r in range(ref.shape[0] // rows):
                out[at] = ref[rows * r : rows * (r + 1), D * c : D * (c + 1)]
                at += 1


def add_core(me, keep, got, outs):
    place = me[0] // 2
    for r, out in enumerate(outs):
        out[...] = keep[r ^ place] + got[r ^ place]


def add_core_small(me, keep, got, mine, other, *outs):
    place = me[0] // 2
    cb, size, cols = keep.shape[1:]
    a, b = mine[...].astype(F32), other[...].astype(F32)
    small = jnp.concatenate([a[0:4], b[0:4], a[4:8], b[4:8], a[8:20] + b[8:20], a[28:32]], axis=0).astype(BF)
    for r, out in enumerate(outs):
        out[0 : cb * size, :] = (keep[r ^ place] + got[r ^ place]).reshape(cb * size, cols)
        out[cb * size :, :] = small


def add_plane(me, parts, cross, *outs):
    more = cross[0].shape[1]
    size = outs[0].shape[0] - SMALL - more
    cb = (parts[0].shape[0] - SMALL) // size
    small = [p[cb * size :, :].astype(F32) for p in parts]
    gains = small[0][16:28] + small[1][16:28] + small[2][16:28] + small[3][16:28]
    line = lax.broadcasted_iota(jnp.int32, (4, 128), 0)

    def pick(rows, which):
        return jnp.sum(jnp.where(line == which, rows, 0.0), axis=0, keepdims=True)

    signals = []
    for p in small:
        for core in range(2):
            row = pick(p[8 + 4 * core : 12 + 4 * core], me[0] // 2)
            turned = jnp.concatenate([row[:, 64:], row[:, :64]], axis=1)
            signals.append(jnp.where(me[0] % 2 == 1, turned, row))
    for r, out in enumerate(outs):
        at = r ^ me[1]
        spot = pl.ds(pl.multiple_of(at * size, size), size)
        total = sum(p[spot, :].astype(F32) for p in parts)
        out[0:size, :] = total.astype(BF)
        out[size : size + more, :] = sum(p[at].astype(F32) for p in cross).astype(BF)
        sums = [pick(p[4 * core : 4 * (core + 1)], at) for p in small for core in range(2)]
        rows = jnp.concatenate(sums + signals + [gains, jnp.zeros((4, 128), F32)], axis=0)
        out[size + more :, :] = rows.astype(BF)


def fold(v):
    return jnp.sum((v * v).reshape(-1, 8, v.shape[-1]), axis=0)


def add_all(me, parts, feed, done1, done2, d_time, d_gains, squares):
    size, more = done1.shape[0], done2.shape[0]
    total1 = sum(p[0:size, :].astype(F32) for p in parts)
    done1[...] = total1
    total2 = sum(p[size : size + more, :].astype(F32) for p in parts)
    done2[...] = total2
    small = [p[size + more :, :].astype(F32) for p in parts]
    sums = jnp.concatenate([p[0:8] for p in small], axis=0).astype(BF)
    signals = jnp.concatenate([p[8:16] for p in small], axis=0).astype(BF)
    rows = d_time.shape[0]
    of_time = dot(signals, sums, 0, 0)[0:rows, :]
    d_time[...] = of_time
    gains = small[0][16:28] + small[1][16:28] + small[2][16:28] + small[3][16:28]
    line = lax.broadcasted_iota(jnp.int32, (4, 128), 0)
    lane = lax.broadcasted_iota(jnp.int32, (1, 128), 1)
    mine = []
    for t in range(3):
        row = jnp.sum(jnp.where(line == me[0] // 2, gains[4 * t : 4 * (t + 1)], 0.0), axis=0, keepdims=True)
        row = jnp.where(me[0] % 2 == 1, jnp.concatenate([row[:, 64:], row[:, :64]], axis=1), row)
        mine.append(jnp.where(lane < 64, row, 0.0))
    block = jnp.concatenate(mine + [jnp.zeros((5, 128), F32)], axis=0)
    d_gains[...] = block[0:8, :]
    wide = feed[...].astype(F32)
    squares[...] = fold(total1) + fold(total2) + fold(wide) + fold(of_time) + fold(block) * 0.25


def take(me, src, keep, send):
    for t in range(2):
        keep[t] = src[(2 * t) ^ me[1]]
        send[t] = src[(2 * t + 1) ^ me[1]]


def join(me, first, second, out):
    out[0] = first[...] if len(first.shape) == 2 else first[1]
    out[1] = second[1]


def place_rows(me, own, across, near, out):
    out[me[1]] = own[...]
    out[2 ^ me[1]] = across[0]
    out[1 ^ me[1]] = near[0]
    out[3 ^ me[1]] = near[1]


def scale_all(me, s0, s1, s2, s3, d_time, d_gains, a1, a2, a3, *outs):
    squares = jnp.sum(s0[...] + s1[...] + s2[...] + s3[...])
    limit = math.sqrt(9 * D * D + 2 * D * FF + 3 * D)
    factor = jnp.minimum(1.0, limit * lax.rsqrt(jnp.full((8, 128), squares, F32)))[0:1, :]
    o_time, o_q, o_k, o_v, o_out, o_cq, o_ck, o_cv, o_cout, o_in, o_fout, o_gains = outs
    o_time[...] = d_time[...] * factor
    rows = d_time.shape[0]
    for src, dsts in ((a1, (o_q, o_k, o_v)), (a2, (o_cout, o_cq, o_ck, o_cv, o_out))):
        for t, dst in enumerate(dsts):
            dst[...] = src[rows * t : rows * (t + 1), :] * factor
    for t in range(CHUNKS):
        o_in[:, 128 * t : 128 * (t + 1)] = a3[rows * t : rows * (t + 1), :].astype(F32) * factor
    o_fout[...] = a3[rows * CHUNKS :, :].astype(F32) * factor
    o_gains[...] = (d_gains[...] * factor)[0:3, 0 : o_gains.shape[1]]


class Late:
    def __init__(self, src, dst, sems):
        self.src, self.ref, self.sems = src, dst, sems

    def copies(self):
        count = self.sems.shape[0]
        if count == 1:
            whole = pl.ds(0, self.ref.shape[0])
            return [pltpu.make_async_copy(self.src.at[whole], self.ref, self.sems.at[0])]
        return [pltpu.make_async_copy(self.src.at[p], self.ref.at[p], self.sems.at[p]) for p in range(count)]


class Early:
    def __init__(self, src, dst, sems):
        self.ref, self.dst, self.sems = src, dst, sems

    def copy(self, b):
        rows = pl.ds(pl.multiple_of(b * ROWS, ROWS), ROWS)
        return pltpu.make_async_copy(self.ref.at[rows, :], self.dst.at[rows, :], self.sems.at[b])

    def finish(self):
        for b in range(self.sems.shape[0]):
            self.copy(b).wait()


def fetch(*operands):
    for one in operands:
        for copy in one.copies():
            copy.start()


def wait(*operands):
    for one in operands:
        for copy in one.copies():
            copy.wait()


def late(array, parts=1, first=None):
    return (array, None, parts, first or array.shape[0])


EARLY = "early"


def full(shape):
    return pl.BlockSpec(shape, lambda i: (0,) * len(shape), pipeline_mode=pl.Buffered(1))


def call(body, name, args, outs, scratch=(), steps=1, flops=0, limit=48, hbm=False, free=()):
    in_specs = [pl.BlockSpec(memory_space=pltpu.SMEM)]
    arrays = [args[0]]
    groups = [None]

    later = []

    def take_in(a):
        if isinstance(a, tuple) and a[1] is None:
            later.append((len(arrays), a[2], a[3]))
            arrays.append(a[0])
            in_specs.append(pl.BlockSpec(memory_space=pl.ANY))
        elif isinstance(a, tuple):
            arrays.append(a[0])
            in_specs.append(a[1])
        else:
            arrays.append(a)
            in_specs.append(full(a.shape))

    for a in args[1:]:
        nested = isinstance(a, list) and isinstance(a[0], list)
        groups.append([len(b) for b in a] if nested else len(a) if isinstance(a, list) else None)
        for one in sum(a, []) if nested else a if isinstance(a, list) else [a]:
            take_in(one)
    flat = []
    out_groups = []
    for o in outs:
        out_groups.append(len(o) if isinstance(o, list) else None)
        flat += o if isinstance(o, list) else [o]

    early = [k for k, o in enumerate(flat) if o[2] is EARLY]

    def grouped(refs, sizes):
        got, at = [], 0
        for size in sizes:
            if isinstance(size, list):
                got.append(grouped(refs[at : at + sum(size)], size))
                at += sum(size)
            else:
                got.append(refs[at] if size is None else list(refs[at : at + size]))
                at += size or 1
        return got

    def run(*refs):
        n_in, n_out = len(arrays), len(flat)
        refs = list(refs)
        for k in reversed(early):
            sems, held = refs.pop(), refs.pop()
            refs[n_in + k] = Early(held, refs[n_in + k], sems)
        for k, _, _ in reversed(later):
            sems, held = refs.pop(), refs.pop()
            refs[k] = Late(refs[k], held, sems)
        body(
            *grouped(refs[:n_in], groups), *grouped(refs[n_in : n_in + n_out], out_groups), *refs[n_in + n_out :]
        )

    if hbm or body in (pack, take):
        arrays = [
            pltpu.with_memory_space_constraint(a, pltpu.HBM) if math.prod(a.shape) >= 2**14 else a for a in arrays
        ]
    made = lambda s, t, k: (
        pltpu.HBM(s, t) if hbm and math.prod(s) >= 2**14 and k not in free else jax.ShapeDtypeStruct(s, t)
    )
    size = sum(math.prod(a.shape) * a.dtype.itemsize for a in arrays)
    size += sum(math.prod(s) * jnp.dtype(t).itemsize for s, t, _ in flat)
    size = size if flops else 0
    got = pl.pallas_call(
        run,
        grid=(steps,),
        in_specs=in_specs,
        out_specs=tuple(
            full(s) if b is None else pl.BlockSpec(memory_space=pl.ANY) if b is EARLY else b for s, _, b in flat
        ),
        out_shape=tuple(made(s, t, k) for k, (s, t, _) in enumerate(flat)),
        scratch_shapes=list(scratch)
        + [
            one
            for k, parts, first in later
            for one in (pltpu.VMEM((first,) + arrays[k].shape[1:], arrays[k].dtype), pltpu.SemaphoreType.DMA((parts,)))
        ]
        + [
            one
            for k in early
            for one in (pltpu.VMEM(flat[k][0], flat[k][1]), pltpu.SemaphoreType.DMA((flat[k][0][0] // ROWS,)))
        ],
        compiler_params=pltpu.CompilerParams(vmem_limit_bytes=limit * 2**20),
        cost_estimate=pl.CostEstimate(flops=int(flops), bytes_accessed=size, transcendentals=0),
        name=name,
    )(*arrays)
    return grouped(got, out_groups)


def step_signal(step_ids, feat_width):
    half_width = feat_width // 2
    frequency = jnp.exp(-math.log(10000.0) * jnp.arange(half_width, dtype=F32) / half_width)
    angles = step_ids.astype(F32)[:, None] * frequency[None, :]
    return jnp.concatenate([jnp.sin(angles), jnp.cos(angles)], axis=1)


def sds(shape, dtype=BF, block=None):
    return (tuple(shape), dtype, block)


def per_device(
    decoder_input, timesteps, memory, cotangent, time_weight, attn_query, attn_key, attn_value, attn_out,
    cross_query, cross_key, cross_value, cross_out, ffn_in, ffn_out, norm_gains,
):
    dp = lax.axis_size("dp")
    mem_count = lax.axis_size("mem")
    rows = D // dp
    cols = D // mem_count
    by_hand = dp == 8 and mem_count == 4
    x = decoder_input[0]
    cot = cotangent[0]
    n = x.shape[0]
    r = memory.shape[0] * memory.shape[1]
    gains = norm_gains.T
    my_dp, my_mem = lax.axis_index("dp"), lax.axis_index("mem")
    me = jnp.stack([my_dp, my_mem]).astype(jnp.int32)

    def to(value, axis, bit):
        size = lax.axis_size(axis)
        return lax.ppermute(value, axis, [(i, i ^ bit) for i in range(size)])

    def after(value, *others):
        return lax.optimization_barrier((value,) + others)[0]

    def plane(own):
        return [own] + [to(own, "dp", 2 * bit) for bit in (1, 2, 3)]

    def swap(parts):
        both = []
        for part in parts:
            both += [part, to(part, "dp", 1)]
        return both

    in_parts = [ffn_in[:, D * c : D * (c + 1)] for c in range(CHUNKS)]
    if by_hand:
        first = (time_weight, attn_query, attn_key, attn_value)
        second = (attn_out, cross_query, cross_key, cross_value, cross_out)
        (own1,) = call(pack, "pack_one", (me,) + first, [sds((4, rows, D))], limit=4)
        plane1 = plane(own1)
        mem_keep, mem_send = call(
            take, "take_memory", (me, after(memory, own1)), [sds((2,) + memory.shape[1:])] * 2, limit=8
        )
        (own2,) = call(pack, "pack_two", (me,) + second, [sds((5, rows, D))], limit=4)
        (own3,) = call(pack, "pack_three", (me, ffn_in, ffn_out), [sds((2 * CHUNKS, rows, D))], limit=8)
        near = to(mem_send, "mem", 1)
        *plane1, near, own2, own3 = lax.optimization_barrier(tuple(plane1[1:]) + (near, own2, own3))
        (passed,) = call(join, "join_memory", (me, mem_keep, near), [sds(mem_keep.shape)], limit=8)
        across = to(passed, "mem", 2)
        g1 = [own1, to(own1, "dp", 1)]
        for part in plane1:
            g1 += [part, to(part, "dp", 1)]
        mem_rows = [late(mem_keep, 1, 1), late(near, 1, 1), late(across)]
        own2 = after(own2, *g1)
        g2 = plane(own2)
        g3 = lax.all_gather(own3, "dp", axis=0, tiled=False)
    else:

        def gather(parts):
            got = lax.all_gather(jnp.stack(parts, 0), "dp", axis=0, tiled=False)
            return got.transpose(1, 0, 2, 3).reshape(1, len(parts), D, D)

        g1 = [gather((time_weight, attn_query, attn_key, attn_value))]
        g2 = [gather((attn_out, cross_query, cross_key, cross_value, cross_out))]
        whole_out = lax.all_gather(ffn_out, "dp", axis=0, tiled=True).reshape(1, CHUNKS, D, D)
        g3 = jnp.concatenate([gather(in_parts), whole_out], axis=1)
        mem_rows = [late(lax.all_to_all(memory, "mem", split_axis=0, concat_axis=1, tiled=True))]
    signal = step_signal(timesteps, D).astype(BF)
    sig = jnp.broadcast_to(signal, (8, D))

    nat = pl.BlockSpec((n, PAIR), lambda i: (0, i))
    paired = lambda m: sds((PAIRS, m, PAIR), BF, pl.BlockSpec((1, m, PAIR), lambda i: (i, 0, 0)))
    nat_r = pl.BlockSpec((r, PAIR), lambda i: (0, i))
    rows2 = pl.BlockSpec((1, 2, n), lambda i: (i, 0, 0))
    wide = lambda m: pltpu.VMEM((PAIRS, m, PAIR), BF)
    tall = lambda m: pltpu.VMEM((PAIRS, PAIR, m), BF)
    weight = pltpu.VMEM((D, D), BF)
    weights = lambda count: pltpu.VMEM((count, D, D), BF)
    proj = 2 * n * D * D * 1.5
    att_cost = 2 * n * r * D * 5
    lse_out = sds((PAIRS, 2, n), F32, rows2)
    four_weights = sds((4, D, D), BF, pl.BlockSpec((1, D, D), lambda i: (i, 0, 0)))
    emb, n1, q, k, v, lse1, attended, held1 = call(
        self_forward, "self_forward", (me, x, sig, gains, g1),
        [sds((1, D), F32)] + [paired(n)] * 4 + [lse_out, paired(n), four_weights],
        [weights(4), wide(n), wide(n), wide(n), wide(n), tall(n), tall(n), tall(n), pltpu.SMEM((PAIRS,), jnp.int32)],
        PAIRS, 3 * proj + 2 * att_cost, 36, True,
    )
    if by_hand:
        attended, *g2 = lax.optimization_barrier((attended,) + tuple(g2))
        g2 = swap(g2)
    mid, n2, cq, ck, cv, lse2, crossed, held2 = call(
        cross_forward, "cross_forward", (me, x, emb, attended, mem_rows, gains, g2),
        [sds((n, D), F32, nat)] + [paired(n)] * 2 + [paired(r)] * 2 + [lse_out, paired(n), four_weights],
        [weights(4), pltpu.VMEM((PAIRS, n, PAIR), F32), wide(n), wide(n), wide(r), wide(r), tall(n), tall(r), tall(n),
         pltpu.SMEM((PAIRS,), jnp.int32)],
        PAIRS, 4 * proj + 2 * att_cost, 42, True,
    )
    if by_hand:
        weight_of = lambda t: [(p, pl.BlockSpec((1, rows, D), lambda i: (t, 0, 0))) for p in g2]
        raw_of = lambda count: [sds((dp // 2, mem_count, count * rows, cols))] * 2
        raw3_of = sds((dp, mem_count, 2 * CHUNKS * rows, cols))
    else:
        weight_of = lambda t: [(g2[0], pl.BlockSpec((1, 1, D, D), lambda i: (0, t, 0, 0)))]
        raw_of = lambda count: [sds((count, D, D))]
        raw3_of = sds((2 * CHUNKS, D, D))
    out, gl, bt, gain3, raw3 = call(
        feed_forward, "feed_forward", (me, mid, crossed, late(cot), gains, weight_of(4), late(g3)),
        [sds((n, D), BF, EARLY), sds((n, D), F32, EARLY), sds((n, D), BF, EARLY), sds((1, D), F32), sds(*raw3_of[:2], pl.BlockSpec(memory_space=pl.ANY))],
        [weights(1), weight, weight, pltpu.VMEM((n, D), BF), pltpu.VMEM((D, n), BF)] + [pltpu.VMEM((n, D), F32)] * 3
        + [pltpu.VMEM((2, n, D), BF)] * 2 + [pltpu.VMEM(raw3_of[0], BF), pltpu.SemaphoreType.DMA((CHUNKS, 2))],
        CHUNKS + 1, 25 * proj, 44, True,
    )
    back_scratch = lambda m, mats: [
        weights(mats), tall(n), tall(m), wide(n), tall(n), pltpu.VMEM((PAIRS, 2, n), F32),
        wide(n), wide(m), wide(m), weights(5), pltpu.VMEM((D, max(n, m)), BF),
    ]
    of_held2 = lambda t: (held2, pl.BlockSpec((1, D, D), lambda i: (t, 0, 0), pipeline_mode=pl.Buffered(1)))
    raw2, gm, b1, gain2, gk, gv = call(
        cross_back, "cross_back",
        (me, bt, crossed, late(cq), late(ck), late(cv), (lse2, rows2), mem_rows, late(n2), late(mid), late(gl), gains,
         weight_of(4), of_held2(1), late(attended)),
        [raw_of(5), sds((n, D), F32, EARLY), sds((n, D), BF, EARLY), sds((1, D), F32), sds((r, D), BF, nat_r),
         sds((r, D), BF, nat_r)],
        back_scratch(r, 1), PAIRS, 8 * proj + 5 * att_cost, 56, True,
    )
    if by_hand:
        got2 = to(raw2[1], "dp", 1)
        grad_of = [sds(memory.shape[1:]), sds(memory.shape[1:]), sds((2,) + memory.shape[1:])]
    else:
        grad_of = [sds((r, D))]
    (mem_grad,) = call(
        memory_back, "memory_back", (me, gk, gv, of_held2(2), of_held2(3)), [grad_of], (), 1, 0, 32, True,
    )
    if by_hand:
        got2 = after(got2, mem_grad[2])
        (parts2,) = call(add_core, "cross_core", (me, raw2[0], got2), [[sds((mem_count, 5 * rows, cols))] * 4], limit=24)
        b1, mem_grad[2], *parts2 = lax.optimization_barrier((b1, mem_grad[2]) + tuple(parts2))
        parts2 = [parts2[0]] + [to(parts2[b], "dp", 2 * b) for b in (1, 2, 3)]
        across = to(mem_grad[2], "mem", 2)
    raw1, input_grad, sums = call(
        self_back, "self_back",
        (me, b1, attended, late(q), late(k), late(v), (lse1, rows2), late(n1), late(held1), of_held2(0),
         late(x), emb, late(gm), gains, sig, gain2, gain3),
        [raw_of(3), sds((n, D), BF, EARLY), sds((SMALL, 128)) if by_hand else sds((8, D), F32)],
        back_scratch(n, 1)[1:] + [pltpu.VMEM((2, D), F32)], PAIRS, 7 * proj + 5 * att_cost, 50, True,
    )
    if by_hand:
        keep, send = raw1
        got1, small1 = to(send, "dp", 1), to(sums, "dp", 1)
        done3 = lax.psum_scatter(raw3, "dp", scatter_dimension=0, tiled=False)
        done3, sums = lax.optimization_barrier((done3, sums))
        done3 = lax.psum_scatter(done3, "mem", scatter_dimension=0, tiled=False)
        done3 = pltpu.with_memory_space_constraint(done3, pltpu.HBM)
        sums, *parts2 = lax.optimization_barrier((sums,) + tuple(parts2))
        (passed,) = call(join, "join_grad", (me, mem_grad[1], after(across, *parts2)), [sds(across.shape)], limit=8, flops=6e9)
        sums, keep, passed = lax.optimization_barrier((sums, keep, passed))

    limit = math.sqrt(9 * D * D + 2 * D * FF + 3 * D)
    if not by_hand:
        memory_grad = lax.all_to_all(mem_grad[0][None], "mem", split_axis=1, concat_axis=0, tiled=True)

        def scatter(raw):
            part = lax.psum_scatter(raw, "dp", scatter_dimension=1, tiled=True)
            part = lax.psum_scatter(part, "mem", scatter_dimension=2, tiled=True)
            return [part[t].astype(F32) for t in range(raw.shape[0])]

        d_in = scatter(raw3[:CHUNKS].transpose(1, 0, 2).reshape(1, D, FF))[0]
        d_fout = scatter(raw3[CHUNKS:].reshape(1, FF, D))[0]
        d_query, d_key, d_value = scatter(raw1[0])
        d_cout, d_cquery, d_ckey, d_cvalue, d_out = scatter(raw2[0])
        everyone = lax.all_gather(sums, ("dp", "mem"), axis=0, tiled=False)
        my_signal = lax.dynamic_slice_in_dim(everyone[:, 1], my_dp * rows, rows, axis=1)
        my_sums = lax.dynamic_slice_in_dim(everyone[:, 0], my_mem * cols, cols, axis=1)
        d_time = jnp.dot(my_signal.T, my_sums, precision=lax.Precision.HIGHEST)
        all_gains = jnp.sum(everyone[:, 2:5], axis=0)
        d_gains = lax.dynamic_slice_in_dim(all_gains, my_dp * rows, rows, axis=1).T
        weights = [d_time, d_query, d_key, d_value, d_out, d_cquery, d_ckey, d_cvalue, d_cout, d_in, d_fout]
        local = sum(jnp.sum(w * w) for w in weights)
        squares = lax.psum(local, ("dp", "mem")) + jnp.sum(all_gains * all_gains)
        factor = jnp.minimum(1.0, limit * lax.rsqrt(squares))
        return (
            (out[None], input_grad[None], memory_grad) + tuple(w * factor for w in weights) + (d_gains * factor,)
        )

    parts1 = call(
        add_core_small, "attn_core", (me, keep, got1, sums, small1),
        [sds((mem_count * 3 * rows + SMALL, cols))] * 4, limit=16,
    )
    parts1 = [parts1[0]] + [to(parts1[b], "dp", 2 * b) for b in (1, 2, 3)]
    parts = call(
        add_plane, "plane_sums", (me, parts1, parts2), [sds((8 * rows + SMALL, cols))] * mem_count, limit=24, hbm=False
    )
    last, done3 = lax.optimization_barrier((parts[3], done3))
    parts = [parts[0], to(parts[1], "mem", 1), to(parts[2], "mem", 2), to(last, "mem", 3)]
    done1, done2, d_time, d_gains, local = call(
        add_all, "add_all", (me, parts, done3),
        [sds((3 * rows, cols), F32), sds((5 * rows, cols), F32), sds((rows, cols), F32), sds((8, cols), F32),
         sds((8, cols), F32)],
        limit=16,
    )
    near = to(after(passed, local), "mem", 1)
    local = local + to(local, "dp", 1)
    local = local + to(local, "dp", 2) + to(local, "dp", 4) + to(local, "dp", 6)
    planes = [local] + [to(local, "mem", b) for b in (1, 2, 3)]
    shapes = [(rows, cols)] * 9 + [(rows, FF // mem_count), (FF // dp, cols), (3, rows)]
    scaled = call(
        scale_all, "scale_all", [me] + planes + [d_time, d_gains, done1, done2, done3],
        [sds(s, F32) for s in shapes], limit=16,
    )
    near = after(near, scaled[0])
    (memory_grad,) = call(place_rows, "place_rows", (me, mem_grad[0], across, near), [sds(memory.shape)], limit=8)
    return (out[None], input_grad[None], memory_grad) + tuple(scaled[:-1]) + (scaled[-1].T,)


def solution(mesh):
    tokens = P(("dp", "mem"), None, None)
    weight = P("dp", None)
    in_specs = (tokens, P(("dp", "mem")), P("dp", "mem", None), tokens) + (weight,) * 11 + (P(),)
    out_specs = (tokens, tokens, P("dp", "mem", None)) + (P("dp", "mem"),) * 11 + (P("dp", None),)
    return jax.shard_map(per_device, mesh=mesh, in_specs=in_specs, out_specs=out_specs, check_vma=False)
```
